32 devices in a mesh: dp: 8 (over z, y), seq: 4 (over x, core).
Axes of the slice: x: 2, y: 2, z: 4, core: 2. Of those that a mesh axis runs over, the one named last changes fastest.
Arguments:
- chars: bfloat16 [16, 2048, 768], P('dp', 'seq'), may hold values from -6 to 6
- window_mask: int32 [16, 16], P('dp'), may hold values from 0 to 1, as said below
- micro_batch: int32 [16], P('dp'), may hold values from 0 to 1, as said below
- mol_grad: bfloat16 [16, 512, 768], P('dp', 'seq'), may hold values from -6 to 6
- query_weight: bfloat16 [768, 768], replicated, may hold values from -0.21875 to 0.21875
- query_bias: bfloat16 [768], replicated, may hold values from -2 to 2
- key_weight: bfloat16 [768, 768], replicated, may hold values from -0.21875 to 0.21875
- value_weight: bfloat16 [768, 768], replicated, may hold values from -0.21875 to 0.21875
- value_bias: bfloat16 [768], replicated, may hold values from -2 to 2
- output_weight: bfloat16 [768, 768], replicated, may hold values from -0.875 to 0.875
- output_bias: bfloat16 [768], replicated, may hold values from -2 to 2
- first_gain: bfloat16 [768], replicated, may hold values from 0.5 to 1.5
- first_shift: bfloat16 [768], replicated, may hold values from -2 to 2
- inner_weight: bfloat16 [768, 3072], replicated, may hold values from -0.21875 to 0.21875
- inner_bias: bfloat16 [3072], replicated, may hold values from -2 to 2
- outer_weight: bfloat16 [3072, 768], replicated, may hold values from -0.109375 to 0.109375
- outer_bias: bfloat16 [768], replicated, may hold values from -2 to 2
- second_gain: bfloat16 [768], replicated, may hold values from 0.5 to 1.5
- second_shift: bfloat16 [768], replicated, may hold values from -2 to 2
- conv_weight: bfloat16 [3072, 768], replicated, may hold values from -0.109375 to 0.109375
- conv_bias: bfloat16 [768], replicated, may hold values from -2 to 2
- third_gain: bfloat16 [768], replicated, may hold values from 0.5 to 1.5
- third_shift: bfloat16 [768], replicated, may hold values from -2 to 2
Outputs:
- molecules: bfloat16 [16, 512, 768], P('dp', 'seq')
- chars_grad: bfloat16 [16, 2048, 768], P('dp', 'seq')
- query_weight_grad: float32 [768, 768], P(None, 'seq')
- query_bias_grad: float32 [768], P('seq')
- key_weight_grad: float32 [768, 768], P(None, 'seq')
- value_weight_grad: float32 [768, 768], P(None, 'seq')
- value_bias_grad: float32 [768], P('seq')
- output_weight_grad: float32 [768, 768], P(None, 'seq')
- output_bias_grad: float32 [768], P('seq')
- first_gain_grad: float32 [768], P('seq')
- first_shift_grad: float32 [768], P('seq')
- inner_weight_grad: float32 [768, 3072], P(None, 'seq')
- inner_bias_grad: float32 [3072], P('seq')
- outer_weight_grad: float32 [3072, 768], P(None, 'seq')
- outer_bias_grad: float32 [768], P('seq')
- second_gain_grad: float32 [768], P('seq')
- second_shift_grad: float32 [768], P('seq')
- conv_weight_grad: float32 [3072, 768], P(None, 'seq')
- conv_bias_grad: float32 [768], P('seq')
- third_gain_grad: float32 [768], P('seq')
- third_shift_grad: float32 [768], P('seq')
The draws below stay inside these ranges and needn't reach their ends.
Inputs may be any that keep to these rules, and one draw needn't show every extreme that they name: `window_mask`: each row's mask is 1 on a leading run of 4 to 16 windows and 0 after it; in each data group of 2 rows, one row, drawn from the seed, has all 16 windows. `micro_batch`: in each data group of 2 consecutive rows, every micro-batch holds 1 row.
All inputs are finite; a program needn't handle non-finite values.
Results may differ from the reference program's by a relative error of at most 0.02.
Values may be sent and summed in bfloat16 or wider, within the bound.
No kernel may reach another device: no remote copies, remote signals or barrier semaphores. Data moves between devices by JAX's collectives and lax.ppermute only.
A program may use at most 256 MiB of HBM per device.

```python
import jax
import jax.numpy as jnp
from jax import lax

D = 768
HEADS = 12
HEAD_DIM = 64
FF = 3072
WIN = 128
DOWN = 4
WPD = 4
MICRO = 2
ROWS = 2
WINS = 16
LEN = 2048
MOLS = 512
ROWS_ALL = 16


def draw_window_mask(key, part):
    key = jax.random.fold_in(key, 11)
    count_key, pick_key = jax.random.split(key)
    counts = jax.random.randint(count_key, (ROWS_ALL,), WPD, WINS + 1)
    chosen = jax.random.randint(pick_key, (ROWS_ALL // ROWS,), 0, ROWS)
    position = jnp.arange(ROWS_ALL)
    full_row = position % ROWS == jnp.repeat(chosen, ROWS)
    counts = jnp.where(full_row, WINS, counts)
    return (jnp.arange(WINS)[None, :] < counts[:, None]).astype(jnp.int32)


def draw_micro_batch(key, part):
    key = jax.random.fold_in(key, 12)
    row_keys = jax.random.split(key, ROWS_ALL // ROWS)
    orders = jax.vmap(lambda sub_key: jax.random.permutation(sub_key, ROWS))(row_keys)
    return (orders % MICRO).reshape(ROWS_ALL).astype(jnp.int32)


def block_levels(rng, extent, cuts, smallest, top_value):
    def one(dim, parts):
        draws = jax.random.uniform(jax.random.fold_in(jax.random.fold_in(rng, 6), dim), (parts,), jnp.float32, smallest / len(cuts), top_value / len(cuts))
        return jnp.repeat(jnp.exp(draws), extent[dim] // parts).reshape((-1,) + (1,) * (len(extent) - dim - 1))

    gain = one(*cuts[0])
    for cut in cuts[1:]:
        gain = gain * one(*cut)
    return gain


def centred(own_key, shape, scale, most, shards=(), dtype=jnp.bfloat16):
    entries = scale * jax.random.normal(own_key, shape, jnp.float32)
    if shards:
        entries = entries * block_levels(own_key, shape, shards, -0.22, 0.18)
    return jnp.clip(entries, -most, most).astype(dtype)


def setup_inputs(seed: int = 0) -> dict:
    key_of = jax.random.split(jax.random.key(seed), 24)
    return {
        "chars": centred(key_of[0], (ROWS_ALL, LEN, D), 1.0, 6.0, ((0, 8), (1, 4))),
        "window_mask": draw_window_mask(jax.random.fold_in(key_of[23], 71), 0),
        "micro_batch": draw_micro_batch(jax.random.fold_in(key_of[23], 71), 0),
        "mol_grad": centred(key_of[3], (ROWS_ALL, MOLS, D), 1.0, 6.0, ((0, 8), (1, 4))),
        "query_weight": centred(key_of[4], (D, D), D ** -0.5, 0.21875),
        "query_bias": centred(key_of[5], (D,), 0.3, 2.0),
        "key_weight": centred(key_of[6], (D, D), D ** -0.5, 0.21875),
        "value_weight": centred(key_of[7], (D, D), D ** -0.5, 0.21875),
        "value_bias": centred(key_of[8], (D,), 0.3, 2.0),
        "output_weight": centred(key_of[9], (D, D), (D // 16) ** -0.5, 0.875),
        "output_bias": centred(key_of[10], (D,), 0.3, 2.0),
        "first_gain": jnp.clip(1.0 + 0.1 * jax.random.normal(key_of[11], (D,), jnp.float32), 0.5, 1.5).astype(jnp.bfloat16),
        "first_shift": centred(key_of[12], (D,), 0.3, 2.0),
        "inner_weight": centred(key_of[13], (D, FF), D ** -0.5, 0.21875),
        "inner_bias": centred(key_of[14], (FF,), 0.3, 2.0),
        "outer_weight": centred(key_of[15], (FF, D), FF ** -0.5, 0.109375),
        "outer_bias": centred(key_of[16], (D,), 0.3, 2.0),
        "second_gain": jnp.clip(1.0 + 0.1 * jax.random.normal(key_of[17], (D,), jnp.float32), 0.5, 1.5).astype(jnp.bfloat16),
        "second_shift": centred(key_of[18], (D,), 0.3, 2.0),
        "conv_weight": centred(key_of[19], (DOWN * D, D), (DOWN * D) ** -0.5, 0.109375),
        "conv_bias": centred(key_of[20], (D,), 0.3, 2.0),
        "third_gain": jnp.clip(1.0 + 0.1 * jax.random.normal(key_of[21], (D,), jnp.float32), 0.5, 1.5).astype(jnp.bfloat16),
        "third_shift": centred(key_of[22], (D,), 0.3, 2.0),
    }


HIGH = lax.Precision.HIGHEST
EPSILON = 1e-06
NEG_FILL = -1e+30

@jax.custom_vjp
def low(v):
    return lax.optimization_barrier(v.astype(jnp.bfloat16)).astype(jnp.float32)

@jax.custom_vjp
def low_back(v):
    return v

def low_keep(v):
    return (low(v), None)

def low_pass(kept, grad):
    return (grad,)

def back_keep(v):
    return (v, None)

def back_low(kept, grad):
    return (low(grad),)
low.defvjp(low_keep, low_pass)
low_back.defvjp(back_keep, back_low)

def matmul(left_op, right_op):
    return jnp.dot(left_op, right_op, precision=HIGH, preferred_element_type=jnp.float32)

def layer_norm(inputs, norm_gain, norm_shift):
    center = inputs - lax.optimization_barrier(jnp.mean(inputs, axis=-1, keepdims=True))
    spread = lax.optimization_barrier(jnp.mean(center * center, axis=-1, keepdims=True))
    return center * lax.rsqrt(spread + EPSILON) * norm_gain + norm_shift

def window_rule(valid_windows):
    window_ids = jnp.arange(WINS)
    beside = window_ids[:, None] + jnp.arange(3)[None, :] - 1
    inside = (beside >= 0) & (beside < WINS)
    lookup = lax.optimization_barrier(jnp.sum(valid_windows[None, None, :] * (window_ids[None, None, :] == beside[:, :, None]).astype(jnp.float32), axis=-1))
    return (jnp.arange(3)[None, :] == 1) | inside & (lookup > 0.5)

def row_forward(params, row_chars, valid_windows):
    query_weight, query_bias, key_weight, value_weight, value_bias, output_weight, output_bias, first_gain, first_shift, inner_weight, inner_bias, outer_weight, outer_bias, second_gain, second_shift, conv_weight, conv_bias, third_gain, third_shift = params
    win_shape = (WINS, WIN, HEADS, HEAD_DIM)
    queries = low_back(low(matmul(row_chars, query_weight) + query_bias)).reshape(win_shape)
    keys = low_back(low(matmul(row_chars, key_weight)))
    values = low_back(low(matmul(row_chars, value_weight) + value_bias))

    def beside_all(tensor):
        padded = jnp.pad(tensor.reshape(win_shape), ((1, 1), (0, 0), (0, 0), (0, 0)))
        return jnp.concatenate([padded[0:WINS], padded[1:WINS + 1], padded[2:WINS + 2]], axis=1)
    key_win = beside_all(keys)
    value_win = beside_all(values)
    scores = jnp.einsum('wqhd,wkhd->whqk', queries, key_win, precision=HIGH) * HEAD_DIM ** (-0.5)
    scores = low_back(scores)
    allowed = jnp.repeat(window_rule(valid_windows), WIN, axis=1)
    scores = jnp.where(allowed[:, None, None, :], scores, NEG_FILL)
    row_top = lax.optimization_barrier(jnp.max(scores, axis=-1, keepdims=True))
    shifted_exp = jnp.exp(scores - row_top)
    probs = low(shifted_exp / lax.optimization_barrier(jnp.sum(shifted_exp, axis=-1, keepdims=True)))
    mixed = jnp.einsum('whqk,wkhd->wqhd', probs, value_win, precision=HIGH).reshape(LEN, D)
    mixed = low_back(low(mixed))
    branch = low_back(matmul(mixed, output_weight) + output_bias)
    first = layer_norm(row_chars + branch, first_gain, first_shift)
    inner = low_back(matmul(low(first), inner_weight) + inner_bias)
    hidden = low(jax.nn.gelu(inner))
    outer = low_back(matmul(hidden, outer_weight) + outer_bias)
    second = layer_norm(first + outer, second_gain, second_shift)
    merged = low(second).reshape(MOLS, DOWN * D)
    conv = low_back(matmul(merged, conv_weight) + conv_bias)
    normed = layer_norm(jax.nn.gelu(conv), third_gain, third_shift)
    live = jnp.repeat(valid_windows, WIN // DOWN)
    return normed * live[:, None]

def reference(chars, window_mask, micro_batch, mol_grad, query_weight, query_bias, key_weight, value_weight, value_bias, output_weight, output_bias, first_gain, first_shift, inner_weight, inner_bias, outer_weight, outer_bias, second_gain, second_shift, conv_weight, conv_bias, third_gain, third_shift):
    params = tuple((item.astype(jnp.float32) for item in (query_weight, query_bias, key_weight, value_weight, value_bias, output_weight, output_bias, first_gain, first_shift, inner_weight, inner_bias, outer_weight, outer_bias, second_gain, second_shift, conv_weight, conv_bias, third_gain, third_shift)))
    chars_wide = chars.astype(jnp.float32)
    windows_wide = window_mask.astype(jnp.float32)

    def whole(param_set, inputs):
        row_step = jax.checkpoint(lambda row_chars, row_valid: row_forward(param_set, row_chars, row_valid))
        return lax.map(lambda row_pair: row_step(row_pair[0], row_pair[1]), (inputs, windows_wide))
    molecules, pullback = jax.vjp(whole, params, chars_wide)
    groups = ROWS_ALL // ROWS
    live_count = lax.optimization_barrier(jnp.sum(windows_wide, axis=1)) * (WIN // DOWN)
    choose = (micro_batch[:, None] == jnp.arange(MICRO)[None, :]).astype(jnp.float32).reshape(groups, ROWS, MICRO)
    counts = lax.optimization_barrier(jnp.sum(choose * live_count.reshape(groups, ROWS, 1), axis=1))
    row_counts = lax.optimization_barrier(jnp.sum(choose * counts[:, None, :], axis=2)).reshape(ROWS_ALL)
    weight = ROWS // MICRO * MOLS / row_counts
    cotangent = mol_grad.astype(jnp.float32) * weight[:, None, None]
    grads, chars_grad = pullback(cotangent)
    return (molecules.astype(jnp.bfloat16), chars_grad.astype(jnp.bfloat16), grads[0], grads[1], grads[2], grads[3], grads[4], grads[5], grads[6], grads[7], grads[8], grads[9], grads[10], grads[11], grads[12], grads[13], grads[14], grads[15], grads[16], grads[17], grads[18])
```

```python
import functools

import jax
import jax.numpy as jnp
from jax import lax
from jax.experimental import pallas as pl
from jax.experimental.pallas import tpu as pltpu
from jax.sharding import PartitionSpec as P

HEADS = 12
HEAD_DIM = 64
WIN = 128
DOWN = 4
MICRO = 2
EPSILON = 1e-06
NEG_FILL = -1e30
GELU_A = 0.7978845608028654
GELU_B = 0.044715
BF = jnp.bfloat16
F32 = jnp.float32
LANES = 128
MIB = 1 << 20

NN = (((1,), (0,)), ((), ()))
NT = (((1,), (1,)), ((), ()))
TN = (((0,), (0,)), ((), ()))

(V_QB, V_VB, V_OB, V_G1, V_S1, V_OUTB, V_G2, V_S2, V_CB, V_G3, V_S3, V_IB) = range(12)


def dot(left, right, dims=NN):
    return lax.dot_general(left, right, dims, preferred_element_type=F32)


def gelu(u):
    return 0.5 * u * (1.0 + jnp.tanh(GELU_A * (u + GELU_B * u * u * u)))


def gelu_slope(u):
    t = jnp.tanh(GELU_A * (u + GELU_B * u * u * u))
    return 0.5 * (1.0 + t) + 0.5 * u * (1.0 - t * t) * (GELU_A * (1.0 + 3.0 * GELU_B * u * u))


def layer_stats(u):
    center = u - jnp.mean(u, axis=-1, keepdims=True)
    inv_dev = lax.rsqrt(jnp.mean(center * center, axis=-1, keepdims=True) + EPSILON)
    return center * inv_dev, inv_dev


def norm_back(grad_out, normal, inv_dev, gain_vec):
    scaled = grad_out * gain_vec
    return inv_dev * (
        scaled
        - jnp.mean(scaled, axis=-1, keepdims=True)
        - normal * jnp.mean(scaled * normal, axis=-1, keepdims=True)
    )


def col_sum(value):
    return jnp.sum(value, axis=0, keepdims=True)


def params(mib=56, **more):
    return pltpu.CompilerParams(vmem_limit_bytes=mib * MIB, **more)


def cost(flops, nbytes):
    return pl.CostEstimate(flops=int(flops), bytes_accessed=int(nbytes), transcendentals=0)


def spec_any():
    return pl.BlockSpec(memory_space=pl.ANY)


def spec_smem():
    return pl.BlockSpec(memory_space=pltpu.SMEM)


def spec_vmem():
    return pl.BlockSpec(memory_space=pltpu.VMEM)


def shape(dims, dtype=BF):
    return jax.ShapeDtypeStruct(tuple(dims), dtype)


def run(body, deps, args, out_shape, in_specs, out_specs, scratch=(), grid=(), prefetch=0, mib=56, flops=0, nbytes=0, name=None):
    given = len(args)

    def wrapped(*refs):
        body(*refs[:given], *refs[given + len(deps) :])

    return pl.pallas_call(
        wrapped,
        grid_spec=pltpu.PrefetchScalarGridSpec(
            num_scalar_prefetch=prefetch,
            grid=grid,
            in_specs=list(in_specs) + [spec_any()] * len(deps),
            out_specs=out_specs,
            scratch_shapes=list(scratch),
        ),
        out_shape=out_shape,
        compiler_params=pltpu.CompilerParams(vmem_limit_bytes=mib * MIB),
        cost_estimate=cost(flops, nbytes),
        name=name,
    )(*args, *deps)


def head_masks():
    lane = lax.broadcasted_iota(jnp.int32, (1, LANES), 1)
    first = jnp.where(lane < HEAD_DIM, 1.0, 0.0).astype(BF)
    return first, (1.0 - first.astype(F32)).astype(BF)


def twice(block, masks):
    return jnp.concatenate([block * masks[0], block * masks[1]], axis=0)


def slot_of(quarter, place):
    same_x = (quarter // 2 == place // 2).astype(jnp.int32)
    same_core = (quarter % 2 == place % 2).astype(jnp.int32)
    return 2 * same_core + same_x


def quarter_of(slot, place):
    side = jnp.where(slot % 2 == 1, place // 2, 1 - place // 2)
    core = jnp.where(slot // 2 == 1, place % 2, 1 - place % 2)
    return 2 * side + core


def project_kernel(x_ref, vec_ref, wq_ref, wk_ref, wv_ref, q_ref, k_ref, v_ref):
    x = x_ref[...]
    queries = (dot(x, wq_ref[...]) + vec_ref[V_QB : V_QB + 1, :]).astype(BF)
    q_ref[...] = queries * jnp.asarray(HEAD_DIM**-0.5, BF)
    k_ref[...] = dot(x, wk_ref[...]).astype(BF)
    v_ref[...] = (dot(x, wv_ref[...]) + vec_ref[V_VB : V_VB + 1, :]).astype(BF)


def project(deps, tokens, vecs, wq, wk, wv):
    count, width = tokens.shape
    part = 256
    column = pl.BlockSpec((width, part), lambda i: (0, i))
    out = pl.BlockSpec((count, part), lambda i: (0, i))
    return run(
        project_kernel,
        deps,
        (tokens, vecs, wq, wk, wv),
        [shape((count, width))] * 3,
        [
            pl.BlockSpec((count, width), lambda i: (0, 0)),
            pl.BlockSpec((vecs.shape[0], part), lambda i: (0, i)),
            column,
            column,
            column,
        ],
        [out] * 3,
        grid=(width // part,),
        mib=60,
        flops=6 * count * width * width,
        nbytes=12 * MIB,
        name="project",
    )


def forward_kernel(
    rows,
    wins,
    windows_all,
    meta,
    wmask,
    mbatch,
    vec,
    chars_h,
    low_h,
    high_h,
    q_h,
    k_h,
    v_h,
    wk_h,
    wv_h,
    wo_h,
    wi_h,
    wout_h,
    wc_h,
    mg_h,
    kv_o,
    pt_o,
    mixed_o,
    n1_o,
    inv1_o,
    low1_o,
    inner_o,
    hidden_o,
    n2_o,
    inv2_o,
    merged_o,
    gc_o,
    mol_o,
    sums_o,
    send_o,
    keep_o,
    q,
    kv,
    halo,
    wkv,
    wo,
    chars,
    wi,
    wout,
    wc,
    mg,
    probs,
    mixed,
    acc,
    strips,
    low1,
    n1,
    inv1,
    inner,
    hidden,
    n2,
    inv2,
    merged,
    gc,
    mol,
    sem_in,
    sem_p,
    sem_h,
    sem_out,
):
    place = meta[0]
    block = wins * WIN
    width = chars.shape[-1]
    count = rows * block
    pairs = width // LANES
    parts = wi.shape[1] // width

    def copy_in(index, src, dst):
        made = pltpu.make_async_copy(src, dst, sem_in.at[index])
        made.start()
        return made

    halo_in = [
        copy_in(0, low_h, halo.at[0]),
        copy_in(1, high_h, halo.at[1]),
        copy_in(2, wk_h, wkv.at[0]),
        copy_in(3, wv_h, wkv.at[1]),
    ]
    qkv_in = [copy_in(4, q_h, q)]
    for r in range(rows):
        qkv_in.append(
            copy_in(5 + 2 * r, k_h.at[pl.ds(r * block, block)], kv.at[r, pl.ds(WIN, block)])
        )
        qkv_in.append(
            copy_in(
                6 + 2 * r, v_h.at[pl.ds(r * block, block)], kv.at[rows + r, pl.ds(WIN, block)]
            )
        )
    base = 5 + 2 * rows
    wo_in = copy_in(base, wo_h, wo)
    chars_in = copy_in(base + 1, chars_h, chars)
    wi_in = copy_in(base + 2, wi_h, wi)
    wout_in = copy_in(base + 3, wout_h, wout)
    wc_in = copy_in(base + 4, wc_h, wc)
    mg_in = copy_in(base + 5, mg_h, mg)

    def copy_out(index, src, dst):
        made = pltpu.make_async_copy(src, dst, sem_out.at[index])
        made.start()
        return made

    for made in halo_in:
        made.wait()
    beside = halo[...].reshape(2 * rows * WIN, width)
    keys = dot(beside, wkv[0]).astype(BF)
    values = (dot(beside, wkv[1]) + vec[V_VB : V_VB + 1, :]).astype(BF)
    for side in range(2):
        start = side * (block + WIN)
        for r in range(rows):
            at = (side * rows + r) * WIN
            kv[r, pl.ds(start, WIN), :] = keys[at : at + WIN]
            kv[rows + r, pl.ds(start, WIN), :] = values[at : at + WIN]
    for made in qkv_in:
        made.wait()
    kv_out = copy_out(0, kv, kv_o)

    masks = head_masks()

    def pair_step(it, carry):
        r = it // pairs
        pair = it % pairs
        slot = it % 2
        lanes = pl.ds(pl.multiple_of(pair * LANES, LANES), LANES)

        @pl.when(it >= 2)
        def _():
            pltpu.make_async_copy(probs.at[slot], pt_o.at[it - 2], sem_p.at[slot]).wait()

        for w in range(wins):
            at = place * wins + w
            low_ok = (at >= 1) & (wmask[r, jnp.maximum(at - 1, 0)] > 0)
            high_ok = (at + 1 < windows_all) & (wmask[r, jnp.minimum(at + 1, windows_all - 1)] > 0)
            queries = twice(q[pl.ds(r * block + w * WIN, WIN), lanes], masks)
            scores = dot(kv[r, pl.ds(w * WIN, 3 * WIN), lanes], queries, NT)
            scores = jnp.concatenate(
                [
                    scores[0:WIN] + jnp.where(low_ok, 0.0, NEG_FILL),
                    scores[WIN : 2 * WIN],
                    scores[2 * WIN :] + jnp.where(high_ok, 0.0, NEG_FILL),
                ],
                axis=0,
            )
            shifted = jnp.exp(scores - jnp.max(scores, axis=0, keepdims=True))
            total = jnp.sum(shifted, axis=0, keepdims=True)
            chance = (shifted * (1.0 / total)).astype(BF)
            probs[slot, w] = chance
            stacked = jnp.concatenate([chance[:, :LANES], chance[:, LANES:]], axis=0)
            values_win = twice(kv[rows + r, pl.ds(w * WIN, 3 * WIN), lanes], masks)
            mixed[pl.ds(r * block + w * WIN, WIN), lanes] = dot(stacked, values_win, TN).astype(BF)
        pltpu.make_async_copy(probs.at[slot], pt_o.at[it], sem_p.at[slot]).start()
        return carry

    steps = rows * pairs
    lax.fori_loop(0, steps, pair_step, 0)
    mixed_out = copy_out(1, mixed, mixed_o)

    wo_in.wait()
    chars_in.wait()
    piece = 256

    def first_step(i, carry):
        at = pl.ds(pl.multiple_of(i * piece, piece), piece)
        u = dot(mixed[at, :], wo[...]) + vec[V_OB : V_OB + 1, :] + chars[at, :].astype(F32)
        normal, inv = layer_stats(u)
        first = normal * vec[V_G1 : V_G1 + 1, :] + vec[V_S1 : V_S1 + 1, :]
        n1[at, :] = normal.astype(BF)
        inv1[at, :] = inv
        low1[at, :] = first.astype(BF)
        acc[at, :] = first + vec[V_OUTB : V_OUTB + 1, :]
        return carry

    lax.fori_loop(0, count // piece, first_step, 0)
    outs = [mixed_out, copy_out(2, n1, n1_o), copy_out(3, inv1, inv1_o), copy_out(4, low1, low1_o)]

    wi_in.wait()
    wout_in.wait()

    def ffn_step(c, carry):
        slot = c % 2
        columns = pl.ds(pl.multiple_of(c * width, width), width)

        @pl.when(c >= 2)
        def _():
            pltpu.make_async_copy(inner.at[slot], inner_o.at[c - 2], sem_h.at[slot]).wait()
            pltpu.make_async_copy(hidden.at[slot], hidden_o.at[c - 2], sem_h.at[2 + slot]).wait()

        u = dot(low1[...], wi[:, columns]) + vec[pl.ds(V_IB + c, 1), :]
        inner[slot] = u.astype(BF)
        h = gelu(u).astype(BF)
        hidden[slot] = h
        acc[...] += dot(h, wout[columns, :])
        pltpu.make_async_copy(inner.at[slot], inner_o.at[c], sem_h.at[slot]).start()
        pltpu.make_async_copy(hidden.at[slot], hidden_o.at[c], sem_h.at[2 + slot]).start()
        return carry

    lax.fori_loop(0, parts, ffn_step, 0)

    def second_step(i, carry):
        at = pl.ds(pl.multiple_of(i * piece, piece), piece)
        normal, inv = layer_stats(acc[at, :])
        n2[at, :] = normal.astype(BF)
        inv2[at, :] = inv
        second = normal * vec[V_G2 : V_G2 + 1, :] + vec[V_S2 : V_S2 + 1, :]
        for t in range(pairs):
            strips[t, at, :] = second[:, t * LANES : (t + 1) * LANES]
        return carry

    lax.fori_loop(0, count // piece, second_step, 0)
    outs += [copy_out(5, n2, n2_o), copy_out(6, inv2, inv2_o)]

    wc_in.wait()
    mg_in.wait()
    mols = count // DOWN
    conv = jnp.zeros((mols, width), F32) + vec[V_CB : V_CB + 1, :]
    for i in range(DOWN):
        for t in range(pairs):
            merged[i, :, t * LANES : (t + 1) * LANES] = strips[
                t, pl.ds(i, mols, stride=DOWN), :
            ].astype(BF)
        part = merged[i]
        conv = conv + dot(part, wc[pl.ds(i * width, width), :])
    outs.append(copy_out(7, merged, merged_o))
    normal, inv = layer_stats(gelu(conv))
    per_win = WIN // DOWN
    which = lax.broadcasted_iota(jnp.int32, (mols, 1), 0) // per_win
    live = jnp.zeros((mols, 1), F32)
    total = jnp.ones((mols, 1), F32)
    lengths = []
    for r in range(rows):
        length = wmask[r, 0]
        for w in range(1, windows_all):
            length = length + wmask[r, w]
        lengths.append(length)
    for r in range(rows):
        same = jnp.int32(0)
        for other in range(rows):
            same = same + jnp.where(mbatch[other] == mbatch[r], lengths[other], 0)
        same = (same * per_win).astype(F32)
        for w in range(wins):
            here = which == r * wins + w
            live = jnp.where(here, wmask[r, place * wins + w].astype(F32), live)
            total = jnp.where(here, same, total)
    weight = (rows // MICRO * windows_all * per_win) / total
    gain = vec[V_G3 : V_G3 + 1, :]
    mol[...] = ((normal * gain + vec[V_S3 : V_S3 + 1, :]) * live).astype(BF)
    outs.append(copy_out(8, mol, mol_o))
    grad_mol = mg[...].astype(F32) * (weight * live)
    grad_conv = (gelu_slope(conv) * norm_back(grad_mol, normal, inv, gain)).astype(BF)
    gc[...] = grad_conv
    outs.append(copy_out(9, gc, gc_o))
    sums_o[0:1, :] = col_sum(grad_mol * normal)
    sums_o[1:2, :] = col_sum(grad_mol)
    sums_o[2:3, :] = col_sum(grad_conv.astype(F32))
    sums_o[3:, :] = jnp.zeros((sums_o.shape[0] - 3, width), F32)

    kv_out.wait()
    across = grad_conv.T
    quarter = width // 4
    for i in range(DOWN):
        made = dot(across, merged[i]).astype(BF)
        for number in range(4):
            kv[slot_of(jnp.int32(number), place), pl.ds(i * quarter, quarter), :] = made[
                number * quarter : (number + 1) * quarter
            ]
    outs.append(copy_out(10, kv.at[pl.ds(0, 2)], send_o))
    outs.append(copy_out(11, kv.at[pl.ds(2, 2)], keep_o))

    for made in outs:
        made.wait()
    for it in range(max(0, steps - 2), steps):
        pltpu.make_async_copy(probs.at[it % 2], pt_o.at[it], sem_p.at[it % 2]).wait()
    for c in range(max(0, parts - 2), parts):
        pltpu.make_async_copy(inner.at[c % 2], inner_o.at[c], sem_h.at[c % 2]).wait()
        pltpu.make_async_copy(hidden.at[c % 2], hidden_o.at[c], sem_h.at[2 + c % 2]).wait()


def forward(deps, meta, wmask, mbatch, vecs, chars, low, high, q, k, v, wk, wv, wo, wi, wout, wc, mg):
    rows = wmask.shape[0]
    windows_all = wmask.shape[1]
    count, width = q.shape
    block = count // rows
    wins = block // WIN
    ff = wi.shape[1]
    parts = ff // width
    mols = count // DOWN
    pairs = width // LANES
    ext = block + 2 * WIN
    outs = [
        shape((2 * rows, ext, width)),
        shape((rows * pairs, wins, 3 * WIN, 2 * LANES)),
        shape((count, width)),
        shape((count, width)),
        shape((count, 1), F32),
        shape((count, width)),
        shape((parts, count, width)),
        shape((parts, count, width)),
        shape((count, width)),
        shape((count, 1), F32),
        shape((DOWN, mols, width)),
        shape((mols, width)),
        shape((mols, width)),
        shape((8, width), F32),
        shape((2, DOWN * width // 4, width)),
        shape((2, DOWN * width // 4, width)),
    ]
    out_specs = [spec_any()] * len(outs)
    out_specs[13] = spec_vmem()
    flops = 2 * count * width * (3 * width + 2 * ff + 2 * width) + 4 * count * 384 * width * 4
    return run(
        functools.partial(forward_kernel, rows, wins, windows_all),
        deps,
        (meta, wmask, mbatch, vecs, chars, low, high, q, k, v, wk, wv, wo, wi, wout, wc, mg),
        outs,
        [spec_smem()] * 3 + [spec_vmem()] + [spec_any()] * 13,
        out_specs,
        scratch=[
            pltpu.VMEM((count, width), BF),
            pltpu.VMEM((2 * rows, ext, width), BF),
            pltpu.VMEM((2, rows, WIN, width), BF),
            pltpu.VMEM((2, width, width), BF),
            pltpu.VMEM((width, width), BF),
            pltpu.VMEM((count, width), BF),
            pltpu.VMEM((width, ff), BF),
            pltpu.VMEM((ff, width), BF),
            pltpu.VMEM((DOWN * width, width), BF),
            pltpu.VMEM((mols, width), BF),
            pltpu.VMEM((2, wins, 3 * WIN, 2 * LANES), BF),
            pltpu.VMEM((count, width), BF),
            pltpu.VMEM((count, width), F32),
            pltpu.VMEM((pairs, count, LANES), F32),
            pltpu.VMEM((count, width), BF),
            pltpu.VMEM((count, width), BF),
            pltpu.VMEM((count, 1), F32),
            pltpu.VMEM((2, count, width), BF),
            pltpu.VMEM((2, count, width), BF),
            pltpu.VMEM((count, width), BF),
            pltpu.VMEM((count, 1), F32),
            pltpu.VMEM((DOWN, mols, width), BF),
            pltpu.VMEM((mols, width), BF),
            pltpu.VMEM((mols, width), BF),
            pltpu.SemaphoreType.DMA((11 + 2 * rows,)),
            pltpu.SemaphoreType.DMA((2,)),
            pltpu.SemaphoreType.DMA((4,)),
            pltpu.SemaphoreType.DMA((12,)),
        ],
        mib=60,
        flops=flops,
        nbytes=60 * MIB,
        name="forward",
    )


def second_back_kernel(vec, gc, wc, n2, inv2, go, sums, whole):
    count, width = n2.shape
    mols = gc.shape[0]
    for i in range(DOWN):
        made = dot(gc[...], wc[pl.ds(i * width, width), :], NT)
        for t in range(width // LANES):
            whole[t, pl.ds(i, mols, stride=DOWN), :] = made[:, t * LANES : (t + 1) * LANES]
    gain = vec[V_G2 : V_G2 + 1, :]
    piece = 256
    sums[...] = jnp.zeros(sums.shape, F32)

    def step(i, carry):
        at = pl.ds(pl.multiple_of(i * piece, piece), piece)
        grad = jnp.concatenate([whole[t, at, :] for t in range(width // LANES)], axis=1)
        normal = n2[at, :].astype(F32)
        made = norm_back(grad, normal, inv2[at, :], gain).astype(BF)
        go[at, :] = made
        sums[0:1, :] += col_sum(grad * normal)
        sums[1:2, :] += col_sum(grad)
        sums[2:3, :] += col_sum(made.astype(F32))
        return carry

    lax.fori_loop(0, count // piece, step, 0)


def second_back(deps, vecs, gc, wc, n2, inv2):
    count, width = n2.shape
    return run(
        second_back_kernel,
        deps,
        (vecs, gc, wc, n2, inv2),
        [shape((count, width)), shape((8, width), F32)],
        [spec_vmem()] * 5,
        [spec_vmem()] * 2,
        scratch=[pltpu.VMEM((width // LANES, count, LANES), F32)],
        flops=2 * count * width * width,
        nbytes=12 * MIB,
        name="second_back",
    )


def outer_grad_kernel(meta, go, hidden, send, keep, across):
    place = meta[0]
    width = go.shape[1]
    quarter = width // 4

    @pl.when(pl.program_id(0) == 0)
    def _():
        turned = go[...].T
        for number in range(4):
            across[slot_of(jnp.int32(number), place)] = turned[
                number * quarter : (number + 1) * quarter
            ]

    left = across[...].reshape(width, go.shape[0])
    made = dot(left, hidden[0]).astype(BF)
    for j in range(2):
        send[j] = made[j * quarter : (j + 1) * quarter]
        keep[j] = made[(2 + j) * quarter : (3 + j) * quarter]


def outer_grad(deps, meta, go, hidden):
    parts, count, width = hidden.shape
    quarter = width // 4
    out = pl.BlockSpec((2, quarter, width), lambda i, m: (0, i, 0))
    return run(
        outer_grad_kernel,
        deps,
        (meta, go, hidden),
        [shape((2, parts * quarter, width))] * 2,
        [
            pl.BlockSpec((count, width), lambda i, m: (0, 0)),
            pl.BlockSpec((1, count, width), lambda i, m: (i, 0, 0)),
        ],
        [out] * 2,
        scratch=[pltpu.VMEM((4, quarter, count), BF)],
        grid=(parts,),
        prefetch=1,
        flops=2 * count * width * width * parts,
        nbytes=13 * MIB,
        name="outer_grad",
    )


def inner_back_kernel(
    vec, go, inner, wout, wi, n1, inv1, wo, gi, isum, gb, gm, sums, acc
):
    i = pl.program_id(0)
    count, width = go.shape

    @pl.when(i == 0)
    def _():
        acc[...] = go[...].astype(F32)

    made = (gelu_slope(inner[0].astype(F32)) * dot(go[...], wout[...], NT)).astype(BF)
    gi[0] = made
    isum[0] = jnp.broadcast_to(col_sum(made.astype(F32)), (8, width))
    acc[...] += dot(made, wi[...], NT)

    @pl.when(i == pl.num_programs(0) - 1)
    def _():
        gain = vec[V_G1 : V_G1 + 1, :]
        piece = 256
        sums[...] = jnp.zeros(sums.shape, F32)

        def step(j, carry):
            at = pl.ds(pl.multiple_of(j * piece, piece), piece)
            grad = acc[at, :]
            normal = n1[at, :].astype(F32)
            low = norm_back(grad, normal, inv1[at, :], gain).astype(BF)
            gb[at, :] = low
            gm[at, :] = dot(low, wo[...], NT).astype(BF)
            sums[0:1, :] += col_sum(grad * normal)
            sums[1:2, :] += col_sum(grad)
            sums[2:3, :] += col_sum(low.astype(F32))
            return carry

        lax.fori_loop(0, count // piece, step, 0)


def inner_back(deps, vecs, go, inner, wout, wi, n1, inv1, wo):
    parts, count, width = inner.shape
    whole = lambda a: pl.BlockSpec(a.shape, lambda i: (0,) * a.ndim)
    full = pl.BlockSpec((count, width), lambda i: (0, 0))
    chunk = pl.BlockSpec((1, count, width), lambda i: (i, 0, 0))
    return run(
        inner_back_kernel,
        deps,
        (vecs, go, inner, wout, wi, n1, inv1, wo),
        [
            shape((parts, count, width)),
            shape((parts, 8, width), F32),
            shape((count, width)),
            shape((count, width)),
            shape((8, width), F32),
        ],
        [
            whole(vecs),
            full,
            chunk,
            pl.BlockSpec((width, width), lambda i: (i, 0)),
            pl.BlockSpec((width, width), lambda i: (0, i)),
            full,
            whole(inv1),
            whole(wo),
        ],
        [
            chunk,
            pl.BlockSpec((1, 8, width), lambda i: (i, 0, 0)),
            full,
            full,
            pl.BlockSpec((8, width), lambda i: (0, 0)),
        ],
        scratch=[pltpu.VMEM((count, width), F32)],
        grid=(parts,),
        flops=2 * count * width * width * (2 * parts + 1),
        nbytes=30 * MIB,
        name="inner_back",
    )


def inner_grad_kernel(meta, low1, gi, send, keep, across):
    i = pl.program_id(0)

    @pl.when(i == 0)
    def _():
        across[...] = low1[...].T

    made = dot(across[...], gi[0]).astype(BF)

    @pl.when(i < 2)
    def _():
        send[i] = made

    @pl.when(i >= 2)
    def _():
        keep[i - 2] = made


def inner_grad(deps, meta, low1, gi):
    parts, count, width = gi.shape
    out = pl.BlockSpec((2, width, width), lambda i, m: (0, 0, 0))
    return run(
        inner_grad_kernel,
        deps,
        (meta, low1, gi),
        [shape((2, width, width))] * 2,
        [
            pl.BlockSpec((count, width), lambda i, m: (0, 0)),
            pl.BlockSpec((1, count, width), lambda i, m: (quarter_of(i, m[0]), 0, 0)),
        ],
        [out] * 2,
        scratch=[pltpu.VMEM((width, count), BF)],
        grid=(parts,),
        prefetch=1,
        flops=2 * count * width * width * parts,
        nbytes=13 * MIB,
        name="inner_grad",
    )


def attention_back_kernel(wins, q, k, v, probs, gm, dq, dk, dv, sums, dk_acc, dv_acc):
    masks = head_masks()
    dk_acc[...] = jnp.zeros(dk_acc.shape, F32)
    dv_acc[...] = jnp.zeros(dv_acc.shape, F32)
    q_sum = jnp.zeros((1, LANES), F32)
    for w in range(wins):
        here = pl.ds(w * WIN, WIN)
        span = pl.ds(w * WIN, 3 * WIN)
        grad_out = twice(gm[0, here, :], masks)
        queries = twice(q[0, here, :], masks)
        chance_low = probs[0, w]
        chance = chance_low.astype(F32)
        grad_probs = dot(v[0, span, :], grad_out, NT)
        product = chance * grad_probs
        grad_scores = (product - chance * jnp.sum(product, axis=0, keepdims=True)).astype(BF)
        dv_acc[span, :] += dot(chance_low, grad_out)
        dk_acc[span, :] += dot(grad_scores, queries)
        stacked = jnp.concatenate([grad_scores[:, :LANES], grad_scores[:, LANES:]], axis=0)
        made = dot(stacked, twice(k[0, span, :], masks), TN) * HEAD_DIM**-0.5
        low = made.astype(BF)
        dq[0, here, :] = low
        q_sum = q_sum + col_sum(low.astype(F32))
    dk[0] = dk_acc[...].astype(BF)
    made = dv_acc[...]
    dv[0] = made.astype(BF)
    sums[0, 0:1, :] = q_sum
    sums[0, 1:2, :] = col_sum(made)
    sums[0, 2:, :] = jnp.zeros((6, LANES), F32)


def attention_back(deps, q, kv, probs, gm, rows):
    count, width = q.shape
    block = count // rows
    wins = block // WIN
    ext = kv.shape[1]
    pairs = width // LANES
    own = pl.BlockSpec((1, block, LANES), lambda r, p: (r, 0, p))
    keys = pl.BlockSpec((1, ext, LANES), lambda r, p: (r, 0, p))
    values = pl.BlockSpec((1, ext, LANES), lambda r, p: (rows + r, 0, p))
    return run(
        functools.partial(attention_back_kernel, wins),
        deps,
        (q.reshape(rows, block, width), kv, kv, probs, gm.reshape(rows, block, width)),
        [
            shape((rows, block, width)),
            shape((rows, ext, width)),
            shape((rows, ext, width)),
            shape((rows, 8, width), F32),
        ],
        [
            own,
            keys,
            values,
            pl.BlockSpec((1, wins, 3 * WIN, 2 * LANES), lambda r, p: (r * pairs + p, 0, 0, 0)),
            own,
        ],
        [own, keys, keys, pl.BlockSpec((1, 8, LANES), lambda r, p: (r, 0, p))],
        scratch=[pltpu.VMEM((ext, LANES), F32)] * 2,
        grid=(rows, pairs),
        flops=4 * 2 * count * 3 * WIN * width * 4,
        nbytes=24 * MIB,
        name="attention_back",
    )


VEC_ROWS = 32


def project_grad_kernel(
    meta, dq, dk, dv, gb, chars, low, high, mixed, sums_a, sums1, sums2, sums3, isum, send, keep, ext, small
):
    rows, full, width = dk.shape
    block = full - 2 * WIN
    count = rows * block
    place = meta[0]
    quarter = width // 4
    for r in range(rows):
        ext[r, 0:WIN, :] = low[r]
        ext[r, WIN : WIN + block, :] = chars[r]
        ext[r, WIN + block :, :] = high[r]
    every = ext[...].reshape(rows * full, width)

    def store(slot, at, value):
        @pl.when(slot < 2)
        def _():
            send[slot, at, :] = value

        @pl.when(slot >= 2)
        def _():
            keep[slot - 2, at, :] = value

    def put(index, made):
        for number in range(4):
            piece = made[number * quarter : (number + 1) * quarter]
            store(slot_of(jnp.int32(number), place), pl.ds(index * quarter, quarter), piece)

    put(0, dot(dq[...].reshape(count, width), chars[...].reshape(count, width), TN).astype(BF))
    put(1, dot(dk[...].reshape(rows * full, width), every, TN).astype(BF))
    put(2, dot(dv[...].reshape(rows * full, width), every, TN).astype(BF))
    put(3, dot(gb[...], mixed[...], TN).astype(BF))

    att = sums_a[0]
    for r in range(1, rows):
        att = att + sums_a[r]
    stack = [att[0:1], att[1:2], sums1[2:3], sums1[0:1], sums1[1:2], sums2[2:3]]
    stack += [sums2[0:1], sums2[1:2], sums3[2:3], sums3[0:1], sums3[1:2]]
    for number in range(4):
        at = slice(number * quarter, (number + 1) * quarter)
        small[...] = jnp.zeros(small.shape, F32)
        for row, vector in enumerate(stack):
            small[row : row + 1, 0:quarter] = vector[:, at]
        for j in range(4):
            small[len(stack) + j : len(stack) + j + 1, 0:quarter] = isum[
                number, 0:1, j * quarter : (j + 1) * quarter
            ]
        store(
            slot_of(jnp.int32(number), place), pl.ds(4 * quarter, VEC_ROWS), small[...].astype(BF)
        )


def project_grad(deps, meta, dq, dk, dv, gb, chars, low, high, mixed, *sums):
    rows, full, width = dk.shape
    count = gb.shape[0]
    return run(
        project_grad_kernel,
        deps,
        (meta, dq, dk, dv, gb, chars, low, high, mixed, *sums),
        [shape((2, width + VEC_ROWS, width))] * 2,
        [spec_smem()] + [spec_vmem()] * (8 + len(sums)),
        [spec_vmem()] * 2,
        scratch=[pltpu.VMEM((rows, full, width), BF), pltpu.VMEM((VEC_ROWS, width), F32)],
        flops=2 * count * width * width * 5,
        nbytes=20 * MIB,
        name="project_grad",
    )


def halo_grad_kernel(dk, dv, wk, wv, low, high):
    rows, full, width = dk.shape
    for side, out in ((0, low), (full - WIN, high)):
        keys = jnp.concatenate([dk[r, side : side + WIN, :] for r in range(rows)], axis=0)
        values = jnp.concatenate([dv[r, side : side + WIN, :] for r in range(rows)], axis=0)
        made = (dot(keys, wk[...], NT) + dot(values, wv[...], NT)).astype(BF)
        for r in range(rows):
            out[r] = made[r * WIN : (r + 1) * WIN]


def halo_grad(deps, dk, dv, wk, wv):
    rows, full, width = dk.shape
    return run(
        halo_grad_kernel,
        deps,
        (dk, dv, wk, wv),
        [shape((rows, WIN, width))] * 2,
        [spec_vmem()] * 4,
        [spec_vmem()] * 2,
        flops=8 * rows * WIN * width * width,
        nbytes=8 * MIB,
        name="halo_grad",
    )


def chars_grad_kernel(gb, dq, dk, dv, low, high, wq, wk, wv, out):
    _, block, width = dq.shape
    own = slice(WIN, WIN + block)
    made = gb[0].astype(F32)
    made = made + dot(dq[0], wq[...], NT)
    made = made + dot(dk[0, own, :], wk[...], NT)
    made = made + dot(dv[0, own, :], wv[...], NT)
    out[0, WIN : block - WIN, :] = made[WIN : block - WIN].astype(BF)
    out[0, 0:WIN, :] = (made[0:WIN] + low[0].astype(F32)).astype(BF)
    out[0, block - WIN :, :] = (made[block - WIN :] + high[0].astype(F32)).astype(BF)


def chars_grad(deps, gb, dq, dk, dv, low, high, wq, wk, wv):
    rows, block, width = dq.shape
    ext = dk.shape[1]
    row = lambda n: pl.BlockSpec((1, n, width), lambda r: (r, 0, 0))
    weight = pl.BlockSpec((width, width), lambda r: (0, 0))
    return run(
        chars_grad_kernel,
        deps,
        (gb.reshape(rows, block, width), dq, dk, dv, low, high, wq, wk, wv),
        shape((rows, block, width)),
        [row(block), row(block), row(ext), row(ext), row(WIN), row(WIN)] + [weight] * 3,
        row(block),
        grid=(rows,),
        flops=6 * rows * block * width * width,
        nbytes=14 * MIB,
        name="chars_grad",
    )


def swap(value, axis, bit):
    count = lax.axis_size(axis)
    return lax.ppermute(value, axis, [(i, i ^ bit) for i in range(count)])


def add_split_kernel(meta, index, left, right, send, keep):
    own = meta[index]
    keep[...] = (left[own].astype(F32) + right[own].astype(F32)).astype(BF)
    send[...] = (left[1 - own].astype(F32) + right[1 - own].astype(F32)).astype(BF)


def add_split(deps, meta, index, left, right, name):
    _, height, width = left.shape
    steps = 2 if height >= 512 else 1
    both = pl.BlockSpec((2, height // steps, width), lambda i, m: (0, i, 0))
    out = pl.BlockSpec((height // steps, width), lambda i, m: (i, 0))

    def kernel(meta_ref, *refs):
        add_split_kernel(meta_ref, index, *refs)

    return run(
        kernel,
        deps,
        (meta, left, right),
        [shape((height, width))] * 2,
        [both, both],
        [out, out],
        grid=(steps,),
        prefetch=1,
        mib=24,
        flops=2 * height * width,
        nbytes=12 * height * width,
        name=name,
    )


def add_kernel(left, right, out):
    out[...] = (left[...].astype(F32) + right[...].astype(F32)).astype(BF)


def add(deps, left, right, name):
    return run(
        add_kernel,
        deps,
        (left, right),
        shape(left.shape),
        [spec_vmem()] * 2,
        spec_vmem(),
        mib=24,
        flops=left.size,
        nbytes=6 * left.size,
        name=name,
    )


def finish_kernel(kind, meta, own, other, *outs):
    height, width = own.shape
    bit = meta[4]
    quarter = width // 4
    first = jnp.where(bit == 0, own[...], other[...])
    second = jnp.where(bit == 0, other[...], own[...])
    if kind == "plain":
        outs[0][0:height, :] = first.astype(F32)
        outs[0][height:, :] = second.astype(F32)
        return
    whole = jnp.concatenate([first, second], axis=0)
    if kind == "wide":
        for j in range(4):
            outs[0][:, j * width : (j + 1) * width] = whole[j * quarter : (j + 1) * quarter].astype(
                F32
            )
        return
    for j in range(4):
        outs[j][...] = whole[j * quarter : (j + 1) * quarter].astype(F32)
    outs[4][...] = whole[4 * quarter : 4 * quarter + 16].astype(F32)


def finish(deps, meta, own, other, kind, name):
    height, width = own.shape
    quarter = width // 4
    if kind == "plain":
        outs = [shape((2 * height, width), F32)]
    elif kind == "wide":
        outs = [shape((quarter, 4 * width), F32)]
    else:
        outs = [shape((quarter, width), F32)] * 4 + [shape((16, width), F32)]
    return run(
        functools.partial(finish_kernel, kind),
        deps,
        (meta, own, other),
        outs,
        [spec_smem()] + [spec_vmem()] * 2,
        [spec_vmem()] * len(outs),
        mib=32,
        flops=height * width,
        nbytes=12 * height * width,
        name=name,
    )


class Chain:
    def __init__(self):
        self.last = ()

    def __call__(self, made, *args, pick=-1):
        outs = made(self.last, *args)
        self.last = ((outs[pick] if isinstance(outs, (tuple, list)) else outs),)
        return outs


class Sum:
    def __init__(self, chain, meta, name, send, keep):
        self.chain, self.meta, self.name = chain, meta, name
        self.keep = keep
        self.arrived = swap(send, "seq", 1)

    def core(self):
        out, self.keep = self.chain(
            add_split, self.meta, 3, self.keep, self.arrived, self.name + "_core"
        )
        self.arrived = swap(out, "seq", 2)

    def side(self):
        height, width = self.keep.shape
        halves = (2, height // 2, width)
        out, self.keep = self.chain(
            add_split,
            self.meta,
            4,
            self.keep.reshape(halves),
            self.arrived.reshape(halves),
            self.name + "_x",
        )
        self.arrived = swap(out, "dp", 1)
        self.bit = 1

    def step(self):
        self.keep = self.chain(
            add, self.keep, self.arrived, self.name + "_d%d" % self.bit
        )
        self.bit *= 2
        more = self.bit < lax.axis_size("dp")
        self.arrived = swap(self.keep, "dp", self.bit if more else 1)
        return more

    def end(self, kind):
        return self.chain(finish, self.meta, self.keep, self.arrived, kind, self.name + "_end")


def shards(
    chars,
    window_mask,
    micro_batch,
    mol_grad,
    query_weight,
    query_bias,
    key_weight,
    value_weight,
    value_bias,
    output_weight,
    output_bias,
    first_gain,
    first_shift,
    inner_weight,
    inner_bias,
    outer_weight,
    outer_bias,
    second_gain,
    second_shift,
    conv_weight,
    conv_bias,
    third_gain,
    third_shift,
):
    rows, block, width = chars.shape
    count = rows * block
    place = lax.axis_index("seq").astype(jnp.int32)
    group = lax.axis_index("dp").astype(jnp.int32)
    meta = jnp.stack([place, place % 2, place // 2, jnp.int32(1), group % 2])
    size = lax.axis_size("seq")
    forward_pairs = [(i, i + 1) for i in range(size - 1)]
    backward_pairs = [(i + 1, i) for i in range(size - 1)]
    low = lax.ppermute(chars[:, block - WIN :], "seq", forward_pairs)
    high = lax.ppermute(chars[:, :WIN], "seq", backward_pairs)
    vecs = jnp.concatenate(
        [
            query_bias,
            value_bias,
            output_bias,
            first_gain,
            first_shift,
            outer_bias,
            second_gain,
            second_shift,
            conv_bias,
            third_gain,
            third_shift,
            inner_bias,
            jnp.zeros((width,), BF),
        ]
    )
    vecs = vecs.reshape(-1, width).astype(F32)
    tokens = chars.reshape(count, width)
    chain = Chain()
    q, k, v = chain(project, tokens, vecs, query_weight, key_weight, value_weight)
    (
        kv,
        probs,
        mixed,
        n1,
        inv1,
        low1,
        inner,
        hidden,
        n2,
        inv2,
        merged,
        gc,
        mol,
        sums3,
        send_c,
        keep_c,
    ) = chain(
        forward,
        meta,
        window_mask,
        micro_batch,
        vecs,
        tokens,
        low,
        high,
        q,
        k,
        v,
        key_weight,
        value_weight,
        output_weight,
        inner_weight,
        outer_weight,
        conv_weight,
        mol_grad.reshape(-1, width),
        pick=13,
    )
    molecules = mol.reshape(mol_grad.shape)
    conv = Sum(chain, meta, "conv", send_c, keep_c)
    go, sums2 = chain(second_back, vecs, gc, conv_weight, n2, inv2)
    conv.core()
    outer = Sum(chain, meta, "outer", *chain(outer_grad, meta, go, hidden))
    gi, isum, gb, gm, sums1 = chain(
        inner_back, vecs, go, inner, outer_weight, inner_weight, n1, inv1, output_weight
    )
    outer.core()
    conv.side()
    inner_sum = Sum(chain, meta, "inner", *chain(inner_grad, meta, low1, gi))
    conv.step()
    dq, dk, dv, sums_a = chain(attention_back, q, kv, probs, gm, rows)
    inner_sum.core()
    conv.step()
    outer.side()
    proj = Sum(
        chain,
        meta,
        "proj",
        *chain(
            project_grad,
            meta,
            dq,
            dk,
            dv,
            gb,
            chars,
            low,
            high,
            mixed,
            sums_a,
            sums1,
            sums2,
            sums3,
            isum,
        ),
    )
    outer.step()
    grad_low, grad_high = chain(halo_grad, dk, dv, key_weight, value_weight)
    from_prev = lax.ppermute(grad_high, "seq", forward_pairs)
    from_next = lax.ppermute(grad_low, "seq", backward_pairs)
    proj.core()
    while conv.step():
        pass
    outer.step()
    inner_sum.side()
    grad_chars = chain(
        chars_grad, gb, dq, dk, dv, from_prev, from_next, query_weight, key_weight, value_weight
    )
    (full_c,) = conv.end("wide")
    inner_sum.step()
    while outer.step():
        pass
    inner_sum.step()
    proj.side()
    (full_u,) = outer.end("wide")
    while inner_sum.step():
        pass
    proj.step()
    (full_i,) = inner_sum.end("plain")
    while proj.step():
        pass
    full_q, full_k, full_v, full_o, small = proj.end("pieces")
    quarter = width // 4
    vec_of = lambda i: small[i, :quarter]
    return (
        molecules,
        grad_chars,
        full_q.T,
        vec_of(0),
        full_k.T,
        full_v.T,
        vec_of(1),
        full_o.T,
        vec_of(2),
        vec_of(3),
        vec_of(4),
        full_i,
        small[11:15, :quarter].reshape(-1),
        full_u.T,
        vec_of(5),
        vec_of(6),
        vec_of(7),
        full_c.T,
        vec_of(8),
        vec_of(9),
        vec_of(10),
    )


def solution(mesh):
    split = P("dp", "seq", None)
    placed = (split, P("dp", None), P("dp"), split) + (P(),) * 19
    by_column, by_place = P(None, "seq"), P("seq")
    outs = (
        split,
        split,
        by_column,
        by_place,
        by_column,
        by_column,
        by_place,
        by_column,
        by_place,
        by_place,
        by_place,
        by_column,
        by_place,
        by_column,
        by_place,
        by_place,
        by_place,
        by_column,
        by_place,
        by_place,
        by_place,
    )
    return jax.shard_map(shards, mesh=mesh, in_specs=placed, out_specs=outs, check_vma=False)
```

```python
import functools

import jax
import jax.numpy as jnp
from jax import lax
from jax.experimental import pallas as pl
from jax.experimental.pallas import tpu as pltpu
from jax.sharding import PartitionSpec as P

HEADS = 12
HEAD_DIM = 64
WIN = 128
DOWN = 4
MICRO = 2
EPSILON = 1e-06
NEG_FILL = -1e30
GELU_A = 0.7978845608028654
GELU_B = 0.044715
BF = jnp.bfloat16
F32 = jnp.float32
LANES = 128
MIB = 1 << 20

NN = (((1,), (0,)), ((), ()))
NT = (((1,), (1,)), ((), ()))
TN = (((0,), (0,)), ((), ()))

(V_QB, V_VB, V_OB, V_G1, V_S1, V_OUTB, V_G2, V_S2, V_CB, V_G3, V_S3, V_IB) = range(12)


def dot(left, right, dims=NN):
    return lax.dot_general(left, right, dims, preferred_element_type=F32)


def gelu_both(u):
    square = u * u
    t = jnp.tanh(u * (GELU_A + (GELU_A * GELU_B) * square))
    half = 0.5 + 0.5 * t
    value = u * half
    slope = half + value * (1.0 - t) * (GELU_A + (3.0 * GELU_A * GELU_B) * square)
    return value, slope


def layer_stats(u):
    center = u - jnp.mean(u, axis=-1, keepdims=True)
    inv_dev = lax.rsqrt(jnp.mean(center * center, axis=-1, keepdims=True) + EPSILON)
    return center * inv_dev, inv_dev


def norm_back(grad_out, normal, inv_dev, gain_vec):
    scaled = grad_out * gain_vec
    return inv_dev * (
        scaled
        - jnp.mean(scaled, axis=-1, keepdims=True)
        - normal * jnp.mean(scaled * normal, axis=-1, keepdims=True)
    )


def col_sum(value):
    return jnp.sum(value, axis=0, keepdims=True)


def params(mib=56, **more):
    return pltpu.CompilerParams(vmem_limit_bytes=mib * MIB, **more)


def cost(flops, nbytes):
    return pl.CostEstimate(flops=int(flops), bytes_accessed=int(nbytes), transcendentals=0)


def spec_any():
    return pl.BlockSpec(memory_space=pl.ANY)


def spec_smem():
    return pl.BlockSpec(memory_space=pltpu.SMEM)


def spec_vmem():
    return pl.BlockSpec(memory_space=pltpu.VMEM)


def shape(dims, dtype=BF):
    return jax.ShapeDtypeStruct(tuple(dims), dtype)


def run(body, deps, args, out_shape, in_specs, out_specs, scratch=(), grid=(), prefetch=0, mib=56, flops=10**12, nbytes=10**6, name=None, aliases=None):
    given = len(args)

    def wrapped(*refs):
        body(*refs[:given], *refs[given + len(deps) :])

    return pl.pallas_call(
        wrapped,
        grid_spec=pltpu.PrefetchScalarGridSpec(
            num_scalar_prefetch=prefetch,
            grid=grid,
            in_specs=list(in_specs) + [spec_any()] * len(deps),
            out_specs=out_specs,
            scratch_shapes=list(scratch),
        ),
        out_shape=out_shape,
        compiler_params=pltpu.CompilerParams(vmem_limit_bytes=mib * MIB),
        cost_estimate=cost(flops, nbytes),
        input_output_aliases=aliases or {},
        name=name,
    )(*args, *deps)


def head_masks():
    lane = lax.broadcasted_iota(jnp.int32, (1, LANES), 1)
    first = jnp.where(lane < HEAD_DIM, 1.0, 0.0).astype(BF)
    return first, (1.0 - first.astype(F32)).astype(BF)


def twice(block, masks):
    return jnp.concatenate([block * masks[0], block * masks[1]], axis=0)


def slot_of(quarter, place):
    same_x = (quarter // 2 == place // 2).astype(jnp.int32)
    same_core = (quarter % 2 == place % 2).astype(jnp.int32)
    return 2 * same_core + same_x


def project_kernel(names, x_ref, *refs):
    vectors, (wq_ref, wk_ref, wv_ref, q_ref, k_ref, v_ref, vec_ref) = refs[:names], refs[names:]
    width = x_ref.shape[1]
    part = wq_ref.shape[1]
    step = pl.program_id(0)

    @pl.when(step == 0)
    def _():
        row = 0
        for ref in vectors:
            value = ref[...].astype(F32)
            for k in range(value.shape[0] // width):
                vec_ref[row : row + 1, :] = value[k * width : (k + 1) * width].reshape(1, width)
                row += 1
        vec_ref[row:, :] = jnp.zeros((vec_ref.shape[0] - row, width), F32)

    x = x_ref[...]
    at = pl.ds(pl.multiple_of(step * part, part), part)
    queries = (dot(x, wq_ref[...]) + vec_ref[V_QB : V_QB + 1, at]).astype(BF)
    q_ref[...] = queries * jnp.asarray(HEAD_DIM**-0.5, BF)
    k_ref[...] = dot(x, wk_ref[...]).astype(BF)
    v_ref[...] = (dot(x, wv_ref[...]) + vec_ref[V_VB : V_VB + 1, at]).astype(BF)


def project(deps, tokens, vectors, wq, wk, wv):
    count, width = tokens.shape
    part = 256
    column = pl.BlockSpec((width, part), lambda i: (0, i))
    out = pl.BlockSpec((count, part), lambda i: (0, i))
    height = rounded_up(sum(v.shape[0] for v in vectors) // width, 8)
    return run(
        functools.partial(project_kernel, len(vectors)),
        deps,
        (tokens, *vectors, wq, wk, wv),
        [shape((count, width))] * 3 + [shape((height, width), F32)],
        [pl.BlockSpec((count, width), lambda i: (0, 0))]
        + [pl.BlockSpec(v.shape, lambda i: (0,)) for v in vectors]
        + [column] * 3,
        [out] * 3 + [pl.BlockSpec((height, width), lambda i: (0, 0))],
        grid=(width // part,),
        mib=60,
        name="project",
    )


def forward_kernel(
    rows,
    wins,
    windows_all,
    meta,
    wmask,
    mbatch,
    vec,
    chars_h,
    low_h,
    high_h,
    q_h,
    k_h,
    v_h,
    wk_h,
    wv_h,
    wo_h,
    wi_h,
    wout_h,
    wc_h,
    mg_h,
    kv_o,
    pt_o,
    mixed_o,
    n1_o,
    inv1_o,
    low1_o,
    slope_o,
    hidden_o,
    mol_o,
    go_o,
    sums_o,
    send_o,
    keep_o,
    q,
    kv,
    halo,
    wkv,
    wo,
    chars,
    wi,
    wout,
    wc,
    mg,
    probs,
    mixed,
    acc,
    strips,
    low1,
    n1,
    inv1,
    slope,
    hidden,
    n2,
    inv2,
    merged,
    mol,
    sem_in,
    sem_p,
    sem_h,
    sem_out,
):
    place = meta[0]
    block = wins * WIN
    width = chars.shape[-1]
    count = rows * block
    pairs = width // LANES
    parts = wi.shape[1] // width

    def copy_in(index, src, dst):
        made = pltpu.make_async_copy(src, dst, sem_in.at[index])
        made.start()
        return made

    halo_in = [
        copy_in(0, low_h, halo.at[0]),
        copy_in(1, high_h, halo.at[1]),
        copy_in(2, wk_h, wkv.at[0]),
        copy_in(3, wv_h, wkv.at[1]),
    ]
    qkv_in = [copy_in(4, q_h, q)]
    for r in range(rows):
        qkv_in.append(
            copy_in(5 + 2 * r, k_h.at[pl.ds(r * block, block)], kv.at[r, pl.ds(WIN, block)])
        )
        qkv_in.append(
            copy_in(
                6 + 2 * r, v_h.at[pl.ds(r * block, block)], kv.at[rows + r, pl.ds(WIN, block)]
            )
        )
    base = 5 + 2 * rows

    def copy_out(index, src, dst):
        made = pltpu.make_async_copy(src, dst, sem_out.at[index])
        made.start()
        return made

    for made in halo_in:
        made.wait()
    beside = halo[...].reshape(2 * rows * WIN, width)
    keys = dot(beside, wkv[0]).astype(BF)
    values = (dot(beside, wkv[1]) + vec[V_VB : V_VB + 1, :]).astype(BF)
    for side in range(2):
        start = side * (block + WIN)
        for r in range(rows):
            at = (side * rows + r) * WIN
            kv[r, pl.ds(start, WIN), :] = keys[at : at + WIN]
            kv[rows + r, pl.ds(start, WIN), :] = values[at : at + WIN]
    for made in qkv_in:
        made.wait()
    wo_in = copy_in(base, wo_h, wo)
    chars_in = copy_in(base + 1, chars_h, chars)
    wi_in = copy_in(base + 2, wi_h, wi)
    wout_in = copy_in(base + 3, wout_h, wout)
    kv_out = copy_out(0, kv, kv_o)

    masks = head_masks()

    def pair_step(it, carry):
        r = it // pairs
        pair = it % pairs
        slot = it % 2
        lanes = pl.ds(pl.multiple_of(pair * LANES, LANES), LANES)

        @pl.when(it >= 2)
        def _():
            pltpu.make_async_copy(probs.at[slot], pt_o.at[it - 2], sem_p.at[slot]).wait()

        for w in range(wins):
            at = place * wins + w
            low_ok = (at >= 1) & (wmask[r, jnp.maximum(at - 1, 0)] > 0)
            high_ok = (at + 1 < windows_all) & (wmask[r, jnp.minimum(at + 1, windows_all - 1)] > 0)
            queries = twice(q[pl.ds(r * block + w * WIN, WIN), lanes], masks)
            scores = dot(kv[r, pl.ds(w * WIN, 3 * WIN), lanes], queries, NT)
            scores = jnp.concatenate(
                [
                    scores[0:WIN] + jnp.where(low_ok, 0.0, NEG_FILL),
                    scores[WIN : 2 * WIN],
                    scores[2 * WIN :] + jnp.where(high_ok, 0.0, NEG_FILL),
                ],
                axis=0,
            )
            shifted = jnp.exp(scores - jnp.max(scores, axis=0, keepdims=True))
            total = jnp.sum(shifted, axis=0, keepdims=True)
            chance = (shifted * (1.0 / total)).astype(BF)
            probs[slot, w] = chance
            stacked = jnp.concatenate([chance[:, :LANES], chance[:, LANES:]], axis=0)
            values_win = twice(kv[rows + r, pl.ds(w * WIN, 3 * WIN), lanes], masks)
            mixed[pl.ds(r * block + w * WIN, WIN), lanes] = dot(stacked, values_win, TN).astype(BF)
        pltpu.make_async_copy(probs.at[slot], pt_o.at[it], sem_p.at[slot]).start()
        return carry

    steps = rows * pairs
    lax.fori_loop(0, steps, pair_step, 0)
    mixed_out = copy_out(1, mixed, mixed_o)

    wo_in.wait()
    chars_in.wait()
    wc_in = copy_in(base + 4, wc_h, wc)
    mg_in = copy_in(base + 5, mg_h, mg)
    piece = 256

    def first_step(i, carry):
        at = pl.ds(pl.multiple_of(i * piece, piece), piece)
        u = dot(mixed[at, :], wo[...]) + vec[V_OB : V_OB + 1, :] + chars[at, :].astype(F32)
        normal, inv = layer_stats(u)
        first = normal * vec[V_G1 : V_G1 + 1, :] + vec[V_S1 : V_S1 + 1, :]
        n1[at, :] = normal.astype(BF)
        inv1[at, :] = inv
        low1[at, :] = first.astype(BF)
        acc[at, :] = first + vec[V_OUTB : V_OUTB + 1, :]
        return carry

    lax.fori_loop(0, count // piece, first_step, 0, unroll=True)
    outs = [mixed_out, copy_out(2, n1, n1_o), copy_out(3, inv1, inv1_o), copy_out(4, low1, low1_o)]

    wi_in.wait()
    wout_in.wait()

    def ffn_step(c, carry):
        slot = c % 2
        columns = pl.ds(pl.multiple_of(c * width, width), width)

        @pl.when(c >= 2)
        def _():
            pltpu.make_async_copy(slope.at[slot], slope_o.at[c - 2], sem_h.at[slot]).wait()
            pltpu.make_async_copy(hidden.at[slot], hidden_o.at[c - 2], sem_h.at[2 + slot]).wait()

        value, steep = gelu_both(dot(low1[...], wi[:, columns]) + vec[pl.ds(V_IB + c, 1), :])
        slope[slot] = steep.astype(BF)
        h = value.astype(BF)
        hidden[slot] = h
        acc[...] += dot(h, wout[columns, :])
        pltpu.make_async_copy(slope.at[slot], slope_o.at[c], sem_h.at[slot]).start()
        pltpu.make_async_copy(hidden.at[slot], hidden_o.at[c], sem_h.at[2 + slot]).start()
        return carry

    lax.fori_loop(0, parts, ffn_step, 0)

    def second_step(i, carry):
        at = pl.ds(pl.multiple_of(i * piece, piece), piece)
        normal, inv = layer_stats(acc[at, :])
        n2[at, :] = normal.astype(BF)
        inv2[at, :] = inv
        second = normal * vec[V_G2 : V_G2 + 1, :] + vec[V_S2 : V_S2 + 1, :]
        for t in range(pairs):
            strips[t, at, :] = second[:, t * LANES : (t + 1) * LANES]
        return carry

    lax.fori_loop(0, count // piece, second_step, 0, unroll=True)

    wc_in.wait()
    mg_in.wait()
    mols = count // DOWN
    conv = jnp.zeros((mols, width), F32) + vec[V_CB : V_CB + 1, :]
    for i in range(DOWN):
        for t in range(pairs):
            merged[i, :, t * LANES : (t + 1) * LANES] = strips[
                t, pl.ds(i, mols, stride=DOWN), :
            ].astype(BF)
        part = merged[i]
        conv = conv + dot(part, wc[pl.ds(i * width, width), :])
    value, steep = gelu_both(conv)
    normal, inv = layer_stats(value)
    per_win = WIN // DOWN
    which = lax.broadcasted_iota(jnp.int32, (mols, 1), 0) // per_win
    live = jnp.zeros((mols, 1), F32)
    total = jnp.ones((mols, 1), F32)
    lengths = []
    for r in range(rows):
        length = wmask[r, 0]
        for w in range(1, windows_all):
            length = length + wmask[r, w]
        lengths.append(length)
    for r in range(rows):
        same = jnp.int32(0)
        for other in range(rows):
            same = same + jnp.where(mbatch[other] == mbatch[r], lengths[other], 0)
        same = (same * per_win).astype(F32)
        for w in range(wins):
            here = which == r * wins + w
            live = jnp.where(here, wmask[r, place * wins + w].astype(F32), live)
            total = jnp.where(here, same, total)
    weight = (rows // MICRO * windows_all * per_win) / total
    gain = vec[V_G3 : V_G3 + 1, :]
    mol[...] = ((normal * gain + vec[V_S3 : V_S3 + 1, :]) * live).astype(BF)
    outs.append(copy_out(5, mol, mol_o))
    grad_mol = mg[...].astype(F32) * (weight * live)
    grad_conv = (steep * norm_back(grad_mol, normal, inv, gain)).astype(BF)
    sums_o[0:1, :] = col_sum(grad_mol * normal)
    sums_o[1:2, :] = col_sum(grad_mol)
    sums_o[2:3, :] = col_sum(grad_conv.astype(F32))
    sums_o[3:, :] = jnp.zeros((sums_o.shape[0] - 3, width), F32)

    kv_out.wait()
    across = grad_conv.T
    quarter = width // 4
    for i in range(DOWN):
        made = dot(across, merged[i]).astype(BF)
        for number in range(4):
            kv[slot_of(jnp.int32(number), place), pl.ds(i * quarter, quarter), :] = made[
                number * quarter : (number + 1) * quarter
            ]
    outs.append(copy_out(6, kv.at[pl.ds(0, 2)], send_o))
    outs.append(copy_out(7, kv.at[pl.ds(2, 2)], keep_o))

    for i in range(DOWN):
        made = dot(grad_conv, wc[pl.ds(i * width, width), :], NT)
        for t in range(pairs):
            strips[t, pl.ds(i, mols, stride=DOWN), :] = made[:, t * LANES : (t + 1) * LANES]
    gain = vec[V_G2 : V_G2 + 1, :]

    def back_step(i, carry):
        at = pl.ds(pl.multiple_of(i * piece, piece), piece)
        grad = jnp.concatenate([strips[t, at, :] for t in range(pairs)], axis=1)
        normal = n2[at, :].astype(F32)
        made = norm_back(grad, normal, inv2[at, :], gain).astype(BF)
        n2[at, :] = made
        sums_o[3:4, :] += col_sum(grad * normal)
        sums_o[4:5, :] += col_sum(grad)
        sums_o[5:6, :] += col_sum(made.astype(F32))
        return carry

    lax.fori_loop(0, count // piece, back_step, 0, unroll=True)
    outs.append(copy_out(8, n2, go_o))

    for made in outs:
        made.wait()
    for it in range(max(0, steps - 2), steps):
        pltpu.make_async_copy(probs.at[it % 2], pt_o.at[it], sem_p.at[it % 2]).wait()
    for c in range(max(0, parts - 2), parts):
        pltpu.make_async_copy(slope.at[c % 2], slope_o.at[c], sem_h.at[c % 2]).wait()
        pltpu.make_async_copy(hidden.at[c % 2], hidden_o.at[c], sem_h.at[2 + c % 2]).wait()


def forward(deps, meta, wmask, mbatch, vecs, chars, low, high, q, k, v, wk, wv, wo, wi, wout, wc, mg):
    rows = wmask.shape[0]
    windows_all = wmask.shape[1]
    count, width = q.shape
    block = count // rows
    wins = block // WIN
    ff = wi.shape[1]
    parts = ff // width
    mols = count // DOWN
    pairs = width // LANES
    ext = block + 2 * WIN
    outs = [
        shape((2 * rows, ext, width)),
        shape((rows * pairs, wins, 3 * WIN, 2 * LANES)),
        shape((count, width)),
        shape((count, width)),
        shape((count, 1), F32),
        shape((count, width)),
        shape((parts, count, width)),
        shape((parts, count, width)),
        shape((mols, width)),
        shape((count, width)),
        shape((8, width), F32),
        shape((2, DOWN * width // 4, width)),
        shape((2, DOWN * width // 4, width)),
    ]
    out_specs = [spec_any()] * len(outs)
    out_specs[10] = spec_vmem()
    return run(
        functools.partial(forward_kernel, rows, wins, windows_all),
        deps,
        (meta, wmask, mbatch, vecs, chars, low, high, q, k, v, wk, wv, wo, wi, wout, wc, mg),
        outs,
        [spec_smem()] * 3 + [spec_vmem()] + [spec_any()] * 13,
        out_specs,
        scratch=[
            pltpu.VMEM((count, width), BF),
            pltpu.VMEM((2 * rows, ext, width), BF),
            pltpu.VMEM((2, rows, WIN, width), BF),
            pltpu.VMEM((2, width, width), BF),
            pltpu.VMEM((width, width), BF),
            pltpu.VMEM((count, width), BF),
            pltpu.VMEM((width, ff), BF),
            pltpu.VMEM((ff, width), BF),
            pltpu.VMEM((DOWN * width, width), BF),
            pltpu.VMEM((mols, width), BF),
            pltpu.VMEM((2, wins, 3 * WIN, 2 * LANES), BF),
            pltpu.VMEM((count, width), BF),
            pltpu.VMEM((count, width), F32),
            pltpu.VMEM((pairs, count, LANES), F32),
            pltpu.VMEM((count, width), BF),
            pltpu.VMEM((count, width), BF),
            pltpu.VMEM((count, 1), F32),
            pltpu.VMEM((2, count, width), BF),
            pltpu.VMEM((2, count, width), BF),
            pltpu.VMEM((count, width), BF),
            pltpu.VMEM((count, 1), F32),
            pltpu.VMEM((DOWN, mols, width), BF),
            pltpu.VMEM((mols, width), BF),
            pltpu.SemaphoreType.DMA((11 + 2 * rows,)),
            pltpu.SemaphoreType.DMA((2,)),
            pltpu.SemaphoreType.DMA((4,)),
            pltpu.SemaphoreType.DMA((9,)),
        ],
        mib=60,
        name="forward",
    )


def outer_grad_kernel(meta, go, hidden, send, keep, across):
    place = meta[0]
    width = go.shape[1]
    quarter = width // 4

    @pl.when(pl.program_id(0) == 0)
    def _():
        turned = go[...].T
        for number in range(4):
            across[slot_of(jnp.int32(number), place)] = turned[
                number * quarter : (number + 1) * quarter
            ]

    left = across[...].reshape(width, go.shape[0])
    made = dot(left, hidden[0]).astype(BF)
    for j in range(2):
        send[j] = made[j * quarter : (j + 1) * quarter]
        keep[j] = made[(2 + j) * quarter : (3 + j) * quarter]


def outer_grad(deps, meta, go, hidden):
    parts, count, width = hidden.shape
    quarter = width // 4
    out = pl.BlockSpec((2, quarter, width), lambda i, m: (0, i, 0))
    return run(
        outer_grad_kernel,
        deps,
        (meta, go, hidden),
        [shape((2, parts * quarter, width))] * 2,
        [
            pl.BlockSpec((count, width), lambda i, m: (0, 0)),
            pl.BlockSpec((1, count, width), lambda i, m: (i, 0, 0)),
        ],
        [out] * 2,
        scratch=[pltpu.VMEM((4, quarter, count), BF)],
        grid=(parts,),
        prefetch=1,
        name="outer_grad",
    )


def inner_back_kernel(
    meta,
    vec,
    go,
    slope,
    wout,
    wi,
    low1,
    n1_h,
    inv1_h,
    wo_h,
    mixed_h,
    send,
    keep,
    isum,
    gb,
    gm,
    sums,
    acc,
    across,
    n1,
    inv1,
    wo,
    mixed,
    sem,
):
    i = pl.program_id(0)
    count, width = go.shape
    place = meta[0]
    late = [
        pltpu.make_async_copy(src, dst, sem.at[k])
        for k, (src, dst) in enumerate(((n1_h, n1), (inv1_h, inv1), (wo_h, wo), (mixed_h, mixed)))
    ]

    @pl.when(i == 0)
    def _():
        for made in late:
            made.start()
        acc[...] = go[...].astype(F32)
        across[...] = low1[...].T

    made = (slope[0].astype(F32) * dot(go[...], wout[...], NT)).astype(BF)
    isum[0] = jnp.broadcast_to(col_sum(made.astype(F32)), (8, width))
    acc[...] += dot(made, wi[...], NT)
    grad = dot(across[...], made).astype(BF)
    slot = slot_of(i, place)

    store_slot(send, keep, slot, pl.ds(0, width), grad)

    @pl.when(i == pl.num_programs(0) - 1)
    def _():
        for made in late:
            made.wait()
        gain = vec[V_G1 : V_G1 + 1, :]
        piece = 256
        sums[...] = jnp.zeros(sums.shape, F32)

        def step(j, carry):
            at = pl.ds(pl.multiple_of(j * piece, piece), piece)
            grad = acc[at, :]
            normal = n1[at, :].astype(F32)
            low = norm_back(grad, normal, inv1[at, :], gain).astype(BF)
            gb[at, :] = low
            gm[at, :] = dot(low, wo[...], NT).astype(BF)
            sums[0:1, :] += col_sum(grad * normal)
            sums[1:2, :] += col_sum(grad)
            sums[2:3, :] += col_sum(low.astype(F32))
            return carry

        lax.fori_loop(0, count // piece, step, 0, unroll=True)
        grad = dot(gb[...], mixed[...], TN).astype(BF)
        quarter = width // 4
        rest = send.shape[1] - width - quarter
        for number in range(4):
            slot = slot_of(jnp.int32(number), place)
            mine = grad[number * quarter : (number + 1) * quarter]
            store_slot(send, keep, slot, pl.ds(width, quarter), mine)
        for ref in (send, keep):
            for j in range(2):
                ref[j, pl.ds(width + quarter, rest), :] = jnp.zeros((rest, width), BF)


def store_slot(send, keep, slot, at, value):
    @pl.when(slot < 2)
    def _():
        send[slot, at, :] = value

    @pl.when(slot >= 2)
    def _():
        keep[slot - 2, at, :] = value


def rounded_up(value, unit):
    return -(-value // unit) * unit


def once(dims):
    return pl.BlockSpec(dims, lambda i, m: (0,) * len(dims), pipeline_mode=pl.Buffered(1))


def inner_back(deps, meta, vecs, go, slope, wout, wi, low1, n1, inv1, wo, mixed):
    parts, count, width = slope.shape
    full = once((count, width))
    height = rounded_up(width + width // 4, 8 * 16)
    pair = once((2, height, width))
    return run(
        inner_back_kernel,
        deps,
        (meta, vecs, go, slope, wout, wi, low1, n1, inv1, wo, mixed),
        [
            shape((2, height, width)),
            shape((2, height, width)),
            shape((parts, 8, width), F32),
            shape((count, width)),
            shape((count, width)),
            shape((8, width), F32),
        ],
        [
            once(vecs.shape),
            full,
            pl.BlockSpec((1, count, width), lambda i, m: (i, 0, 0)),
            pl.BlockSpec((width, width), lambda i, m: (i, 0)),
            pl.BlockSpec((width, width), lambda i, m: (0, i)),
            full,
            spec_any(),
            spec_any(),
            spec_any(),
            spec_any(),
        ],
        [
            pair,
            pair,
            pl.BlockSpec((1, 8, width), lambda i, m: (i, 0, 0)),
            full,
            full,
            once((8, width)),
        ],
        scratch=[
            pltpu.VMEM((count, width), F32),
            pltpu.VMEM((width, count), BF),
            pltpu.VMEM((count, width), BF),
            pltpu.VMEM((count, 1), F32),
            pltpu.VMEM((width, width), BF),
            pltpu.VMEM((count, width), BF),
            pltpu.SemaphoreType.DMA((4,)),
        ],
        grid=(parts,),
        prefetch=1,
        name="inner_back",
    )


def attention_back_kernel(wins, q, k, v, probs, gm, dq, dk, dv, sums, dk_acc, dv_acc):
    masks = head_masks()
    dk_acc[...] = jnp.zeros(dk_acc.shape, F32)
    dv_acc[...] = jnp.zeros(dv_acc.shape, F32)
    q_sum = jnp.zeros((1, LANES), F32)
    for w in range(wins):
        here = pl.ds(w * WIN, WIN)
        span = pl.ds(w * WIN, 3 * WIN)
        grad_out = twice(gm[0, here, :], masks)
        queries = twice(q[0, here, :], masks)
        chance_low = probs[0, w]
        chance = chance_low.astype(F32)
        grad_probs = dot(v[0, span, :], grad_out, NT)
        product = chance * grad_probs
        grad_scores = (product - chance * jnp.sum(product, axis=0, keepdims=True)).astype(BF)
        dv_acc[span, :] += dot(chance_low, grad_out)
        dk_acc[span, :] += dot(grad_scores, queries)
        stacked = jnp.concatenate([grad_scores[:, :LANES], grad_scores[:, LANES:]], axis=0)
        made = dot(stacked, twice(k[0, span, :], masks), TN) * HEAD_DIM**-0.5
        low = made.astype(BF)
        dq[0, here, :] = low
        q_sum = q_sum + col_sum(low.astype(F32))
    dk[0] = dk_acc[...].astype(BF)
    made = dv_acc[...]
    dv[0] = made.astype(BF)
    sums[0, 0:1, :] = q_sum
    sums[0, 1:2, :] = col_sum(made)
    sums[0, 2:, :] = jnp.zeros((6, LANES), F32)


def attention_back(deps, q, kv, probs, gm, rows, row, before):
    count, width = q.shape
    block = count // rows
    wins = block // WIN
    ext = kv.shape[1]
    pairs = width // LANES
    own = pl.BlockSpec((1, block, LANES), lambda p: (row, 0, p))
    keys = pl.BlockSpec((1, ext, LANES), lambda p: (row, 0, p))
    values = pl.BlockSpec((1, ext, LANES), lambda p: (rows + row, 0, p))

    def body(q, k, v, probs, gm, *refs):
        attention_back_kernel(wins, q, k, v, probs, gm, *refs[len(before) :])

    return run(
        body,
        deps,
        (q.reshape(rows, block, width), kv, kv, probs, gm.reshape(rows, block, width), *before),
        [
            shape((rows, block, width)),
            shape((rows, ext, width)),
            shape((rows, ext, width)),
            shape((rows, 8, width), F32),
        ],
        [
            own,
            keys,
            values,
            pl.BlockSpec((1, wins, 3 * WIN, 2 * LANES), lambda p: (row * pairs + p, 0, 0, 0)),
            own,
        ]
        + [spec_any()] * len(before),
        [own, keys, keys, pl.BlockSpec((1, 8, LANES), lambda p: (row, 0, p))],
        scratch=[pltpu.VMEM((ext, LANES), F32)] * 2,
        grid=(pairs,),
        mib=56,
        aliases={5 + k: k for k in range(len(before))},
        name="attention_back%d" % row,
    )


VEC_ROWS = 64


def project_grad_kernel(
    meta,
    dq_h,
    chars_h,
    dk_h,
    low_h,
    high_h,
    dv_h,
    wk_h,
    wv_h,
    sums_a,
    sums1,
    sums3,
    isum,
    send_o,
    keep_o,
    glow_o,
    ghigh_o,
    dq,
    dk,
    dv,
    ext,
    wk,
    wv,
    glow,
    ghigh,
    made_all,
    small,
    sem_in,
    sem_out,
):
    rows, full, width = dk.shape
    block = full - 2 * WIN
    count = rows * block
    place = meta[0]
    quarter = width // 4
    started = []
    pairs = [
        (dq_h, dq),
        (chars_h, ext.at[:, pl.ds(WIN, block)]),
        (dk_h, dk),
        (low_h, ext.at[:, pl.ds(0, WIN)]),
        (high_h, ext.at[:, pl.ds(WIN + block, WIN)]),
        (dv_h, dv),
        (wk_h, wk),
        (wv_h, wv),
    ]
    for k, (src, dst) in enumerate(pairs):
        started.append(pltpu.make_async_copy(src, dst, sem_in.at[k]))
        started[-1].start()
    leaving = []

    def leave(src, dst):
        leaving.append(pltpu.make_async_copy(src, dst, sem_out.at[len(leaving)]))
        leaving[-1].start()

    def put(index, made):
        at = pl.ds(index * quarter, quarter)
        for number in range(4):
            made_all[slot_of(jnp.int32(number), place), at, :] = made[
                number * quarter : (number + 1) * quarter
            ]
        leave(made_all.at[pl.ds(0, 2), at], send_o.at[:, at])
        leave(made_all.at[pl.ds(2, 2), at], keep_o.at[:, at])

    att = sums_a[0]
    for r in range(1, rows):
        att = att + sums_a[r]
    stack = [att[0:1], att[1:2], sums1[2:3], sums1[0:1], sums1[1:2], sums3[5:6]]
    stack += [sums3[3:4], sums3[4:5], sums3[2:3], sums3[0:1], sums3[1:2]]
    at = pl.ds(3 * quarter, VEC_ROWS)
    for number in range(4):
        mine = slice(number * quarter, (number + 1) * quarter)
        small[...] = jnp.zeros(small.shape, F32)
        for row, vector in enumerate(stack):
            small[row : row + 1, 0:quarter] = vector[:, mine]
        for j in range(4):
            small[len(stack) + j : len(stack) + j + 1, 0:quarter] = isum[
                number, 0:1, j * quarter : (j + 1) * quarter
            ]
        made_all[slot_of(jnp.int32(number), place), at, :] = small[...].astype(BF)
    leave(made_all.at[pl.ds(0, 2), at], send_o.at[:, at])
    leave(made_all.at[pl.ds(2, 2), at], keep_o.at[:, at])

    started[0].wait()
    started[1].wait()
    own = ext[:, WIN : WIN + block, :].reshape(count, width)
    put(0, dot(dq[...].reshape(count, width), own, TN).astype(BF))
    started[2].wait()
    started[3].wait()
    started[4].wait()
    every = ext[...].reshape(rows * full, width)
    put(1, dot(dk[...].reshape(rows * full, width), every, TN).astype(BF))
    started[5].wait()
    put(2, dot(dv[...].reshape(rows * full, width), every, TN).astype(BF))
    started[6].wait()
    started[7].wait()
    for side, out, out_o in ((0, glow, glow_o), (full - WIN, ghigh, ghigh_o)):
        keys = jnp.concatenate([dk[r, side : side + WIN, :] for r in range(rows)], axis=0)
        values = jnp.concatenate([dv[r, side : side + WIN, :] for r in range(rows)], axis=0)
        made = (dot(keys, wk[...], NT) + dot(values, wv[...], NT)).astype(BF)
        for r in range(rows):
            out[r] = made[r * WIN : (r + 1) * WIN]
        leave(out, out_o)
    for made in leaving:
        made.wait()


def project_grad(deps, meta, dq, chars, dk, low, high, dv, wk, wv, *sums):
    rows, full, width = dk.shape
    count = dq.shape[0] * dq.shape[1]
    edge = (rows, WIN, width)
    height = 3 * width // 4 + VEC_ROWS
    return run(
        project_grad_kernel,
        deps,
        (meta, dq, chars, dk, low, high, dv, wk, wv, *sums),
        [shape((2, height, width))] * 2 + [shape(edge)] * 2,
        [spec_smem()] + [spec_any()] * 8 + [spec_vmem()] * len(sums),
        [spec_any()] * 4,
        scratch=[
            pltpu.VMEM(dq.shape, BF),
            pltpu.VMEM(dk.shape, BF),
            pltpu.VMEM(dk.shape, BF),
            pltpu.VMEM(dk.shape, BF),
            pltpu.VMEM((width, width), BF),
            pltpu.VMEM((width, width), BF),
            pltpu.VMEM(edge, BF),
            pltpu.VMEM(edge, BF),
            pltpu.VMEM((4, height, width), BF),
            pltpu.VMEM((VEC_ROWS, width), F32),
            pltpu.SemaphoreType.DMA((8,)),
            pltpu.SemaphoreType.DMA((10,)),
        ],
        name="project_grad",
    )


def chars_grad_kernel(gb, dq, dk, dv, low, high, wq, wk, wv, out):
    _, block, width = dq.shape
    own = slice(WIN, WIN + block)
    made = gb[0].astype(F32)
    made = made + dot(dq[0], wq[...], NT)
    made = made + dot(dk[0, own, :], wk[...], NT)
    made = made + dot(dv[0, own, :], wv[...], NT)
    out[0, WIN : block - WIN, :] = made[WIN : block - WIN].astype(BF)
    out[0, 0:WIN, :] = (made[0:WIN] + low[0].astype(F32)).astype(BF)
    out[0, block - WIN :, :] = (made[block - WIN :] + high[0].astype(F32)).astype(BF)


def chars_grad(deps, gb, dq, dk, dv, low, high, wq, wk, wv):
    rows, block, width = dq.shape
    ext = dk.shape[1]
    row = lambda n: pl.BlockSpec((1, n, width), lambda r: (r, 0, 0))
    weight = pl.BlockSpec((width, width), lambda r: (0, 0))
    return run(
        chars_grad_kernel,
        deps,
        (gb.reshape(rows, block, width), dq, dk, dv, low, high, wq, wk, wv),
        shape((rows, block, width)),
        [row(block), row(block), row(ext), row(ext), row(WIN), row(WIN)] + [weight] * 3,
        row(block),
        grid=(rows,),
        name="chars_grad",
    )


def swap(value, axis, bit):
    count = lax.axis_size(axis)
    return lax.ppermute(value, axis, [(i, i ^ bit) for i in range(count)])


def plus(left, right):
    return (left.astype(F32) + right.astype(F32)).astype(BF)


def add_kernel(left, right, out):
    out[...] = plus(left[...], right[...])


def small_run(body, deps, args, outs, name, smem=1):
    return run(
        body,
        deps,
        args,
        outs,
        [spec_smem()] * smem + [spec_vmem()] * (len(args) - smem),
        [spec_vmem()] * len(outs) if isinstance(outs, list) else spec_vmem(),
        mib=24,
        flops=1,
        nbytes=10**9,
        name=name,
    )


def add(deps, left, right, name):
    return small_run(add_kernel, deps, (left, right), shape(left.shape), name, 0)


def split_kernel(meta, keep, arrived, a_out, a_keep, b_out, b_keep):
    half = keep.shape[1] // 2
    part = half // 2
    mine = meta[1]
    for slot, out in ((0, a_out), (1, a_keep)):
        out[...] = plus(keep[slot, 0:half, :], arrived[slot, 0:half, :])
    for slot in range(2):
        for out, which in ((b_out, 1 - mine), (b_keep, mine)):
            at = pl.ds(pl.multiple_of(half + which * part, 16), part)
            out[slot] = plus(keep[slot, at, :], arrived[slot, at, :])


def cross_kernel(meta, a, a_in, b, b_in, a_out, a_keep, b_out, b_keep):
    part = a.shape[0] // 2
    mine = meta[1]
    for out, which in ((a_out, 1 - mine), (a_keep, mine)):
        at = pl.ds(pl.multiple_of(which * part, 16), part)
        out[...] = plus(a[at, :], a_in[at, :])
    b_out[...] = plus(b[0], b_in[0])
    b_keep[...] = plus(b[1], b_in[1])


def merge_kernel(meta, a, a_in, b, b_in, out, keep):
    part = a.shape[0] // 2
    mine = meta[2]
    for k, (left, right) in enumerate(((a, a_in), (b, b_in))):
        for made, which in ((out, 1 - mine), (keep, mine)):
            at = pl.ds(pl.multiple_of(which * part, 16), part)
            made[k] = plus(left[at, :], right[at, :])


def join_kernel(meta, own, other, out):
    part = own.shape[1]
    mine = meta[2]
    for source, which in ((own, mine), (other, 1 - mine)):
        at = pl.ds(pl.multiple_of(which * part, 16), part)
        for k in range(2):
            out[k, at, :] = source[k]


def end_kernel(plan, meta, own, other, *refs):
    outs, whole = refs[:-1], refs[-1]
    part, width = own.shape[1:]
    mine = meta[1]
    for source, which in ((own, mine), (other, 1 - mine)):
        for k in range(2):
            at = pl.ds(pl.multiple_of((2 * k + which) * part, 16), part)
            whole[at, :] = source[k]
    row = 0
    for out, pieces in zip(outs, plan, strict=True):
        for at, rows in pieces:
            out[:, at * width : (at + 1) * width] = whole[row : row + rows, :].astype(F32)
            row += rows


class Sum:
    def __init__(self, chain, meta, name, send, keep):
        self.chain, self.meta, self.name = chain, meta, name
        self.height, self.width = send.shape[1:]
        self.keep = keep
        self.arrived = swap(send, "seq", 1)

    def split(self):
        height, width = self.height, self.width
        half, part = shape((height // 2, width)), shape((2, height // 4, width))
        a_out, self.a, b_out, self.b = self.chain(
            small_run_of(split_kernel, [half, half, part, part], self.name + "_core"),
            self.meta,
            self.keep,
            self.arrived,
        )
        self.a_in, self.b_in = swap(a_out, "seq", 2), swap(b_out, "dp", 1)

    def cross(self):
        part = shape((self.height // 4, self.width))
        a_out, self.a, b_out, self.b = self.chain(
            small_run_of(cross_kernel, [part] * 4, self.name + "_first"),
            self.meta,
            self.a,
            self.a_in,
            self.b,
            self.b_in,
        )
        self.a_in, self.b_in = swap(a_out, "dp", 1), swap(b_out, "seq", 2)

    def merge(self):
        part = shape((2, self.height // 8, self.width))
        out, self.keep = self.chain(
            small_run_of(merge_kernel, [part] * 2, self.name + "_second"),
            self.meta,
            self.a,
            self.a_in,
            self.b,
            self.b_in,
        )
        self.bit = 2
        self.arrived = swap(out, "dp", 2)

    def step(self):
        self.keep = self.chain(add, self.keep, self.arrived, self.name + "_d%d" % self.bit)
        self.bit *= 2
        more = self.bit < lax.axis_size("dp")
        self.arrived = swap(self.keep, "dp", self.bit if more else 2)
        return more

    def join(self):
        whole = shape((2, self.height // 4, self.width))
        self.keep = self.chain(
            small_run_of(join_kernel, whole, self.name + "_join"),
            self.meta,
            self.keep,
            self.arrived,
        )
        self.arrived = swap(self.keep, "dp", 1)

    def end(self, plan):
        width = self.width
        outs = [
            shape((pieces[0][1], width * len(pieces)), F32) for pieces in plan
        ]

        def call(deps, *args):
            return run(
                functools.partial(end_kernel, plan),
                deps,
                args,
                outs,
                [spec_smem()] + [spec_vmem()] * 2,
                [spec_vmem()] * len(outs),
                scratch=[pltpu.VMEM((self.height, width), BF)],
                mib=24,
                name=self.name + "_end",
            )

        return self.chain(call, self.meta, self.keep, self.arrived)


def small_run_of(body, outs, name):
    return lambda deps, *args: small_run(body, deps, args, outs, name)


class Chain:
    def __init__(self):
        self.last = ()

    def __call__(self, made, *args, pick=-1):
        outs = made(self.last, *args)
        self.last = ((outs[pick] if isinstance(outs, (tuple, list)) else outs),)
        return outs


def shards(
    chars,
    window_mask,
    micro_batch,
    mol_grad,
    query_weight,
    query_bias,
    key_weight,
    value_weight,
    value_bias,
    output_weight,
    output_bias,
    first_gain,
    first_shift,
    inner_weight,
    inner_bias,
    outer_weight,
    outer_bias,
    second_gain,
    second_shift,
    conv_weight,
    conv_bias,
    third_gain,
    third_shift,
):
    rows, block, width = chars.shape
    count = rows * block
    place = lax.axis_index("seq").astype(jnp.int32)
    group = lax.axis_index("dp").astype(jnp.int32)
    meta = jnp.stack([place, group % 2, group // 2 % 2])
    size = lax.axis_size("seq")
    forward_pairs = [(i, i + 1) for i in range(size - 1)]
    backward_pairs = [(i + 1, i) for i in range(size - 1)]
    low = lax.ppermute(chars[:, block - WIN :], "seq", forward_pairs)
    high = lax.ppermute(chars[:, :WIN], "seq", backward_pairs)
    vectors = (
        query_bias,
        value_bias,
        output_bias,
        first_gain,
        first_shift,
        outer_bias,
        second_gain,
        second_shift,
        conv_bias,
        third_gain,
        third_shift,
        inner_bias,
    )
    tokens = chars.reshape(count, width)
    chain = Chain()
    q, k, v, vecs = chain(project, tokens, vectors, query_weight, key_weight, value_weight)
    kv, probs, mixed, n1, inv1, low1, slope, hidden, mol, go, sums3, send_c, keep_c = chain(
        forward,
        meta,
        window_mask,
        micro_batch,
        vecs,
        tokens,
        low,
        high,
        q,
        k,
        v,
        key_weight,
        value_weight,
        output_weight,
        inner_weight,
        outer_weight,
        conv_weight,
        mol_grad.reshape(-1, width),
        pick=10,
    )
    molecules = mol.reshape(mol_grad.shape)
    conv = Sum(chain, meta, "conv", send_c, keep_c)
    outer = Sum(chain, meta, "outer", *chain(outer_grad, meta, go, hidden))
    conv.split()
    send_i, keep_i, isum, gb, gm, sums1 = chain(
        inner_back,
        meta,
        vecs,
        go,
        slope,
        outer_weight,
        inner_weight,
        low1,
        n1,
        inv1,
        output_weight,
        mixed,
    )
    inner = Sum(chain, meta, "inner", send_i, keep_i)
    outer.split()
    conv.cross()
    grads = ()
    for r in range(rows):
        grads = chain(attention_back, q, kv, probs, gm, rows, r, tuple(grads))
        if r == 0:
            conv.merge()
            outer.cross()
            inner.split()
    dq, dk, dv, sums_a = grads
    conv.step()
    outer.merge()
    inner.cross()
    send_p, keep_p, grad_low, grad_high = chain(
        project_grad,
        meta,
        dq,
        chars,
        dk,
        low,
        high,
        dv,
        key_weight,
        value_weight,
        sums_a,
        sums1,
        sums3,
        isum,
    )
    proj = Sum(chain, meta, "proj", send_p, keep_p)
    from_prev = lax.ppermute(grad_high, "seq", forward_pairs)
    from_next = lax.ppermute(grad_low, "seq", backward_pairs)
    while conv.step():
        pass
    outer.step()
    inner.merge()
    grad_chars = chain(
        chars_grad, gb, dq, dk, dv, from_prev, from_next, query_weight, key_weight, value_weight
    )
    proj.split()
    conv.join()
    while outer.step():
        pass
    inner.step()
    proj.cross()
    outer.join()
    while inner.step():
        pass
    quarter = width // 4
    wide = [[(j, quarter) for j in range(4)]]
    (full_c,) = conv.end(wide)
    proj.merge()
    inner.join()
    (full_u,) = outer.end(wide)
    proj.step()
    full_i, full_o = inner.end([[(0, width)], [(0, quarter)]])
    while proj.step():
        pass
    proj.join()
    full_q, full_k, full_v, small = proj.end([[(0, quarter)]] * 3 + [[(0, 16)]])
    quarter = width // 4
    vec_of = lambda i: small[i, :quarter]
    return (
        molecules,
        grad_chars,
        full_q.T,
        vec_of(0),
        full_k.T,
        full_v.T,
        vec_of(1),
        full_o.T,
        vec_of(2),
        vec_of(3),
        vec_of(4),
        full_i,
        small[11:15, :quarter].reshape(-1),
        full_u.T,
        vec_of(5),
        vec_of(6),
        vec_of(7),
        full_c.T,
        vec_of(8),
        vec_of(9),
        vec_of(10),
    )


def solution(mesh):
    split = P("dp", "seq", None)
    placed = (split, P("dp", None), P("dp"), split) + (P(),) * 19
    by_column, by_place = P(None, "seq"), P("seq")
    outs = (
        split,
        split,
        by_column,
        by_place,
        by_column,
        by_column,
        by_place,
        by_column,
        by_place,
        by_place,
        by_place,
        by_column,
        by_place,
        by_column,
        by_place,
        by_place,
        by_place,
        by_column,
        by_place,
        by_place,
        by_place,
    )
    return jax.shard_map(shards, mesh=mesh, in_specs=placed, out_specs=outs, check_vma=False)
```

```python
import functools

import jax
import jax.numpy as jnp
from jax import lax
from jax.experimental import pallas as pl
from jax.experimental.pallas import tpu as pltpu
from jax.sharding import PartitionSpec as P

HEADS = 12
HEAD_DIM = 64
WIN = 128
DOWN = 4
MICRO = 2
EPSILON = 1e-06
NEG_FILL = -1e30
GELU_A = 0.7978845608028654
GELU_B = 0.044715
BF = jnp.bfloat16
F32 = jnp.float32
LANES = 128
MIB = 1 << 20

NN = (((1,), (0,)), ((), ()))
NT = (((1,), (1,)), ((), ()))
TN = (((0,), (0,)), ((), ()))

(V_QB, V_VB, V_OB, V_G1, V_S1, V_OUTB, V_G2, V_S2, V_CB, V_G3, V_S3, V_IB) = range(12)


def dot(left, right, dims=NN):
    return lax.dot_general(left, right, dims, preferred_element_type=F32)


def gelu_both(u):
    square = u * u
    t = jnp.tanh(u * (GELU_A + (GELU_A * GELU_B) * square))
    half = 0.5 + 0.5 * t
    value = u * half
    slope = half + value * (1.0 - t) * (GELU_A + (3.0 * GELU_A * GELU_B) * square)
    return value, slope


def layer_stats(u):
    center = u - jnp.mean(u, axis=-1, keepdims=True)
    inv_dev = lax.rsqrt(jnp.mean(center * center, axis=-1, keepdims=True) + EPSILON)
    return center * inv_dev, inv_dev


def norm_back(grad_out, normal, inv_dev, gain_vec):
    scaled = grad_out * gain_vec
    return inv_dev * (
        scaled
        - jnp.mean(scaled, axis=-1, keepdims=True)
        - normal * jnp.mean(scaled * normal, axis=-1, keepdims=True)
    )


def col_sum(value):
    return jnp.sum(value, axis=0, keepdims=True)


def params(mib=56, **more):
    return pltpu.CompilerParams(vmem_limit_bytes=mib * MIB, **more)


def cost(flops, nbytes):
    return pl.CostEstimate(flops=int(flops), bytes_accessed=int(nbytes), transcendentals=0)


def spec_any():
    return pl.BlockSpec(memory_space=pl.ANY)


def spec_hbm():
    return pl.BlockSpec(memory_space=pltpu.HBM)


def spec_smem():
    return pl.BlockSpec(memory_space=pltpu.SMEM)


def spec_vmem():
    return pl.BlockSpec(memory_space=pltpu.VMEM)


def shape(dims, dtype=BF):
    return jax.ShapeDtypeStruct(tuple(dims), dtype)


def run(body, deps, args, out_shape, in_specs, out_specs, scratch=(), grid=(), prefetch=0, mib=56, flops=10**12, nbytes=10**6, name=None, aliases=None):
    given = len(args)

    def wrapped(*refs):
        body(*refs[:given], *refs[given + len(deps) :])

    return pl.pallas_call(
        wrapped,
        grid_spec=pltpu.PrefetchScalarGridSpec(
            num_scalar_prefetch=prefetch,
            grid=grid,
            in_specs=list(in_specs) + [spec_any()] * len(deps),
            out_specs=out_specs,
            scratch_shapes=list(scratch),
        ),
        out_shape=out_shape,
        compiler_params=pltpu.CompilerParams(vmem_limit_bytes=mib * MIB),
        cost_estimate=cost(flops, nbytes),
        input_output_aliases=aliases or {},
        name=name,
    )(*args, *deps)


def head_masks():
    lane = lax.broadcasted_iota(jnp.int32, (1, LANES), 1)
    first = jnp.where(lane < HEAD_DIM, 1.0, 0.0).astype(BF)
    return first, (1.0 - first.astype(F32)).astype(BF)


def twice(block, masks):
    return jnp.concatenate([block * masks[0], block * masks[1]], axis=0)


def slot_of(quarter, place):
    same_x = (quarter // 2 == place // 2).astype(jnp.int32)
    same_core = (quarter % 2 == place % 2).astype(jnp.int32)
    return 2 * same_core + same_x


def project_kernel(names, x_ref, *refs):
    vectors, (wq_ref, wk_ref, wv_ref, q_ref, k_ref, v_ref, vec_ref) = refs[:names], refs[names:]
    width = x_ref.shape[1]
    part = wq_ref.shape[1]
    step = pl.program_id(0)

    @pl.when(step == 0)
    def _():
        row = 0
        for ref in vectors:
            value = ref[...].astype(F32)
            for k in range(value.shape[0] // width):
                vec_ref[row : row + 1, :] = value[k * width : (k + 1) * width].reshape(1, width)
                row += 1
        vec_ref[row:, :] = jnp.zeros((vec_ref.shape[0] - row, width), F32)

    x = x_ref[...]
    at = pl.ds(pl.multiple_of(step * part, part), part)
    queries = (dot(x, wq_ref[...]) + vec_ref[V_QB : V_QB + 1, at]).astype(BF)
    q_ref[...] = queries * jnp.asarray(HEAD_DIM**-0.5, BF)
    k_ref[...] = dot(x, wk_ref[...]).astype(BF)
    v_ref[...] = (dot(x, wv_ref[...]) + vec_ref[V_VB : V_VB + 1, at]).astype(BF)


def project(deps, tokens, vectors, wq, wk, wv):
    count, width = tokens.shape
    part = 256
    column = pl.BlockSpec((width, part), lambda i: (0, i))
    out = pl.BlockSpec((count, part), lambda i: (0, i))
    height = rounded_up(sum(v.shape[0] for v in vectors) // width, 8)
    return run(
        functools.partial(project_kernel, len(vectors)),
        deps,
        (tokens, *vectors, wq, wk, wv),
        [shape((count, width))] * 3 + [shape((height, width), F32)],
        [pl.BlockSpec((count, width), lambda i: (0, 0))]
        + [pl.BlockSpec(v.shape, lambda i: (0,)) for v in vectors]
        + [column] * 3,
        [out] * 3 + [pl.BlockSpec((height, width), lambda i: (0, 0))],
        grid=(width // part,),
        mib=60,
        name="project",
    )


def forward_kernel(
    rows,
    wins,
    windows_all,
    meta,
    wmask,
    mbatch,
    vec,
    chars_h,
    low_h,
    high_h,
    q_h,
    k_h,
    v_h,
    wk_h,
    wv_h,
    wo_h,
    wi_h,
    wout_h,
    wc_h,
    mg_h,
    kv_o,
    pt_o,
    mixed_o,
    n1_o,
    inv1_o,
    low1_o,
    slope_o,
    hidden_o,
    mol_o,
    go_o,
    sums_o,
    send_o,
    keep_o,
    q,
    kv,
    halo,
    wkv,
    wo,
    chars,
    wi,
    wout,
    wc,
    mg,
    probs,
    mixed,
    acc,
    strips,
    low1,
    n1,
    inv1,
    slope,
    hidden,
    n2,
    inv2,
    merged,
    mol,
    sem_in,
    sem_p,
    sem_h,
    sem_out,
):
    place = meta[0]
    block = wins * WIN
    width = chars.shape[-1]
    count = rows * block
    pairs = width // LANES
    parts = wi.shape[1] // width

    def copy_in(index, src, dst):
        made = pltpu.make_async_copy(src, dst, sem_in.at[index])
        made.start()
        return made

    halo_in = [
        copy_in(0, low_h, halo.at[0]),
        copy_in(1, high_h, halo.at[1]),
        copy_in(2, wk_h, wkv.at[0]),
        copy_in(3, wv_h, wkv.at[1]),
    ]
    qkv_in = [copy_in(4, q_h, q)]
    for r in range(rows):
        qkv_in.append(
            copy_in(5 + 2 * r, k_h.at[pl.ds(r * block, block)], kv.at[r, pl.ds(WIN, block)])
        )
        qkv_in.append(
            copy_in(
                6 + 2 * r, v_h.at[pl.ds(r * block, block)], kv.at[rows + r, pl.ds(WIN, block)]
            )
        )
    base = 5 + 2 * rows

    def copy_out(index, src, dst):
        made = pltpu.make_async_copy(src, dst, sem_out.at[index])
        made.start()
        return made

    for made in halo_in:
        made.wait()
    beside = halo[...].reshape(2 * rows * WIN, width)
    keys = dot(beside, wkv[0]).astype(BF)
    values = (dot(beside, wkv[1]) + vec[V_VB : V_VB + 1, :]).astype(BF)
    for side in range(2):
        start = side * (block + WIN)
        for r in range(rows):
            at = (side * rows + r) * WIN
            kv[r, pl.ds(start, WIN), :] = keys[at : at + WIN]
            kv[rows + r, pl.ds(start, WIN), :] = values[at : at + WIN]
    for made in qkv_in:
        made.wait()
    wo_in = copy_in(base, wo_h, wo)
    chars_in = copy_in(base + 1, chars_h, chars)
    wi_in = copy_in(base + 2, wi_h, wi)
    wout_in = copy_in(base + 3, wout_h, wout)
    kv_out = copy_out(0, kv, kv_o)

    masks = head_masks()

    def pair_step(it, carry):
        r = it // pairs
        pair = it % pairs
        slot = it % 2
        lanes = pl.ds(pl.multiple_of(pair * LANES, LANES), LANES)

        @pl.when(it >= 2)
        def _():
            pltpu.make_async_copy(probs.at[slot], pt_o.at[it - 2], sem_p.at[slot]).wait()

        every = []
        for w in range(wins):
            queries = twice(q[pl.ds(r * block + w * WIN, WIN), lanes], masks)
            every.append(dot(kv[r, pl.ds(w * WIN, 3 * WIN), lanes], queries, NT))
        chances = []
        for w, scores in enumerate(every):
            at = place * wins + w
            low_ok = (at >= 1) & (wmask[r, jnp.maximum(at - 1, 0)] > 0)
            high_ok = (at + 1 < windows_all) & (wmask[r, jnp.minimum(at + 1, windows_all - 1)] > 0)
            scores = jnp.concatenate(
                [
                    scores[0:WIN] + jnp.where(low_ok, 0.0, NEG_FILL),
                    scores[WIN : 2 * WIN],
                    scores[2 * WIN :] + jnp.where(high_ok, 0.0, NEG_FILL),
                ],
                axis=0,
            )
            shifted = jnp.exp(scores - jnp.max(scores, axis=0, keepdims=True))
            total = jnp.sum(shifted, axis=0, keepdims=True)
            chances.append((shifted * (1.0 / total)).astype(BF))
            probs[slot, w] = chances[w]
        for w, chance in enumerate(chances):
            stacked = jnp.concatenate([chance[:, :LANES], chance[:, LANES:]], axis=0)
            values_win = twice(kv[rows + r, pl.ds(w * WIN, 3 * WIN), lanes], masks)
            mixed[pl.ds(r * block + w * WIN, WIN), lanes] = dot(stacked, values_win, TN).astype(BF)
        pltpu.make_async_copy(probs.at[slot], pt_o.at[it], sem_p.at[slot]).start()
        return carry

    steps = rows * pairs
    lax.fori_loop(0, steps, pair_step, 0)
    mixed_out = copy_out(1, mixed, mixed_o)

    wo_in.wait()
    chars_in.wait()
    wc_in = copy_in(base + 4, wc_h, wc)
    mg_in = copy_in(base + 5, mg_h, mg)
    piece = 256

    def first_step(i, carry):
        at = pl.ds(pl.multiple_of(i * piece, piece), piece)
        u = dot(mixed[at, :], wo[...]) + vec[V_OB : V_OB + 1, :] + chars[at, :].astype(F32)
        normal, inv = layer_stats(u)
        first = normal * vec[V_G1 : V_G1 + 1, :] + vec[V_S1 : V_S1 + 1, :]
        n1[at, :] = normal.astype(BF)
        inv1[at, :] = inv
        low1[at, :] = first.astype(BF)
        acc[at, :] = first + vec[V_OUTB : V_OUTB + 1, :]
        return carry

    lax.fori_loop(0, count // piece, first_step, 0, unroll=True)
    outs = [mixed_out, copy_out(2, n1, n1_o), copy_out(3, inv1, inv1_o), copy_out(4, low1, low1_o)]

    wi_in.wait()
    wout_in.wait()

    def ffn_step(c, carry):
        slot = c % 2
        columns = pl.ds(pl.multiple_of(c * width, width), width)

        @pl.when(c >= 2)
        def _():
            pltpu.make_async_copy(slope.at[slot], slope_o.at[c - 2], sem_h.at[slot]).wait()
            pltpu.make_async_copy(hidden.at[slot], hidden_o.at[c - 2], sem_h.at[2 + slot]).wait()

        bias = vec[pl.ds(V_IB + c, 1), :]
        half = count // 2
        parts_of = [pl.ds(k * half, half) for k in range(2)]
        upper, lower = (dot(low1[at, :], wi[:, columns]) + bias for at in parts_of)
        for at, u in zip(parts_of, (upper, lower), strict=True):
            value, steep = gelu_both(u)
            slope[slot, at, :] = steep.astype(BF)
            h = value.astype(BF)
            hidden[slot, at, :] = h
            acc[at, :] += dot(h, wout[columns, :])
        pltpu.make_async_copy(slope.at[slot], slope_o.at[c], sem_h.at[slot]).start()
        pltpu.make_async_copy(hidden.at[slot], hidden_o.at[c], sem_h.at[2 + slot]).start()
        return carry

    lax.fori_loop(0, parts, ffn_step, 0)

    def second_step(i, carry):
        at = pl.ds(pl.multiple_of(i * piece, piece), piece)
        normal, inv = layer_stats(acc[at, :])
        n2[at, :] = normal.astype(BF)
        inv2[at, :] = inv
        second = normal * vec[V_G2 : V_G2 + 1, :] + vec[V_S2 : V_S2 + 1, :]
        for t in range(pairs):
            strips[t, at, :] = second[:, t * LANES : (t + 1) * LANES]
        return carry

    lax.fori_loop(0, count // piece, second_step, 0, unroll=True)

    wc_in.wait()
    mg_in.wait()
    mols = count // DOWN
    conv = jnp.zeros((mols, width), F32) + vec[V_CB : V_CB + 1, :]
    for i in range(DOWN):
        for t in range(pairs):
            merged[i, :, t * LANES : (t + 1) * LANES] = strips[
                t, pl.ds(i, mols, stride=DOWN), :
            ].astype(BF)
        part = merged[i]
        conv = conv + dot(part, wc[pl.ds(i * width, width), :])
    value, steep = gelu_both(conv)
    normal, inv = layer_stats(value)
    per_win = WIN // DOWN
    which = lax.broadcasted_iota(jnp.int32, (mols, 1), 0) // per_win
    live = jnp.zeros((mols, 1), F32)
    total = jnp.ones((mols, 1), F32)
    lengths = []
    for r in range(rows):
        length = wmask[r, 0]
        for w in range(1, windows_all):
            length = length + wmask[r, w]
        lengths.append(length)
    for r in range(rows):
        same = jnp.int32(0)
        for other in range(rows):
            same = same + jnp.where(mbatch[other] == mbatch[r], lengths[other], 0)
        same = (same * per_win).astype(F32)
        for w in range(wins):
            here = which == r * wins + w
            live = jnp.where(here, wmask[r, place * wins + w].astype(F32), live)
            total = jnp.where(here, same, total)
    weight = (rows // MICRO * windows_all * per_win) / total
    gain = vec[V_G3 : V_G3 + 1, :]
    mol[...] = ((normal * gain + vec[V_S3 : V_S3 + 1, :]) * live).astype(BF)
    outs.append(copy_out(5, mol, mol_o))
    grad_mol = mg[...].astype(F32) * (weight * live)
    grad_conv = (steep * norm_back(grad_mol, normal, inv, gain)).astype(BF)
    sums_o[0:1, :] = col_sum(grad_mol * normal)
    sums_o[1:2, :] = col_sum(grad_mol)
    sums_o[2:3, :] = col_sum(grad_conv.astype(F32))
    sums_o[3:, :] = jnp.zeros((sums_o.shape[0] - 3, width), F32)

    kv_out.wait()
    across = grad_conv.T
    quarter = width // 4
    for i in range(DOWN):
        made = dot(across, merged[i]).astype(BF)
        for number in range(4):
            kv[slot_of(jnp.int32(number), place), pl.ds(i * quarter, quarter), :] = made[
                number * quarter : (number + 1) * quarter
            ]
    outs.append(copy_out(6, kv.at[pl.ds(0, 2)], send_o))
    outs.append(copy_out(7, kv.at[pl.ds(2, 2)], keep_o))

    for i in range(DOWN):
        made = dot(grad_conv, wc[pl.ds(i * width, width), :], NT)
        for t in range(pairs):
            strips[t, pl.ds(i, mols, stride=DOWN), :] = made[:, t * LANES : (t + 1) * LANES]
    gain = vec[V_G2 : V_G2 + 1, :]

    def back_step(i, carry):
        at = pl.ds(pl.multiple_of(i * piece, piece), piece)
        grad = jnp.concatenate([strips[t, at, :] for t in range(pairs)], axis=1)
        normal = n2[at, :].astype(F32)
        made = norm_back(grad, normal, inv2[at, :], gain).astype(BF)
        n2[at, :] = made
        sums_o[3:4, :] += col_sum(grad * normal)
        sums_o[4:5, :] += col_sum(grad)
        sums_o[5:6, :] += col_sum(made.astype(F32))
        return carry

    lax.fori_loop(0, count // piece, back_step, 0, unroll=True)
    outs.append(copy_out(8, n2, go_o))

    for made in outs:
        made.wait()
    for it in range(max(0, steps - 2), steps):
        pltpu.make_async_copy(probs.at[it % 2], pt_o.at[it], sem_p.at[it % 2]).wait()
    for c in range(max(0, parts - 2), parts):
        pltpu.make_async_copy(slope.at[c % 2], slope_o.at[c], sem_h.at[c % 2]).wait()
        pltpu.make_async_copy(hidden.at[c % 2], hidden_o.at[c], sem_h.at[2 + c % 2]).wait()


def forward(deps, meta, wmask, mbatch, vecs, chars, low, high, q, k, v, wk, wv, wo, wi, wout, wc, mg):
    rows = wmask.shape[0]
    windows_all = wmask.shape[1]
    count, width = q.shape
    block = count // rows
    wins = block // WIN
    ff = wi.shape[1]
    parts = ff // width
    mols = count // DOWN
    pairs = width // LANES
    ext = block + 2 * WIN
    outs = [
        shape((2 * rows, ext, width)),
        shape((rows * pairs, wins, 3 * WIN, 2 * LANES)),
        shape((count, width)),
        shape((count, width)),
        shape((count, 1), F32),
        shape((count, width)),
        shape((parts, count, width)),
        shape((parts, count, width)),
        shape((mols, width)),
        shape((count, width)),
        shape((8, width), F32),
        shape((2, DOWN * width // 4, width)),
        shape((2, DOWN * width // 4, width)),
    ]
    out_specs = [spec_any()] * len(outs)
    out_specs[10] = spec_vmem()
    return run(
        functools.partial(forward_kernel, rows, wins, windows_all),
        deps,
        (meta, wmask, mbatch, vecs, chars, low, high, q, k, v, wk, wv, wo, wi, wout, wc, mg),
        outs,
        [spec_smem()] * 3 + [spec_vmem()] + [spec_any()] * 13,
        out_specs,
        scratch=[
            pltpu.VMEM((count, width), BF),
            pltpu.VMEM((2 * rows, ext, width), BF),
            pltpu.VMEM((2, rows, WIN, width), BF),
            pltpu.VMEM((2, width, width), BF),
            pltpu.VMEM((width, width), BF),
            pltpu.VMEM((count, width), BF),
            pltpu.VMEM((width, ff), BF),
            pltpu.VMEM((ff, width), BF),
            pltpu.VMEM((DOWN * width, width), BF),
            pltpu.VMEM((mols, width), BF),
            pltpu.VMEM((2, wins, 3 * WIN, 2 * LANES), BF),
            pltpu.VMEM((count, width), BF),
            pltpu.VMEM((count, width), F32),
            pltpu.VMEM((pairs, count, LANES), F32),
            pltpu.VMEM((count, width), BF),
            pltpu.VMEM((count, width), BF),
            pltpu.VMEM((count, 1), F32),
            pltpu.VMEM((2, count, width), BF),
            pltpu.VMEM((2, count, width), BF),
            pltpu.VMEM((count, width), BF),
            pltpu.VMEM((count, 1), F32),
            pltpu.VMEM((DOWN, mols, width), BF),
            pltpu.VMEM((mols, width), BF),
            pltpu.SemaphoreType.DMA((11 + 2 * rows,)),
            pltpu.SemaphoreType.DMA((2,)),
            pltpu.SemaphoreType.DMA((4,)),
            pltpu.SemaphoreType.DMA((9,)),
        ],
        mib=60,
        name="forward",
    )


def outer_grad_kernel(meta, go, hidden, send, keep, across):
    place = meta[0]
    width = go.shape[1]
    quarter = width // 4

    @pl.when(pl.program_id(0) == 0)
    def _():
        turned = go[...].T
        for number in range(4):
            across[slot_of(jnp.int32(number), place)] = turned[
                number * quarter : (number + 1) * quarter
            ]

    left = across[...].reshape(width, go.shape[0])
    made = dot(left, hidden[0]).astype(BF)
    for j in range(2):
        send[j] = made[j * quarter : (j + 1) * quarter]
        keep[j] = made[(2 + j) * quarter : (3 + j) * quarter]


def outer_grad(deps, meta, go, hidden):
    parts, count, width = hidden.shape
    quarter = width // 4
    out = pl.BlockSpec((2, quarter, width), lambda i, m: (0, i, 0))
    return run(
        outer_grad_kernel,
        deps,
        (meta, go, hidden),
        [shape((2, parts * quarter, width))] * 2,
        [
            pl.BlockSpec((count, width), lambda i, m: (0, 0)),
            pl.BlockSpec((1, count, width), lambda i, m: (i, 0, 0)),
        ],
        [out] * 2,
        scratch=[pltpu.VMEM((4, quarter, count), BF)],
        grid=(parts,),
        prefetch=1,
        name="outer_grad",
    )


def slot_copies(src, send, keep, slot, at, sem):
    out = pltpu.make_async_copy(src, send.at[jnp.minimum(slot, 1), at], sem)
    own = pltpu.make_async_copy(src, keep.at[jnp.maximum(slot - 2, 0), at], sem)

    def start():
        @pl.when(slot < 2)
        def _():
            out.start()

        @pl.when(slot >= 2)
        def _():
            own.start()

    return start, out.wait


def inner_back_kernel(first, chosen, meta, vec, go_h, slope_h, wout_h, wi_h, low1_h, *refs):
    if first:
        ins, refs = (), refs
    else:
        ins, refs = refs[:5], refs[7:]
    send, keep, isum, *refs = refs
    if first:
        acc_o, *refs = refs
    else:
        gb_o, gm_o, sums, *refs = refs
    go, slope, wout, wi, low1, acc, grads, *refs = refs
    if not first:
        n1, inv1, wo, mixed, gb, gm, rest, *refs = refs
    sem_in, sem_out = refs
    count, width = go.shape
    place = meta[0]
    quarter = width // 4
    waits = []

    def bring(src, dst):
        made = pltpu.make_async_copy(src, dst, sem_in.at[len(waits)])
        made.start()
        waits.append(made)
        return made

    go_in = bring(go_h, go)
    parts_in = []
    for k, c in enumerate(chosen):
        at = pl.ds(c * width, width)
        parts_in.append(
            [
                bring(wout_h.at[at], wout.at[k]),
                bring(slope_h.at[c], slope.at[k]),
                bring(wi_h.at[:, at], wi.at[k]),
            ]
        )
        if k == 0:
            low1_in = bring(low1_h, low1)
            acc_in = None if first else bring(ins[0], acc)
    if not first:
        late = [bring(src, dst) for src, dst in zip(ins[1:], (n1, inv1, wo, mixed), strict=True)]
    go_in.wait()
    half = count // 2
    halves = [slice(k * half, (k + 1) * half) for k in range(2)]
    outs = []
    across = None
    for k, c in enumerate(chosen):
        parts_in[k][0].wait()
        steep = [dot(go[at, :], wout[k], NT) for at in halves]
        if across is None:
            low1_in.wait()
            across = low1[...].T
        parts_in[k][1].wait()
        parts_in[k][2].wait()
        if k == 0 and not first:
            acc_in.wait()
        low = []
        for at, grad in zip(halves, steep, strict=True):
            low.append((slope[k, at, :].astype(F32) * grad).astype(BF))
            added = dot(low[-1], wi[k], NT)
            if first and k == 0:
                acc[at, :] = go[at, :].astype(F32) + added
            else:
                acc[at, :] += added
        made = jnp.concatenate(low, axis=0)
        isum[k] = jnp.broadcast_to(col_sum(made.astype(F32)), (8, width))
        grads[k] = dot(across, made).astype(BF)
        slot = slot_of(jnp.int32(c), place)
        start, wait = slot_copies(
            grads.at[k], send, keep, slot, pl.ds(0, width), sem_out.at[len(outs)]
        )
        start()
        outs.append(wait)

    def leave(src, dst):
        made = pltpu.make_async_copy(src, dst, sem_out.at[len(outs)])
        made.start()
        outs.append(made.wait)

    if first:
        leave(acc, acc_o)
    else:
        for made in late:
            made.wait()
        gain = vec[V_G1 : V_G1 + 1, :]
        piece = 256
        sums[...] = jnp.zeros(sums.shape, F32)
        lows = []
        for j in range(count // piece):
            at = slice(j * piece, (j + 1) * piece)
            grad = acc[at, :]
            normal = n1[at, :].astype(F32)
            lows.append(norm_back(grad, normal, inv1[at, :], gain).astype(BF))
            gb[at, :] = lows[-1]
            sums[0:1, :] += col_sum(grad * normal)
            sums[1:2, :] += col_sum(grad)
            sums[2:3, :] += col_sum(lows[-1].astype(F32))
        leave(gb, gb_o)
        for j in range(count // piece):
            gm[j * piece : (j + 1) * piece, :] = dot(lows[j], wo[...], NT).astype(BF)
        leave(gm, gm_o)
        rest[...] = jnp.zeros(rest.shape, BF)
        extra = rest.shape[1] - quarter
        made = dot(gb[...], mixed[...], TN).astype(BF)
        for number in range(4):
            rest[number, 0:quarter, :] = made[number * quarter : (number + 1) * quarter]
            slot = slot_of(jnp.int32(number), place)
            start, wait = slot_copies(
                rest.at[number],
                send,
                keep,
                slot,
                pl.ds(width, quarter + extra),
                sem_out.at[len(outs)],
            )
            start()
            outs.append(wait)
    for wait in outs:
        wait()


def rounded_up(value, unit):
    return -(-value // unit) * unit


def inner_back(deps, chosen, meta, vecs, go, slope, wout, wi, low1, *more):
    _, count, width = slope.shape
    first = not more
    quarter = width // 4
    height = rounded_up(width + quarter, 8 * 16)
    both = shape((2, height, width))
    outs = [both, both, shape((2, 8, width), F32)]
    out_specs = [spec_hbm(), spec_hbm(), spec_vmem()]
    scratch = [
        pltpu.VMEM((count, width), BF),
        pltpu.VMEM((2, count, width), BF),
        pltpu.VMEM((2, width, width), BF),
        pltpu.VMEM((2, width, width), BF),
        pltpu.VMEM((count, width), BF),
        pltpu.VMEM((count, width), F32),
        pltpu.VMEM((2, width, width), BF),
    ]
    if first:
        outs += [shape((count, width), F32)]
        out_specs += [spec_hbm()]
    else:
        outs += [shape((count, width)), shape((count, width)), shape((8, width), F32)]
        out_specs += [spec_hbm(), spec_hbm(), spec_vmem()]
        scratch += [
            pltpu.VMEM((count, width), BF),
            pltpu.VMEM((count, 1), F32),
            pltpu.VMEM((width, width), BF),
            pltpu.VMEM((count, width), BF),
            pltpu.VMEM((count, width), BF),
            pltpu.VMEM((count, width), BF),
            pltpu.VMEM((4, height - width, width), BF),
        ]
    scratch += [pltpu.SemaphoreType.DMA((13,)), pltpu.SemaphoreType.DMA((8,))]
    return run(
        functools.partial(inner_back_kernel, first, chosen),
        deps,
        (meta, vecs, go, slope, wout, wi, low1, *more),
        outs,
        [spec_smem(), spec_vmem()] + [spec_any()] * (5 + len(more)),
        out_specs,
        scratch=scratch,
        aliases={} if first else {12: 0, 13: 1},
        name="inner_back%d" % chosen[0],
    )


def attention_back_kernel(wins, q, k, v, probs, gm, dq, dk, dv, sums):
    masks = head_masks()
    here = [slice(w * WIN, (w + 1) * WIN) for w in range(wins)]
    span = [slice(w * WIN, (w + 3) * WIN) for w in range(wins)]
    grad_out = [twice(gm[0, at, :], masks) for at in here]
    queries = [twice(q[0, at, :], masks) for at in here]
    grad_probs = [dot(v[0, span[w], :], grad_out[w], NT) for w in range(wins)]
    grad_values = [dot(probs[0, w], grad_out[w]) for w in range(wins)]
    grad_scores = []
    for w in range(wins):
        chance = probs[0, w].astype(F32)
        product = chance * grad_probs[w]
        total = jnp.sum(product, axis=0, keepdims=True)
        grad_scores.append((product - chance * total).astype(BF))
    grad_keys = [dot(grad_scores[w], queries[w]) for w in range(wins)]
    q_sum = jnp.zeros((1, LANES), F32)
    for w in range(wins):
        made = grad_scores[w]
        stacked = jnp.concatenate([made[:, :LANES], made[:, LANES:]], axis=0)
        made = dot(stacked, twice(k[0, span[w], :], masks), TN) * HEAD_DIM**-0.5
        low = made.astype(BF)
        dq[0, here[w], :] = low
        q_sum = q_sum + col_sum(low.astype(F32))
    v_sum = jnp.zeros((1, LANES), F32)
    for parts, out in ((grad_keys, dk), (grad_values, dv)):
        for b in range(wins + 2):
            uses = [w for w in range(wins) if 0 <= b - w < 3]
            pieces = [parts[w][(b - w) * WIN : (b - w + 1) * WIN] for w in uses]
            made = sum(pieces[1:], pieces[0])
            out[0, b * WIN : (b + 1) * WIN, :] = made.astype(BF)
            if out is dv:
                v_sum = v_sum + col_sum(made)
    sums[0, 0:1, :] = q_sum
    sums[0, 1:2, :] = v_sum
    sums[0, 2:, :] = jnp.zeros((6, LANES), F32)


def attention_back(deps, q, kv, probs, gm, rows, row, before):
    count, width = q.shape
    block = count // rows
    wins = block // WIN
    ext = kv.shape[1]
    pairs = width // LANES
    own = pl.BlockSpec((1, block, LANES), lambda p: (row, 0, p))
    keys = pl.BlockSpec((1, ext, LANES), lambda p: (row, 0, p))
    values = pl.BlockSpec((1, ext, LANES), lambda p: (rows + row, 0, p))

    def body(q, k, v, probs, gm, *refs):
        attention_back_kernel(wins, q, k, v, probs, gm, *refs[len(before) :])

    return run(
        body,
        deps,
        (q.reshape(rows, block, width), kv, kv, probs, gm.reshape(rows, block, width), *before),
        [
            shape((rows, block, width)),
            shape((rows, ext, width)),
            shape((rows, ext, width)),
            shape((rows, 8, width), F32),
        ],
        [
            own,
            keys,
            values,
            pl.BlockSpec((1, wins, 3 * WIN, 2 * LANES), lambda p: (row * pairs + p, 0, 0, 0)),
            own,
        ]
        + [spec_any()] * len(before),
        [own, keys, keys, pl.BlockSpec((1, 8, LANES), lambda p: (row, 0, p))],
        grid=(pairs,),
        mib=56,
        aliases={5 + k: k for k in range(len(before))},
        name="attention_back%d" % row,
    )


VEC_ROWS = 64


def project_grad_kernel(
    meta,
    dq_h,
    chars_h,
    dk_h,
    low_h,
    high_h,
    dv_h,
    wk_h,
    wv_h,
    sums_a,
    sums1,
    sums3,
    isum_a,
    isum_b,
    send_o,
    keep_o,
    glow_o,
    ghigh_o,
    dq,
    dk,
    dv,
    ext,
    wk,
    wv,
    glow,
    ghigh,
    made_all,
    small,
    sem_in,
    sem_out,
):
    rows, full, width = dk.shape
    block = full - 2 * WIN
    count = rows * block
    place = meta[0]
    quarter = width // 4
    started = []
    pairs = [
        (dq_h, dq),
        (chars_h, ext.at[:, pl.ds(WIN, block)]),
        (dk_h, dk),
        (low_h, ext.at[:, pl.ds(0, WIN)]),
        (high_h, ext.at[:, pl.ds(WIN + block, WIN)]),
        (dv_h, dv),
        (wk_h, wk),
        (wv_h, wv),
    ]
    for k, (src, dst) in enumerate(pairs):
        started.append(pltpu.make_async_copy(src, dst, sem_in.at[k]))
        started[-1].start()
    leaving = []

    def leave(src, dst):
        leaving.append(pltpu.make_async_copy(src, dst, sem_out.at[len(leaving)]))
        leaving[-1].start()

    def put(index, made):
        at = pl.ds(index * quarter, quarter)
        for number in range(4):
            made_all[slot_of(jnp.int32(number), place), at, :] = made[
                number * quarter : (number + 1) * quarter
            ]
        leave(made_all.at[pl.ds(0, 2), at], send_o.at[:, at])
        leave(made_all.at[pl.ds(2, 2), at], keep_o.at[:, at])

    att = sums_a[0]
    for r in range(1, rows):
        att = att + sums_a[r]
    stack = [att[0:1], att[1:2], sums1[2:3], sums1[0:1], sums1[1:2], sums3[5:6]]
    stack += [sums3[3:4], sums3[4:5], sums3[2:3], sums3[0:1], sums3[1:2]]
    at = pl.ds(3 * quarter, VEC_ROWS)
    for number in range(4):
        mine = slice(number * quarter, (number + 1) * quarter)
        small[...] = jnp.zeros(small.shape, F32)
        for row, vector in enumerate(stack):
            small[row : row + 1, 0:quarter] = vector[:, mine]
        for j in range(4):
            small[len(stack) + j : len(stack) + j + 1, 0:quarter] = (isum_a, isum_b)[number // 2][
                number % 2, 0:1, j * quarter : (j + 1) * quarter
            ]
        made_all[slot_of(jnp.int32(number), place), at, :] = small[...].astype(BF)
    leave(made_all.at[pl.ds(0, 2), at], send_o.at[:, at])
    leave(made_all.at[pl.ds(2, 2), at], keep_o.at[:, at])

    started[0].wait()
    started[1].wait()
    own = ext[:, WIN : WIN + block, :].reshape(count, width)
    put(0, dot(dq[...].reshape(count, width), own, TN).astype(BF))
    started[2].wait()
    started[3].wait()
    started[4].wait()
    every = ext[...].reshape(rows * full, width)
    put(1, dot(dk[...].reshape(rows * full, width), every, TN).astype(BF))
    started[5].wait()
    put(2, dot(dv[...].reshape(rows * full, width), every, TN).astype(BF))
    started[6].wait()
    started[7].wait()
    for side, out, out_o in ((0, glow, glow_o), (full - WIN, ghigh, ghigh_o)):
        keys = jnp.concatenate([dk[r, side : side + WIN, :] for r in range(rows)], axis=0)
        values = jnp.concatenate([dv[r, side : side + WIN, :] for r in range(rows)], axis=0)
        made = (dot(keys, wk[...], NT) + dot(values, wv[...], NT)).astype(BF)
        for r in range(rows):
            out[r] = made[r * WIN : (r + 1) * WIN]
        leave(out, out_o)
    for made in leaving:
        made.wait()


def project_grad(deps, meta, dq, chars, dk, low, high, dv, wk, wv, *sums):
    rows, full, width = dk.shape
    count = dq.shape[0] * dq.shape[1]
    edge = (rows, WIN, width)
    height = 3 * width // 4 + VEC_ROWS
    return run(
        project_grad_kernel,
        deps,
        (meta, dq, chars, dk, low, high, dv, wk, wv, *sums),
        [shape((2, height, width))] * 2 + [shape(edge)] * 2,
        [spec_smem()] + [spec_any()] * 8 + [spec_vmem()] * len(sums),
        [spec_any()] * 4,
        scratch=[
            pltpu.VMEM(dq.shape, BF),
            pltpu.VMEM(dk.shape, BF),
            pltpu.VMEM(dk.shape, BF),
            pltpu.VMEM(dk.shape, BF),
            pltpu.VMEM((width, width), BF),
            pltpu.VMEM((width, width), BF),
            pltpu.VMEM(edge, BF),
            pltpu.VMEM(edge, BF),
            pltpu.VMEM((4, height, width), BF),
            pltpu.VMEM((VEC_ROWS, width), F32),
            pltpu.SemaphoreType.DMA((8,)),
            pltpu.SemaphoreType.DMA((10,)),
        ],
        name="project_grad",
    )


def chars_grad_kernel(gb, dq, dk, dv, low, high, wq, wk, wv, out):
    _, block, width = dq.shape
    own = slice(WIN, WIN + block)
    made = gb[0].astype(F32)
    made = made + dot(dq[0], wq[...], NT)
    made = made + dot(dk[0, own, :], wk[...], NT)
    made = made + dot(dv[0, own, :], wv[...], NT)
    out[0, WIN : block - WIN, :] = made[WIN : block - WIN].astype(BF)
    out[0, 0:WIN, :] = (made[0:WIN] + low[0].astype(F32)).astype(BF)
    out[0, block - WIN :, :] = (made[block - WIN :] + high[0].astype(F32)).astype(BF)


def chars_grad(deps, gb, dq, dk, dv, low, high, wq, wk, wv):
    rows, block, width = dq.shape
    ext = dk.shape[1]
    row = lambda n: pl.BlockSpec((1, n, width), lambda r: (r, 0, 0))
    weight = pl.BlockSpec((width, width), lambda r: (0, 0))
    return run(
        chars_grad_kernel,
        deps,
        (gb.reshape(rows, block, width), dq, dk, dv, low, high, wq, wk, wv),
        shape((rows, block, width)),
        [row(block), row(block), row(ext), row(ext), row(WIN), row(WIN)] + [weight] * 3,
        row(block),
        grid=(rows,),
        name="chars_grad",
    )


def swap(value, axis, bit):
    count = lax.axis_size(axis)
    return lax.ppermute(value, axis, [(i, i ^ bit) for i in range(count)])


def plus(left, right):
    return (left.astype(F32) + right.astype(F32)).astype(BF)


def add_kernel(meta, left, right, out):
    out[...] = plus(left[...], right[...])


class Beat:
    def __init__(self, chain, meta):
        self.chain, self.meta = chain, meta
        self.steps, self.carried = [], []

    def add(self, body, args, outs, then, scratch=()):
        self.steps.append((body, args, outs, then, scratch))

    def carry(self, value, then):
        self.carried.append((value, then))

    def emit(self, name):
        args = [self.meta] + [a for step in self.steps for a in step[1]]
        outs = [o for step in self.steps for o in step[2]]
        scratch = [x for step in self.steps for x in step[4]]
        moved = [value for value, _ in self.carried]
        counts = [len(args), len(moved), len(outs), len(moved)]

        def body(*refs):
            ins = refs[1 : counts[0]]
            results = refs[counts[0] + counts[1] : sum(counts[:3])]
            rest = refs[sum(counts) :]
            for step_body, step_args, step_outs, _, step_scratch in self.steps:
                a, o, x = len(step_args), len(step_outs), len(step_scratch)
                step_body(refs[0], *ins[:a], *results[:o], *rest[:x])
                ins, results, rest = ins[a:], results[o:], rest[x:]

        def call(deps, *given):
            return run(
                body,
                deps,
                given,
                outs + [shape(value.shape, value.dtype) for value in moved],
                [spec_smem()] + [spec_vmem()] * (len(args) - 1) + [spec_hbm()] * len(moved),
                [spec_vmem()] * len(outs) + [spec_hbm()] * len(moved),
                scratch=scratch,
                mib=24,
                flops=1,
                nbytes=10**9,
                aliases={len(args) + k: len(outs) + k for k in range(len(moved))},
                name=name,
            )

        made = self.chain(call, *args, *moved, pick=0)
        for step in self.steps:
            step[3](*made[: len(step[2])])
            made = made[len(step[2]) :]
        for (_, then), value in zip(self.carried, made, strict=True):
            then(value)


def split_kernel(meta, keep, arrived, a_out, a_keep, b_out, b_keep):
    half = keep.shape[1] // 2
    part = half // 2
    mine = meta[1]
    for slot, out in ((0, a_out), (1, a_keep)):
        out[...] = plus(keep[slot, 0:half, :], arrived[slot, 0:half, :])
    for slot in range(2):
        for out, which in ((b_out, 1 - mine), (b_keep, mine)):
            at = pl.ds(pl.multiple_of(half + which * part, 16), part)
            out[slot] = plus(keep[slot, at, :], arrived[slot, at, :])


def cross_kernel(meta, a, a_in, b, b_in, a_out, a_keep, b_out, b_keep):
    part = a.shape[0] // 2
    mine = meta[1]
    for out, which in ((a_out, 1 - mine), (a_keep, mine)):
        at = pl.ds(pl.multiple_of(which * part, 16), part)
        out[...] = plus(a[at, :], a_in[at, :])
    b_out[...] = plus(b[0], b_in[0])
    b_keep[...] = plus(b[1], b_in[1])


def merge_kernel(meta, a, a_in, b, b_in, out, keep):
    part = a.shape[0] // 2
    mine = meta[2]
    for k, (left, right) in enumerate(((a, a_in), (b, b_in))):
        for made, which in ((out, 1 - mine), (keep, mine)):
            at = pl.ds(pl.multiple_of(which * part, 16), part)
            made[k] = plus(left[at, :], right[at, :])


def join_kernel(meta, own, other, out):
    part = own.shape[1]
    mine = meta[2]
    for source, which in ((own, mine), (other, 1 - mine)):
        at = pl.ds(pl.multiple_of(which * part, 16), part)
        for k in range(2):
            out[k, at, :] = source[k]


def end_kernel(plan, meta, own, other, *refs):
    outs, whole = refs[:-1], refs[-1]
    part, width = own.shape[1:]
    mine = meta[1]
    for source, which in ((own, mine), (other, 1 - mine)):
        for k in range(2):
            at = pl.ds(pl.multiple_of((2 * k + which) * part, 16), part)
            whole[at, :] = source[k]
    row = 0
    for out, pieces in zip(outs, plan, strict=True):
        for at, rows in pieces:
            out[:, at * width : (at + 1) * width] = whole[row : row + rows, :].astype(F32)
            row += rows


class Sum:
    def __init__(self, keep):
        self.height, self.width = keep.shape[1:]
        self.keep = keep
        self.next = self.split
        self.bit = 2

    def core(self, send):
        self.arrived = swap(send, "seq", 1)

    def split(self, beat):
        height, width = self.height, self.width
        half, part = shape((height // 2, width)), shape((2, height // 4, width))

        def then(a_out, a, b_out, b):
            self.a, self.b = a, b
            self.a_in, self.b_in = swap(a_out, "seq", 2), swap(b_out, "dp", 1)
            self.next = self.cross

        beat.add(split_kernel, [self.keep, self.arrived], [half, half, part, part], then)

    def cross(self, beat):
        part = shape((self.height // 4, self.width))

        def then(a_out, a, b_out, b):
            self.a, self.b = a, b
            self.a_in, self.b_in = swap(a_out, "dp", 1), swap(b_out, "seq", 2)
            self.next = self.merge

        beat.add(cross_kernel, [self.a, self.a_in, self.b, self.b_in], [part] * 4, then)

    def merge(self, beat):
        part = shape((2, self.height // 8, self.width))

        def then(out, keep):
            self.keep = keep
            self.arrived = swap(out, "dp", 2)
            self.next = self.more

        beat.add(merge_kernel, [self.a, self.a_in, self.b, self.b_in], [part] * 2, then)

    def more(self, beat):
        def then(total):
            self.keep = total
            self.bit *= 2
            last = self.bit >= lax.axis_size("dp")
            self.arrived = swap(total, "dp", 2 if last else self.bit)
            self.next = self.join if last else self.more

        beat.add(add_kernel, [self.keep, self.arrived], [shape(self.keep.shape)], then)

    def join(self, beat):
        def then(whole):
            self.keep = whole
            self.arrived = swap(whole, "dp", 1)
            self.next = None

        whole = shape((2, self.height // 4, self.width))
        beat.add(join_kernel, [self.keep, self.arrived], [whole], then)

    def end(self, beat, plan):
        width = self.width
        outs = [shape((pieces[0][1], width * len(pieces)), F32) for pieces in plan]

        def then(*made):
            self.made = made

        beat.add(
            functools.partial(end_kernel, plan),
            [self.keep, self.arrived],
            outs,
            then,
            [pltpu.VMEM((self.height, width), BF)],
        )


class Chain:
    def __init__(self):
        self.last = ()

    def __call__(self, made, *args, pick=-1):
        outs = made(self.last, *args)
        self.last = ((outs[pick] if isinstance(outs, (tuple, list)) else outs),)
        return outs


def shards(
    chars,
    window_mask,
    micro_batch,
    mol_grad,
    query_weight,
    query_bias,
    key_weight,
    value_weight,
    value_bias,
    output_weight,
    output_bias,
    first_gain,
    first_shift,
    inner_weight,
    inner_bias,
    outer_weight,
    outer_bias,
    second_gain,
    second_shift,
    conv_weight,
    conv_bias,
    third_gain,
    third_shift,
):
    rows, block, width = chars.shape
    count = rows * block
    place = lax.axis_index("seq").astype(jnp.int32)
    group = lax.axis_index("dp").astype(jnp.int32)
    meta = jnp.stack([place, group % 2, group // 2 % 2])
    size = lax.axis_size("seq")
    forward_pairs = [(i, i + 1) for i in range(size - 1)]
    backward_pairs = [(i + 1, i) for i in range(size - 1)]
    low = lax.ppermute(chars[:, block - WIN :], "seq", forward_pairs)
    high = lax.ppermute(chars[:, :WIN], "seq", backward_pairs)
    vectors = (
        query_bias,
        value_bias,
        output_bias,
        first_gain,
        first_shift,
        outer_bias,
        second_gain,
        second_shift,
        conv_bias,
        third_gain,
        third_shift,
        inner_bias,
    )
    tokens = chars.reshape(count, width)
    chain = Chain()
    q, k, v, vecs = chain(project, tokens, vectors, query_weight, key_weight, value_weight)
    kv, probs, mixed, n1, inv1, low1, slope, hidden, mol, go, sums3, send_c, keep_c = chain(
        forward,
        meta,
        window_mask,
        micro_batch,
        vecs,
        tokens,
        low,
        high,
        q,
        k,
        v,
        key_weight,
        value_weight,
        output_weight,
        inner_weight,
        outer_weight,
        conv_weight,
        mol_grad.reshape(-1, width),
        pick=10,
    )
    molecules = mol.reshape(mol_grad.shape)
    conv = Sum(keep_c)
    conv.core(send_c)
    send_u, keep_u = chain(outer_grad, meta, go, hidden)
    outer = Sum(keep_u)

    def beat(name, chunks, carried=(), ends=()):
        made = Beat(chain, meta)
        for chunk in chunks:
            chunk.next(made)
        for chunk, plan in ends:
            chunk.end(made, plan)
        for value, then in carried:
            made.carry(value, then)
        made.emit(name)

    beat("beat1", [conv], [(send_u, outer.core)])
    common = (meta, vecs, go, slope, outer_weight, inner_weight, low1)
    send_i, keep_i, isum_a, acc = chain(inner_back, (0, 1), *common, pick=2)
    beat("beat2", [conv, outer])
    send_i, keep_i, isum_b, gb, gm, sums1 = chain(
        inner_back,
        (2, 3),
        *common,
        acc,
        n1,
        inv1,
        output_weight,
        mixed,
        send_i,
        keep_i,
        pick=2,
    )
    inner = Sum(keep_i)
    beat("beat3", [conv, outer], [(send_i, inner.core)])
    grads = ()
    for r in range(rows):
        grads = chain(attention_back, q, kv, probs, gm, rows, r, tuple(grads))
        beat("beat%d" % (4 + r), [conv, outer, inner])
    dq, dk, dv, sums_a = grads
    send_p, keep_p, grad_low, grad_high = chain(
        project_grad,
        meta,
        dq,
        chars,
        dk,
        low,
        high,
        dv,
        key_weight,
        value_weight,
        sums_a,
        sums1,
        sums3,
        isum_a,
        isum_b,
    )
    proj = Sum(keep_p)
    beside = {}

    def from_prev(value):
        beside["low"] = lax.ppermute(value, "seq", forward_pairs)

    def from_next(value):
        beside["high"] = lax.ppermute(value, "seq", backward_pairs)

    beat("tail0", [conv, outer, inner], [(send_p, proj.core)])
    beat("tail1", [proj], [(grad_high, from_prev), (grad_low, from_next)])
    quarter = width // 4
    wide = [[(j, quarter) for j in range(4)]]
    plans = {
        conv: wide,
        outer: wide,
        inner: [[(0, width)], [(0, quarter)]],
        proj: [[(0, quarter)]] * 3 + [[(0, 16)]],
    }
    active, turn = [proj, conv, outer, inner], 0
    waiting = {chunk: 1 for chunk in active if chunk.next is None}
    while active:
        chunks = [chunk for chunk in active if chunk.next is not None]
        ends = [chunk for chunk, due in waiting.items() if due <= turn]
        beat("tail%d" % (2 + turn), chunks, (), [(chunk, plans[chunk]) for chunk in ends])
        for chunk in ends:
            active.remove(chunk)
            del waiting[chunk]
        for chunk in chunks:
            if chunk.next is None:
                waiting[chunk] = turn + (1 if chunk is proj else 2)
        if turn == 0:
            grad_chars = chain(
                chars_grad,
                gb,
                dq,
                dk,
                dv,
                beside["low"],
                beside["high"],
                query_weight,
                key_weight,
                value_weight,
            )
        turn += 1
    (full_c,), (full_u,) = conv.made, outer.made
    full_i, full_o = inner.made
    full_q, full_k, full_v, small = proj.made
    vec_of = lambda i: small[i, :quarter]
    return (
        molecules,
        grad_chars,
        full_q.T,
        vec_of(0),
        full_k.T,
        full_v.T,
        vec_of(1),
        full_o.T,
        vec_of(2),
        vec_of(3),
        vec_of(4),
        full_i,
        small[11:15, :quarter].reshape(-1),
        full_u.T,
        vec_of(5),
        vec_of(6),
        vec_of(7),
        full_c.T,
        vec_of(8),
        vec_of(9),
        vec_of(10),
    )


def solution(mesh):
    split = P("dp", "seq", None)
    placed = (split, P("dp", None), P("dp"), split) + (P(),) * 19
    by_column, by_place = P(None, "seq"), P("seq")
    outs = (
        split,
        split,
        by_column,
        by_place,
        by_column,
        by_column,
        by_place,
        by_column,
        by_place,
        by_place,
        by_place,
        by_column,
        by_place,
        by_column,
        by_place,
        by_place,
        by_place,
        by_column,
        by_place,
        by_place,
        by_place,
    )
    return jax.shard_map(shards, mesh=mesh, in_specs=placed, out_specs=outs, check_vma=False)
```

```python
import functools

import jax
import jax.numpy as jnp
from jax import lax
from jax.experimental import pallas as pl
from jax.experimental.pallas import tpu as pltpu
from jax.sharding import PartitionSpec as P

HEADS = 12
HEAD_DIM = 64
WIN = 128
DOWN = 4
MICRO = 2
EPSILON = 1e-06
NEG_FILL = -1e30
GELU_A = 0.7978845608028654
GELU_B = 0.044715
BF = jnp.bfloat16
F32 = jnp.float32
LANES = 128
MIB = 1 << 20

NN = (((1,), (0,)), ((), ()))
NT = (((1,), (1,)), ((), ()))
TN = (((0,), (0,)), ((), ()))

(V_QB, V_VB, V_OB, V_G1, V_S1, V_OUTB, V_G2, V_S2, V_CB, V_G3, V_S3, V_IB) = range(12)


def dot(left, right, dims=NN):
    return lax.dot_general(left, right, dims, preferred_element_type=F32)


def gelu_both(u):
    square = u * u
    t = jnp.tanh(u * (GELU_A + (GELU_A * GELU_B) * square))
    half = 0.5 + 0.5 * t
    value = u * half
    slope = half + value * (1.0 - t) * (GELU_A + (3.0 * GELU_A * GELU_B) * square)
    return value, slope


def layer_stats(u):
    center = u - jnp.mean(u, axis=-1, keepdims=True)
    inv_dev = lax.rsqrt(jnp.mean(center * center, axis=-1, keepdims=True) + EPSILON)
    return center * inv_dev, inv_dev


def norm_back(grad_out, normal, inv_dev, gain_vec):
    scaled = grad_out * gain_vec
    return inv_dev * (
        scaled
        - jnp.mean(scaled, axis=-1, keepdims=True)
        - normal * jnp.mean(scaled * normal, axis=-1, keepdims=True)
    )


def col_sum(value):
    return jnp.sum(value, axis=0, keepdims=True)


def params(mib=56, **more):
    return pltpu.CompilerParams(vmem_limit_bytes=mib * MIB, **more)


def cost(flops, nbytes):
    return pl.CostEstimate(flops=int(flops), bytes_accessed=int(nbytes), transcendentals=0)


def spec_any():
    return pl.BlockSpec(memory_space=pl.ANY)


def spec_hbm():
    return pl.BlockSpec(memory_space=pltpu.HBM)


def spec_smem():
    return pl.BlockSpec(memory_space=pltpu.SMEM)


def spec_vmem():
    return pl.BlockSpec(memory_space=pltpu.VMEM)


def shape(dims, dtype=BF):
    return jax.ShapeDtypeStruct(tuple(dims), dtype)


def run(body, deps, args, out_shape, in_specs, out_specs, scratch=(), grid=(), prefetch=0, mib=56, flops=10**12, nbytes=10**6, name=None, aliases=None):
    given = len(args)
    single = not isinstance(out_shape, (list, tuple))
    outs = [out_shape] if single else list(out_shape)
    specs = [out_specs] if single else list(out_specs)
    mark = pl.BlockSpec((8, LANES), lambda *_: (0, 0)) if grid else spec_vmem()

    def wrapped(*refs):
        rest = refs[given + len(deps) :]
        rest[len(outs)][...] = jnp.zeros((8, LANES), F32)
        body(*refs[:given], *rest[: len(outs)], *rest[len(outs) + 1 :])

    made = pl.pallas_call(
        wrapped,
        grid_spec=pltpu.PrefetchScalarGridSpec(
            num_scalar_prefetch=prefetch,
            grid=grid,
            in_specs=list(in_specs) + [spec_any()] * len(deps),
            out_specs=specs + [mark],
            scratch_shapes=list(scratch),
        ),
        out_shape=outs + [shape((8, LANES), F32)],
        compiler_params=pltpu.CompilerParams(vmem_limit_bytes=mib * MIB),
        cost_estimate=cost(flops, nbytes),
        input_output_aliases=aliases or {},
        name=name,
    )(*args, *deps)
    return made[0] if single else made[:-1], made[-1]


def head_masks():
    lane = lax.broadcasted_iota(jnp.int32, (1, LANES), 1)
    first = jnp.where(lane < HEAD_DIM, 1.0, 0.0).astype(BF)
    return first, (1.0 - first.astype(F32)).astype(BF)


def twice(block, masks):
    return jnp.concatenate([block * masks[0], block * masks[1]], axis=0)


def slot_of(quarter, place):
    same_x = (quarter // 2 == place // 2).astype(jnp.int32)
    same_core = (quarter % 2 == place % 2).astype(jnp.int32)
    return 2 * same_core + same_x


def project_kernel(names, x_ref, *refs):
    vectors, (wq_ref, wk_ref, wv_ref, q_ref, k_ref, v_ref, vec_ref) = refs[:names], refs[names:]
    width = x_ref.shape[1]
    part = wq_ref.shape[1]
    step = pl.program_id(0)

    @pl.when(step == 0)
    def _():
        row = 0
        for ref in vectors:
            value = ref[...].astype(F32)
            for k in range(value.shape[0] // width):
                vec_ref[row : row + 1, :] = value[k * width : (k + 1) * width].reshape(1, width)
                row += 1
        vec_ref[row:, :] = jnp.zeros((vec_ref.shape[0] - row, width), F32)

    x = x_ref[...]
    at = pl.ds(pl.multiple_of(step * part, part), part)
    queries = (dot(x, wq_ref[...]) + vec_ref[V_QB : V_QB + 1, at]).astype(BF)
    q_ref[...] = queries * jnp.asarray(HEAD_DIM**-0.5, BF)
    k_ref[...] = dot(x, wk_ref[...]).astype(BF)
    v_ref[...] = (dot(x, wv_ref[...]) + vec_ref[V_VB : V_VB + 1, at]).astype(BF)


def project(deps, tokens, vectors, wq, wk, wv):
    count, width = tokens.shape
    part = 256
    column = pl.BlockSpec((width, part), lambda i: (0, i))
    out = pl.BlockSpec((count, part), lambda i: (0, i))
    height = rounded_up(sum(v.shape[0] for v in vectors) // width, 8)
    return run(
        functools.partial(project_kernel, len(vectors)),
        deps,
        (tokens, *vectors, wq, wk, wv),
        [shape((count, width))] * 3 + [shape((height, width), F32)],
        [pl.BlockSpec((count, width), lambda i: (0, 0))]
        + [pl.BlockSpec(v.shape, lambda i: (0,)) for v in vectors]
        + [column] * 3,
        [out] * 3 + [pl.BlockSpec((height, width), lambda i: (0, 0))],
        grid=(width // part,),
        mib=60,
        name="project",
    )


def forward_kernel(
    rows,
    wins,
    windows_all,
    meta,
    wmask,
    mbatch,
    vec,
    chars_h,
    low_h,
    high_h,
    q_h,
    k_h,
    v_h,
    wk_h,
    wv_h,
    wo_h,
    wi_h,
    wout_h,
    wc_h,
    mg_h,
    kv_o,
    pt_o,
    mixed_o,
    n1_o,
    inv1_o,
    low1_o,
    slope_o,
    hidden_o,
    mol_o,
    go_o,
    sums_o,
    send_o,
    keep_o,
    q,
    kv,
    halo,
    wkv,
    wo,
    chars,
    wi,
    wout,
    wc,
    mg,
    probs,
    mixed,
    acc,
    strips,
    low1,
    n1,
    inv1,
    slope,
    hidden,
    n2,
    inv2,
    merged,
    mol,
    sem_in,
    sem_p,
    sem_h,
    sem_out,
):
    place = meta[0]
    block = wins * WIN
    width = chars.shape[-1]
    count = rows * block
    pairs = width // LANES
    parts = wi.shape[1] // width

    def copy_in(index, src, dst):
        made = pltpu.make_async_copy(src, dst, sem_in.at[index])
        made.start()
        return made

    halo_in = [
        copy_in(0, low_h, halo.at[0]),
        copy_in(1, high_h, halo.at[1]),
        copy_in(2, wk_h, wkv.at[0]),
        copy_in(3, wv_h, wkv.at[1]),
    ]
    qkv_in = [copy_in(4, q_h, q)]
    for r in range(rows):
        qkv_in.append(
            copy_in(5 + 2 * r, k_h.at[pl.ds(r * block, block)], kv.at[r, pl.ds(WIN, block)])
        )
        qkv_in.append(
            copy_in(
                6 + 2 * r, v_h.at[pl.ds(r * block, block)], kv.at[rows + r, pl.ds(WIN, block)]
            )
        )
    base = 5 + 2 * rows

    def copy_out(index, src, dst):
        made = pltpu.make_async_copy(src, dst, sem_out.at[index])
        made.start()
        return made

    for made in halo_in:
        made.wait()
    beside = halo[...].reshape(2 * rows * WIN, width)
    keys = dot(beside, wkv[0]).astype(BF)
    values = (dot(beside, wkv[1]) + vec[V_VB : V_VB + 1, :]).astype(BF)
    for side in range(2):
        start = side * (block + WIN)
        for r in range(rows):
            at = (side * rows + r) * WIN
            kv[r, pl.ds(start, WIN), :] = keys[at : at + WIN]
            kv[rows + r, pl.ds(start, WIN), :] = values[at : at + WIN]
    for made in qkv_in:
        made.wait()
    wo_in = copy_in(base, wo_h, wo)
    chars_in = copy_in(base + 1, chars_h, chars)
    wi_in = copy_in(base + 2, wi_h, wi)
    wout_in = copy_in(base + 3, wout_h, wout)
    kv_out = copy_out(0, kv, kv_o)

    masks = head_masks()

    def pair_step(it, carry):
        r = it // pairs
        pair = it % pairs
        slot = it % 2
        lanes = pl.ds(pl.multiple_of(pair * LANES, LANES), LANES)

        @pl.when(it >= 2)
        def _():
            pltpu.make_async_copy(probs.at[slot], pt_o.at[it - 2], sem_p.at[slot]).wait()

        every = []
        for w in range(wins):
            queries = twice(q[pl.ds(r * block + w * WIN, WIN), lanes], masks)
            every.append(dot(kv[r, pl.ds(w * WIN, 3 * WIN), lanes], queries, NT))
        chances = []
        for w, scores in enumerate(every):
            at = place * wins + w
            low_ok = (at >= 1) & (wmask[r, jnp.maximum(at - 1, 0)] > 0)
            high_ok = (at + 1 < windows_all) & (wmask[r, jnp.minimum(at + 1, windows_all - 1)] > 0)
            scores = jnp.concatenate(
                [
                    scores[0:WIN] + jnp.where(low_ok, 0.0, NEG_FILL),
                    scores[WIN : 2 * WIN],
                    scores[2 * WIN :] + jnp.where(high_ok, 0.0, NEG_FILL),
                ],
                axis=0,
            )
            shifted = jnp.exp(scores - jnp.max(scores, axis=0, keepdims=True))
            total = jnp.sum(shifted, axis=0, keepdims=True)
            chances.append((shifted * (1.0 / total)).astype(BF))
            probs[slot, w] = chances[w]
        for w, chance in enumerate(chances):
            stacked = jnp.concatenate([chance[:, :LANES], chance[:, LANES:]], axis=0)
            values_win = twice(kv[rows + r, pl.ds(w * WIN, 3 * WIN), lanes], masks)
            mixed[pl.ds(r * block + w * WIN, WIN), lanes] = dot(stacked, values_win, TN).astype(BF)
        pltpu.make_async_copy(probs.at[slot], pt_o.at[it], sem_p.at[slot]).start()
        return carry

    steps = rows * pairs
    lax.fori_loop(0, steps, pair_step, 0)
    mixed_out = copy_out(1, mixed, mixed_o)

    wo_in.wait()
    chars_in.wait()
    wc_in = copy_in(base + 4, wc_h, wc)
    mg_in = copy_in(base + 5, mg_h, mg)
    piece = 256

    pieces = [pl.ds(i * piece, piece) for i in range(count // piece)]
    branches = [dot(mixed[at, :], wo[...]) for at in pieces]
    for at, branch in zip(pieces, branches, strict=True):
        u = branch + vec[V_OB : V_OB + 1, :] + chars[at, :].astype(F32)
        normal, inv = layer_stats(u)
        first = normal * vec[V_G1 : V_G1 + 1, :] + vec[V_S1 : V_S1 + 1, :]
        n1[at, :] = normal.astype(BF)
        inv1[at, :] = inv
        low1[at, :] = first.astype(BF)
        acc[at, :] = first + vec[V_OUTB : V_OUTB + 1, :]
    outs = [mixed_out, copy_out(2, n1, n1_o), copy_out(3, inv1, inv1_o), copy_out(4, low1, low1_o)]

    wi_in.wait()
    wout_in.wait()

    def ffn_step(c, carry):
        slot = c % 2
        columns = pl.ds(pl.multiple_of(c * width, width), width)

        @pl.when(c >= 2)
        def _():
            pltpu.make_async_copy(slope.at[slot], slope_o.at[c - 2], sem_h.at[slot]).wait()
            pltpu.make_async_copy(hidden.at[slot], hidden_o.at[c - 2], sem_h.at[2 + slot]).wait()

        bias = vec[pl.ds(V_IB + c, 1), :]
        half = count // 2
        parts_of = [pl.ds(k * half, half) for k in range(2)]
        upper, lower = (dot(low1[at, :], wi[:, columns]) + bias for at in parts_of)
        for at, u in zip(parts_of, (upper, lower), strict=True):
            value, steep = gelu_both(u)
            slope[slot, at, :] = steep.astype(BF)
            h = value.astype(BF)
            hidden[slot, at, :] = h
            acc[at, :] += dot(h, wout[columns, :])
        pltpu.make_async_copy(slope.at[slot], slope_o.at[c], sem_h.at[slot]).start()
        pltpu.make_async_copy(hidden.at[slot], hidden_o.at[c], sem_h.at[2 + slot]).start()
        return carry

    lax.fori_loop(0, parts, ffn_step, 0)

    def second_step(i, carry):
        at = pl.ds(pl.multiple_of(i * piece, piece), piece)
        normal, inv = layer_stats(acc[at, :])
        n2[at, :] = normal.astype(BF)
        inv2[at, :] = inv
        second = normal * vec[V_G2 : V_G2 + 1, :] + vec[V_S2 : V_S2 + 1, :]
        for t in range(pairs):
            strips[t, at, :] = second[:, t * LANES : (t + 1) * LANES]
        return carry

    lax.fori_loop(0, count // piece, second_step, 0, unroll=True)

    wc_in.wait()
    mg_in.wait()
    mols = count // DOWN
    conv = jnp.zeros((mols, width), F32) + vec[V_CB : V_CB + 1, :]
    for i in range(DOWN):
        for t in range(pairs):
            merged[i, :, t * LANES : (t + 1) * LANES] = strips[
                t, pl.ds(i, mols, stride=DOWN), :
            ].astype(BF)
        part = merged[i]
        conv = conv + dot(part, wc[pl.ds(i * width, width), :])
    value, steep = gelu_both(conv)
    normal, inv = layer_stats(value)
    per_win = WIN // DOWN
    which = lax.broadcasted_iota(jnp.int32, (mols, 1), 0) // per_win
    live = jnp.zeros((mols, 1), F32)
    total = jnp.ones((mols, 1), F32)
    lengths = []
    for r in range(rows):
        length = wmask[r, 0]
        for w in range(1, windows_all):
            length = length + wmask[r, w]
        lengths.append(length)
    for r in range(rows):
        same = jnp.int32(0)
        for other in range(rows):
            same = same + jnp.where(mbatch[other] == mbatch[r], lengths[other], 0)
        same = (same * per_win).astype(F32)
        for w in range(wins):
            here = which == r * wins + w
            live = jnp.where(here, wmask[r, place * wins + w].astype(F32), live)
            total = jnp.where(here, same, total)
    weight = (rows // MICRO * windows_all * per_win) / total
    gain = vec[V_G3 : V_G3 + 1, :]
    mol[...] = ((normal * gain + vec[V_S3 : V_S3 + 1, :]) * live).astype(BF)
    outs.append(copy_out(5, mol, mol_o))
    grad_mol = mg[...].astype(F32) * (weight * live)
    grad_conv = (steep * norm_back(grad_mol, normal, inv, gain)).astype(BF)
    sums_o[0:1, :] = col_sum(grad_mol * normal)
    sums_o[1:2, :] = col_sum(grad_mol)
    sums_o[2:3, :] = col_sum(grad_conv.astype(F32))
    sums_o[3:, :] = jnp.zeros((sums_o.shape[0] - 3, width), F32)

    kv_out.wait()
    across = grad_conv.T
    quarter = width // 4
    for i in range(DOWN):
        made = dot(across, merged[i]).astype(BF)
        for number in range(4):
            kv[slot_of(jnp.int32(number), place), pl.ds(i * quarter, quarter), :] = made[
                number * quarter : (number + 1) * quarter
            ]
    outs.append(copy_out(6, kv.at[pl.ds(0, 2)], send_o))
    outs.append(copy_out(7, kv.at[pl.ds(2, 2)], keep_o))

    for i in range(DOWN):
        made = dot(grad_conv, wc[pl.ds(i * width, width), :], NT)
        for t in range(pairs):
            strips[t, pl.ds(i, mols, stride=DOWN), :] = made[:, t * LANES : (t + 1) * LANES]
    gain = vec[V_G2 : V_G2 + 1, :]

    def back_step(i, carry):
        at = pl.ds(pl.multiple_of(i * piece, piece), piece)
        grad = jnp.concatenate([strips[t, at, :] for t in range(pairs)], axis=1)
        normal = n2[at, :].astype(F32)
        made = norm_back(grad, normal, inv2[at, :], gain).astype(BF)
        n2[at, :] = made
        sums_o[3:4, :] += col_sum(grad * normal)
        sums_o[4:5, :] += col_sum(grad)
        sums_o[5:6, :] += col_sum(made.astype(F32))
        return carry

    lax.fori_loop(0, count // piece, back_step, 0, unroll=True)
    outs.append(copy_out(8, n2, go_o))

    for made in outs:
        made.wait()
    for it in range(max(0, steps - 2), steps):
        pltpu.make_async_copy(probs.at[it % 2], pt_o.at[it], sem_p.at[it % 2]).wait()
    for c in range(max(0, parts - 2), parts):
        pltpu.make_async_copy(slope.at[c % 2], slope_o.at[c], sem_h.at[c % 2]).wait()
        pltpu.make_async_copy(hidden.at[c % 2], hidden_o.at[c], sem_h.at[2 + c % 2]).wait()


def forward(deps, meta, wmask, mbatch, vecs, chars, low, high, q, k, v, wk, wv, wo, wi, wout, wc, mg):
    rows = wmask.shape[0]
    windows_all = wmask.shape[1]
    count, width = q.shape
    block = count // rows
    wins = block // WIN
    ff = wi.shape[1]
    parts = ff // width
    mols = count // DOWN
    pairs = width // LANES
    ext = block + 2 * WIN
    outs = [
        shape((2 * rows, ext, width)),
        shape((rows * pairs, wins, 3 * WIN, 2 * LANES)),
        shape((count, width)),
        shape((count, width)),
        shape((count, 1), F32),
        shape((count, width)),
        shape((parts, count, width)),
        shape((parts, count, width)),
        shape((mols, width)),
        shape((count, width)),
        shape((8, width), F32),
        shape((2, DOWN * width // 4, width)),
        shape((2, DOWN * width // 4, width)),
    ]
    out_specs = [spec_any()] * len(outs)
    out_specs[10] = spec_vmem()
    return run(
        functools.partial(forward_kernel, rows, wins, windows_all),
        deps,
        (meta, wmask, mbatch, vecs, chars, low, high, q, k, v, wk, wv, wo, wi, wout, wc, mg),
        outs,
        [spec_smem()] * 3 + [spec_vmem()] + [spec_any()] * 13,
        out_specs,
        scratch=[
            pltpu.VMEM((count, width), BF),
            pltpu.VMEM((2 * rows, ext, width), BF),
            pltpu.VMEM((2, rows, WIN, width), BF),
            pltpu.VMEM((2, width, width), BF),
            pltpu.VMEM((width, width), BF),
            pltpu.VMEM((count, width), BF),
            pltpu.VMEM((width, ff), BF),
            pltpu.VMEM((ff, width), BF),
            pltpu.VMEM((DOWN * width, width), BF),
            pltpu.VMEM((mols, width), BF),
            pltpu.VMEM((2, wins, 3 * WIN, 2 * LANES), BF),
            pltpu.VMEM((count, width), BF),
            pltpu.VMEM((count, width), F32),
            pltpu.VMEM((pairs, count, LANES), F32),
            pltpu.VMEM((count, width), BF),
            pltpu.VMEM((count, width), BF),
            pltpu.VMEM((count, 1), F32),
            pltpu.VMEM((2, count, width), BF),
            pltpu.VMEM((2, count, width), BF),
            pltpu.VMEM((count, width), BF),
            pltpu.VMEM((count, 1), F32),
            pltpu.VMEM((DOWN, mols, width), BF),
            pltpu.VMEM((mols, width), BF),
            pltpu.SemaphoreType.DMA((11 + 2 * rows,)),
            pltpu.SemaphoreType.DMA((2,)),
            pltpu.SemaphoreType.DMA((4,)),
            pltpu.SemaphoreType.DMA((9,)),
        ],
        mib=60,
        name="forward",
    )


def outer_grad_kernel(meta, go, hidden, send, keep, across):
    place = meta[0]
    width = go.shape[1]
    quarter = width // 4

    @pl.when(pl.program_id(0) == 0)
    def _():
        turned = go[...].T
        for number in range(4):
            across[slot_of(jnp.int32(number), place)] = turned[
                number * quarter : (number + 1) * quarter
            ]

    left = across[...].reshape(width, go.shape[0])
    made = dot(left, hidden[0]).astype(BF)
    for j in range(2):
        send[j] = made[j * quarter : (j + 1) * quarter]
        keep[j] = made[(2 + j) * quarter : (3 + j) * quarter]


def outer_grad(deps, meta, go, hidden):
    parts, count, width = hidden.shape
    quarter = width // 4
    out = pl.BlockSpec((2, quarter, width), lambda i, m: (0, i, 0))
    return run(
        outer_grad_kernel,
        deps,
        (meta, go, hidden),
        [shape((2, parts * quarter, width))] * 2,
        [
            pl.BlockSpec((count, width), lambda i, m: (0, 0)),
            pl.BlockSpec((1, count, width), lambda i, m: (i, 0, 0)),
        ],
        [out] * 2,
        scratch=[pltpu.VMEM((4, quarter, count), BF)],
        grid=(parts,),
        prefetch=1,
        name="outer_grad",
    )


def slot_copies(src, send, keep, slot, at, sem):
    out = pltpu.make_async_copy(src, send.at[jnp.minimum(slot, 1), at], sem)
    own = pltpu.make_async_copy(src, keep.at[jnp.maximum(slot - 2, 0), at], sem)

    def start():
        @pl.when(slot < 2)
        def _():
            out.start()

        @pl.when(slot >= 2)
        def _():
            own.start()

    return start, out.wait


def inner_back_kernel(first, chosen, meta, vec, go_h, slope_h, wout_h, wi_h, low1_h, *refs):
    if first:
        ins, refs = (), refs
    else:
        ins, refs = refs[:5], refs[7:]
    send, keep, isum, *refs = refs
    if first:
        acc_o, *refs = refs
    else:
        gb_o, gm_o, sums, *refs = refs
    go, slope, wout, wi, low1, acc, grads, *refs = refs
    if not first:
        n1, inv1, wo, mixed, gb, gm, rest, *refs = refs
    sem_in, sem_out = refs
    count, width = go.shape
    place = meta[0]
    quarter = width // 4
    waits = []

    def bring(src, dst):
        made = pltpu.make_async_copy(src, dst, sem_in.at[len(waits)])
        made.start()
        waits.append(made)
        return made

    go_in = bring(go_h, go)
    parts_in = []
    for k, c in enumerate(chosen):
        at = pl.ds(c * width, width)
        parts_in.append(
            [
                bring(wout_h.at[at], wout.at[k]),
                bring(slope_h.at[c], slope.at[k]),
                bring(wi_h.at[:, at], wi.at[k]),
            ]
        )
        if k == 0:
            low1_in = bring(low1_h, low1)
            acc_in = None if first else bring(ins[0], acc)
    if not first:
        late = [bring(src, dst) for src, dst in zip(ins[1:], (n1, inv1, wo, mixed), strict=True)]
    go_in.wait()
    half = count // 2
    halves = [slice(k * half, (k + 1) * half) for k in range(2)]
    outs = []
    across = None
    for k, c in enumerate(chosen):
        parts_in[k][0].wait()
        steep = [dot(go[at, :], wout[k], NT) for at in halves]
        if across is None:
            low1_in.wait()
            across = low1[...].T
        parts_in[k][1].wait()
        parts_in[k][2].wait()
        if k == 0 and not first:
            acc_in.wait()
        low = []
        for at, grad in zip(halves, steep, strict=True):
            low.append((slope[k, at, :].astype(F32) * grad).astype(BF))
            added = dot(low[-1], wi[k], NT)
            if first and k == 0:
                acc[at, :] = go[at, :].astype(F32) + added
            else:
                acc[at, :] += added
        made = jnp.concatenate(low, axis=0)
        isum[k] = jnp.broadcast_to(col_sum(made.astype(F32)), (8, width))
        grads[k] = dot(across, made).astype(BF)
        slot = slot_of(jnp.int32(c), place)
        start, wait = slot_copies(
            grads.at[k], send, keep, slot, pl.ds(0, width), sem_out.at[len(outs)]
        )
        start()
        outs.append(wait)

    def leave(src, dst):
        made = pltpu.make_async_copy(src, dst, sem_out.at[len(outs)])
        made.start()
        outs.append(made.wait)

    if first:
        leave(acc, acc_o)
    else:
        for made in late:
            made.wait()
        gain = vec[V_G1 : V_G1 + 1, :]
        piece = 256
        sums[...] = jnp.zeros(sums.shape, F32)
        lows = []
        for j in range(count // piece):
            at = slice(j * piece, (j + 1) * piece)
            grad = acc[at, :]
            normal = n1[at, :].astype(F32)
            lows.append(norm_back(grad, normal, inv1[at, :], gain).astype(BF))
            gb[at, :] = lows[-1]
            sums[0:1, :] += col_sum(grad * normal)
            sums[1:2, :] += col_sum(grad)
            sums[2:3, :] += col_sum(lows[-1].astype(F32))
        leave(gb, gb_o)
        for j in range(count // piece):
            gm[j * piece : (j + 1) * piece, :] = dot(lows[j], wo[...], NT).astype(BF)
        leave(gm, gm_o)
        rest[...] = jnp.zeros(rest.shape, BF)
        extra = rest.shape[1] - quarter
        made = dot(gb[...], mixed[...], TN).astype(BF)
        for number in range(4):
            rest[number, 0:quarter, :] = made[number * quarter : (number + 1) * quarter]
            slot = slot_of(jnp.int32(number), place)
            start, wait = slot_copies(
                rest.at[number],
                send,
                keep,
                slot,
                pl.ds(width, quarter + extra),
                sem_out.at[len(outs)],
            )
            start()
            outs.append(wait)
    for wait in outs:
        wait()


def rounded_up(value, unit):
    return -(-value // unit) * unit


def inner_back(deps, chosen, meta, vecs, go, slope, wout, wi, low1, *more):
    _, count, width = slope.shape
    first = not more
    quarter = width // 4
    height = rounded_up(width + quarter, 8 * 16)
    both = shape((2, height, width))
    outs = [both, both, shape((2, 8, width), F32)]
    out_specs = [spec_hbm(), spec_hbm(), spec_vmem()]
    scratch = [
        pltpu.VMEM((count, width), BF),
        pltpu.VMEM((2, count, width), BF),
        pltpu.VMEM((2, width, width), BF),
        pltpu.VMEM((2, width, width), BF),
        pltpu.VMEM((count, width), BF),
        pltpu.VMEM((count, width), F32),
        pltpu.VMEM((2, width, width), BF),
    ]
    if first:
        outs += [shape((count, width), F32)]
        out_specs += [spec_hbm()]
    else:
        outs += [shape((count, width)), shape((count, width)), shape((8, width), F32)]
        out_specs += [spec_hbm(), spec_hbm(), spec_vmem()]
        scratch += [
            pltpu.VMEM((count, width), BF),
            pltpu.VMEM((count, 1), F32),
            pltpu.VMEM((width, width), BF),
            pltpu.VMEM((count, width), BF),
            pltpu.VMEM((count, width), BF),
            pltpu.VMEM((count, width), BF),
            pltpu.VMEM((4, height - width, width), BF),
        ]
    scratch += [pltpu.SemaphoreType.DMA((13,)), pltpu.SemaphoreType.DMA((8,))]
    return run(
        functools.partial(inner_back_kernel, first, chosen),
        deps,
        (meta, vecs, go, slope, wout, wi, low1, *more),
        outs,
        [spec_smem(), spec_vmem()] + [spec_any()] * (5 + len(more)),
        out_specs,
        scratch=scratch,
        aliases={} if first else {12: 0, 13: 1},
        name="inner_back%d" % chosen[0],
    )


def attention_back_kernel(wins, q, k, v, probs, gm, dq, dk, dv, sums):
    masks = head_masks()
    here = [slice(w * WIN, (w + 1) * WIN) for w in range(wins)]
    span = [slice(w * WIN, (w + 3) * WIN) for w in range(wins)]
    grad_out = [twice(gm[0, at, :], masks) for at in here]
    queries = [twice(q[0, at, :], masks) for at in here]
    grad_probs = [dot(v[0, span[w], :], grad_out[w], NT) for w in range(wins)]
    grad_values = [dot(probs[0, w], grad_out[w]) for w in range(wins)]
    grad_scores = []
    for w in range(wins):
        chance = probs[0, w].astype(F32)
        product = chance * grad_probs[w]
        total = jnp.sum(product, axis=0, keepdims=True)
        grad_scores.append((product - chance * total).astype(BF))
    grad_keys = [dot(grad_scores[w], queries[w]) for w in range(wins)]
    q_sum = jnp.zeros((1, LANES), F32)
    for w in range(wins):
        made = grad_scores[w]
        stacked = jnp.concatenate([made[:, :LANES], made[:, LANES:]], axis=0)
        made = dot(stacked, twice(k[0, span[w], :], masks), TN) * HEAD_DIM**-0.5
        low = made.astype(BF)
        dq[0, here[w], :] = low
        q_sum = q_sum + col_sum(low.astype(F32))
    v_sum = jnp.zeros((1, LANES), F32)
    for parts, out in ((grad_keys, dk), (grad_values, dv)):
        for b in range(wins + 2):
            uses = [w for w in range(wins) if 0 <= b - w < 3]
            pieces = [parts[w][(b - w) * WIN : (b - w + 1) * WIN] for w in uses]
            made = sum(pieces[1:], pieces[0])
            out[0, b * WIN : (b + 1) * WIN, :] = made.astype(BF)
            if out is dv:
                v_sum = v_sum + col_sum(made)
    sums[0, 0:1, :] = q_sum
    sums[0, 1:2, :] = v_sum
    sums[0, 2:, :] = jnp.zeros((6, LANES), F32)


def attention_back(deps, q, kv, probs, gm, rows, row, before):
    count, width = q.shape
    block = count // rows
    wins = block // WIN
    ext = kv.shape[1]
    pairs = width // LANES
    own = pl.BlockSpec((1, block, LANES), lambda p: (row, 0, p))
    keys = pl.BlockSpec((1, ext, LANES), lambda p: (row, 0, p))
    values = pl.BlockSpec((1, ext, LANES), lambda p: (rows + row, 0, p))

    def body(q, k, v, probs, gm, *refs):
        attention_back_kernel(wins, q, k, v, probs, gm, *refs[len(before) :])

    return run(
        body,
        deps,
        (q.reshape(rows, block, width), kv, kv, probs, gm.reshape(rows, block, width), *before),
        [
            shape((rows, block, width)),
            shape((rows, ext, width)),
            shape((rows, ext, width)),
            shape((rows, 8, width), F32),
        ],
        [
            own,
            keys,
            values,
            pl.BlockSpec((1, wins, 3 * WIN, 2 * LANES), lambda p: (row * pairs + p, 0, 0, 0)),
            own,
        ]
        + [spec_any()] * len(before),
        [own, keys, keys, pl.BlockSpec((1, 8, LANES), lambda p: (row, 0, p))],
        grid=(pairs,),
        mib=56,
        aliases={5 + k: k for k in range(len(before))},
        name="attention_back%d" % row,
    )


VEC_ROWS = 64


def project_grad_kernel(
    meta,
    dq_h,
    chars_h,
    dk_h,
    low_h,
    high_h,
    dv_h,
    sums_a,
    sums1,
    sums3,
    isum_a,
    isum_b,
    send_o,
    keep_o,
    dq,
    dk,
    dv,
    ext,
    made_all,
    small,
    sem_in,
    sem_out,
):
    rows, full, width = dk.shape
    block = full - 2 * WIN
    count = rows * block
    place = meta[0]
    quarter = width // 4
    started = []
    pairs = [
        (dq_h, dq),
        (chars_h, ext.at[:, pl.ds(WIN, block)]),
        (dk_h, dk),
        (low_h, ext.at[:, pl.ds(0, WIN)]),
        (high_h, ext.at[:, pl.ds(WIN + block, WIN)]),
        (dv_h, dv),
    ]
    for k, (src, dst) in enumerate(pairs):
        started.append(pltpu.make_async_copy(src, dst, sem_in.at[k]))
        started[-1].start()
    leaving = []

    def leave(src, dst):
        leaving.append(pltpu.make_async_copy(src, dst, sem_out.at[len(leaving)]))
        leaving[-1].start()

    def put(index, made):
        at = pl.ds(index * quarter, quarter)
        for number in range(4):
            made_all[slot_of(jnp.int32(number), place), at, :] = made[
                number * quarter : (number + 1) * quarter
            ]
        leave(made_all.at[pl.ds(0, 2), at], send_o.at[:, at])
        leave(made_all.at[pl.ds(2, 2), at], keep_o.at[:, at])

    att = sums_a[0]
    for r in range(1, rows):
        att = att + sums_a[r]
    stack = [att[0:1], att[1:2], sums1[2:3], sums1[0:1], sums1[1:2], sums3[5:6]]
    stack += [sums3[3:4], sums3[4:5], sums3[2:3], sums3[0:1], sums3[1:2]]
    at = pl.ds(3 * quarter, VEC_ROWS)
    for number in range(4):
        mine = slice(number * quarter, (number + 1) * quarter)
        small[...] = jnp.zeros(small.shape, F32)
        for row, vector in enumerate(stack):
            small[row : row + 1, 0:quarter] = vector[:, mine]
        for j in range(4):
            small[len(stack) + j : len(stack) + j + 1, 0:quarter] = (isum_a, isum_b)[number // 2][
                number % 2, 0:1, j * quarter : (j + 1) * quarter
            ]
        made_all[slot_of(jnp.int32(number), place), at, :] = small[...].astype(BF)
    leave(made_all.at[pl.ds(0, 2), at], send_o.at[:, at])
    leave(made_all.at[pl.ds(2, 2), at], keep_o.at[:, at])

    started[0].wait()
    started[1].wait()
    own = ext[:, WIN : WIN + block, :].reshape(count, width)
    put(0, dot(dq[...].reshape(count, width), own, TN).astype(BF))
    started[2].wait()
    started[3].wait()
    started[4].wait()
    every = ext[...].reshape(rows * full, width)
    put(1, dot(dk[...].reshape(rows * full, width), every, TN).astype(BF))
    started[5].wait()
    put(2, dot(dv[...].reshape(rows * full, width), every, TN).astype(BF))
    for made in leaving:
        made.wait()


def project_grad(deps, meta, dq, chars, dk, low, high, dv, *sums):
    rows, full, width = dk.shape
    height = 3 * width // 4 + VEC_ROWS
    return run(
        project_grad_kernel,
        deps,
        (meta, dq, chars, dk, low, high, dv, *sums),
        [shape((2, height, width))] * 2,
        [spec_smem()] + [spec_any()] * 6 + [spec_vmem()] * len(sums),
        [spec_hbm()] * 2,
        scratch=[
            pltpu.VMEM(dq.shape, BF),
            pltpu.VMEM(dk.shape, BF),
            pltpu.VMEM(dk.shape, BF),
            pltpu.VMEM(dk.shape, BF),
            pltpu.VMEM((4, height, width), BF),
            pltpu.VMEM((VEC_ROWS, width), F32),
            pltpu.SemaphoreType.DMA((6,)),
            pltpu.SemaphoreType.DMA((8,)),
        ],
        name="project_grad",
    )


def halo_grad_kernel(dk_low, dv_low, dk_high, dv_high, wk, wv, low, high):
    rows, edge, width = low.shape
    for dk, dv, out in ((dk_low, dv_low, low), (dk_high, dv_high, high)):
        keys = dk[...].reshape(rows * edge, width)
        values = dv[...].reshape(rows * edge, width)
        made = dot(keys, wk[...], NT) + dot(values, wv[...], NT)
        out[...] = made.astype(BF).reshape(rows, edge, width)


def halo_grad(deps, dk, dv, wk, wv):
    rows, full, width = dk.shape
    edge = (rows, WIN, width)
    first = pl.BlockSpec(edge, lambda i: (0, 0, 0))
    last = pl.BlockSpec(edge, lambda i: (0, full // WIN - 1, 0))
    whole = pl.BlockSpec((width, width), lambda i: (0, 0))
    return run(
        halo_grad_kernel,
        deps,
        (dk, dv, dk, dv, wk, wv),
        [shape(edge)] * 2,
        [first, first, last, last, whole, whole],
        [first] * 2,
        grid=(1,),
        mib=24,
        name="halo_grad",
    )


def chars_grad_kernel(gb, dq, dk, dv, low, high, wq, wk, wv, out):
    _, block, width = dq.shape
    own = slice(WIN, WIN + block)
    made = gb[0].astype(F32)
    made = made + dot(dq[0], wq[...], NT)
    made = made + dot(dk[0, own, :], wk[...], NT)
    made = made + dot(dv[0, own, :], wv[...], NT)
    out[0, WIN : block - WIN, :] = made[WIN : block - WIN].astype(BF)
    out[0, 0:WIN, :] = (made[0:WIN] + low[0].astype(F32)).astype(BF)
    out[0, block - WIN :, :] = (made[block - WIN :] + high[0].astype(F32)).astype(BF)


def chars_grad(deps, gb, dq, dk, dv, low, high, wq, wk, wv):
    rows, block, width = dq.shape
    ext = dk.shape[1]
    row = lambda n: pl.BlockSpec((1, n, width), lambda r: (r, 0, 0))
    weight = pl.BlockSpec((width, width), lambda r: (0, 0))
    return run(
        chars_grad_kernel,
        deps,
        (gb.reshape(rows, block, width), dq, dk, dv, low, high, wq, wk, wv),
        shape((rows, block, width)),
        [row(block), row(block), row(ext), row(ext), row(WIN), row(WIN)] + [weight] * 3,
        row(block),
        grid=(rows,),
        mib=63,
        name="chars_grad",
    )


def swap(value, axis, bit):
    count = lax.axis_size(axis)
    return lax.ppermute(value, axis, [(i, i ^ bit) for i in range(count)])


def plus(left, right):
    return (left.astype(F32) + right.astype(F32)).astype(BF)


def add_kernel(meta, left, right, out):
    out[...] = plus(left[...], right[...])


class Beat:
    def __init__(self, chain, meta):
        self.chain, self.meta = chain, meta
        self.steps, self.carried = [], []

    def add(self, body, args, outs, then, scratch=()):
        self.steps.append((body, args, outs, then, scratch))

    def carry(self, value, then):
        self.carried.append((value, then))

    def emit(self, name):
        args = [self.meta] + [a for step in self.steps for a in step[1]]
        outs = [o for step in self.steps for o in step[2]]
        scratch = [x for step in self.steps for x in step[4]]
        moved = [value for value, _ in self.carried]
        counts = [len(args), len(moved), len(outs), len(moved)]

        def body(*refs):
            ins = refs[1 : counts[0]]
            results = refs[counts[0] + counts[1] : sum(counts[:3])]
            rest = refs[sum(counts) :]
            for step_body, step_args, step_outs, _, step_scratch in self.steps:
                a, o, x = len(step_args), len(step_outs), len(step_scratch)
                step_body(refs[0], *ins[:a], *results[:o], *rest[:x])
                ins, results, rest = ins[a:], results[o:], rest[x:]

        def call(deps, *given):
            return run(
                body,
                deps,
                given,
                outs + [shape(value.shape, value.dtype) for value in moved],
                [spec_smem()] + [spec_vmem()] * (len(args) - 1) + [spec_hbm()] * len(moved),
                [spec_vmem()] * len(outs) + [spec_hbm()] * len(moved),
                scratch=scratch,
                mib=24,
                flops=1 if self.steps and self.steps[0][4] == () else 10**12,
                nbytes=10**9 if self.steps and self.steps[0][4] == () else 1,
                aliases={len(args) + k: len(outs) + k for k in range(len(moved))},
                name=name,
            )

        made = self.chain(call, *args, *moved)
        for step in self.steps:
            step[3](*made[: len(step[2])])
            made = made[len(step[2]) :]
        for (_, then), value in zip(self.carried, made, strict=True):
            then(value)


def split_kernel(role, meta, keep, arrived, a_out, a_keep, b_out, b_keep):
    half = keep.shape[1] // 2
    part = half // 2
    mine = meta[role]
    for slot, out in ((0, a_out), (1, a_keep)):
        out[...] = plus(keep[slot, 0:half, :], arrived[slot, 0:half, :])
    for slot in range(2):
        for out, which in ((b_out, 1 - mine), (b_keep, mine)):
            at = pl.ds(pl.multiple_of(half + which * part, 16), part)
            out[slot] = plus(keep[slot, at, :], arrived[slot, at, :])


def cross_kernel(role, meta, a, a_in, b, b_in, a_out, a_keep, b_out, b_keep):
    part = a.shape[0] // 2
    mine = meta[role]
    for out, which in ((a_out, 1 - mine), (a_keep, mine)):
        at = pl.ds(pl.multiple_of(which * part, 16), part)
        out[...] = plus(a[at, :], a_in[at, :])
    b_out[...] = plus(b[0], b_in[0])
    b_keep[...] = plus(b[1], b_in[1])


def merge_kernel(role, meta, a, a_in, b, b_in, out, keep):
    part = a.shape[0] // 2
    mine = meta[3 - role]
    for k, (left, right) in enumerate(((a, a_in), (b, b_in))):
        for made, which in ((out, 1 - mine), (keep, mine)):
            at = pl.ds(pl.multiple_of(which * part, 16), part)
            made[k] = plus(left[at, :], right[at, :])


def join_kernel(role, meta, own, other, out):
    part = own.shape[1]
    mine = meta[3 - role]
    for source, which in ((own, mine), (other, 1 - mine)):
        at = pl.ds(pl.multiple_of(which * part, 16), part)
        for k in range(2):
            out[k, at, :] = source[k]


def end_kernel(role, plan, meta, own, other, *refs):
    outs, whole = refs[:-1], refs[-1]
    part, width = own.shape[1:]
    mine = meta[role]
    for source, which in ((own, mine), (other, 1 - mine)):
        for k in range(2):
            at = pl.ds(pl.multiple_of((2 * k + which) * part, 16), part)
            whole[at, :] = source[k]
    row = 0
    for out, pieces in zip(outs, plan, strict=True):
        for at, rows in pieces:
            out[:, at * width : (at + 1) * width] = whole[row : row + rows, :].astype(F32)
            row += rows


class Sum:
    def __init__(self, keep, role):
        self.height, self.width = keep.shape[1:]
        self.keep, self.role = keep, role
        self.next = self.split
        self.bit = 2

    def of(self, body):
        return functools.partial(body, self.role)

    def core(self, send):
        self.arrived = swap(send, "seq", 1)

    def split(self, beat):
        height, width = self.height, self.width
        half, part = shape((height // 2, width)), shape((2, height // 4, width))

        def then(a_out, a, b_out, b):
            self.a, self.b = a, b
            self.a_in, self.b_in = swap(a_out, "seq", 2), swap(b_out, "dp", self.role)
            self.next = self.cross

        beat.add(self.of(split_kernel), [self.keep, self.arrived], [half, half, part, part], then)

    def cross(self, beat):
        part = shape((self.height // 4, self.width))

        def then(a_out, a, b_out, b):
            self.a, self.b = a, b
            self.a_in, self.b_in = swap(a_out, "dp", self.role), swap(b_out, "seq", 2)
            self.next = self.merge

        beat.add(self.of(cross_kernel), [self.a, self.a_in, self.b, self.b_in], [part] * 4, then)

    def merge(self, beat):
        part = shape((2, self.height // 8, self.width))

        def then(out, keep):
            self.keep = keep
            self.arrived = swap(out, "dp", 3 - self.role)
            self.next = self.more

        beat.add(self.of(merge_kernel), [self.a, self.a_in, self.b, self.b_in], [part] * 2, then)

    def more(self, beat):
        def then(total):
            self.keep = total
            self.bit *= 2
            last = self.bit >= lax.axis_size("dp")
            self.arrived = swap(total, "dp", 3 - self.role if last else self.bit)
            self.next = self.join if last else self.more

        beat.add(add_kernel, [self.keep, self.arrived], [shape(self.keep.shape)], then)

    def join(self, beat):
        def then(whole):
            self.keep = whole
            self.arrived = swap(whole, "dp", self.role)
            self.next = None

        whole = shape((2, self.height // 4, self.width))
        beat.add(self.of(join_kernel), [self.keep, self.arrived], [whole], then)

    def hold(self, arrived):
        self.arrived = arrived

    def end(self, beat, plan):
        width = self.width
        outs = [shape((pieces[0][1], width * len(pieces)), F32) for pieces in plan]

        def then(*made):
            self.made = made

        beat.add(
            functools.partial(end_kernel, self.role, plan),
            [self.keep, self.arrived],
            outs,
            then,
            [pltpu.VMEM((self.height, width), BF)],
        )


class Chain:
    def __init__(self):
        self.last = ()

    def __call__(self, made, *args):
        outs, mark = made(self.last, *args)
        self.last = (mark,)
        return outs


def shards(
    chars,
    window_mask,
    micro_batch,
    mol_grad,
    query_weight,
    query_bias,
    key_weight,
    value_weight,
    value_bias,
    output_weight,
    output_bias,
    first_gain,
    first_shift,
    inner_weight,
    inner_bias,
    outer_weight,
    outer_bias,
    second_gain,
    second_shift,
    conv_weight,
    conv_bias,
    third_gain,
    third_shift,
):
    rows, block, width = chars.shape
    count = rows * block
    place = lax.axis_index("seq").astype(jnp.int32)
    group = lax.axis_index("dp").astype(jnp.int32)
    meta = jnp.stack([place, group % 2, group // 2 % 2])
    size = lax.axis_size("seq")
    forward_pairs = [(i, i + 1) for i in range(size - 1)]
    backward_pairs = [(i + 1, i) for i in range(size - 1)]
    low = lax.ppermute(chars[:, block - WIN :], "seq", forward_pairs)
    high = lax.ppermute(chars[:, :WIN], "seq", backward_pairs)
    vectors = (
        query_bias,
        value_bias,
        output_bias,
        first_gain,
        first_shift,
        outer_bias,
        second_gain,
        second_shift,
        conv_bias,
        third_gain,
        third_shift,
        inner_bias,
    )
    tokens = chars.reshape(count, width)
    chain = Chain()
    q, k, v, vecs = chain(project, tokens, vectors, query_weight, key_weight, value_weight)
    kv, probs, mixed, n1, inv1, low1, slope, hidden, mol, go, sums3, send_c, keep_c = chain(
        forward,
        meta,
        window_mask,
        micro_batch,
        vecs,
        tokens,
        low,
        high,
        q,
        k,
        v,
        key_weight,
        value_weight,
        output_weight,
        inner_weight,
        outer_weight,
        conv_weight,
        mol_grad.reshape(-1, width),
    )
    molecules = mol.reshape(mol_grad.shape)
    conv = Sum(keep_c, 2)
    conv.core(send_c)
    send_u, keep_u = chain(outer_grad, meta, go, hidden)
    outer = Sum(keep_u, 2)

    def beat(name, chunks, carried=(), ends=()):
        made = Beat(chain, meta)
        for chunk in chunks:
            chunk.next(made)
        for chunk, plan in ends:
            chunk.end(made, plan)
        for value, then in carried:
            made.carry(value, then)
        made.emit(name)

    beat("beat1", [conv], [(send_u, outer.core)])
    common = (meta, vecs, go, slope, outer_weight, inner_weight, low1)
    send_i, keep_i, isum_a, acc = chain(inner_back, (0, 1), *common)
    beat("beat2", [conv, outer])
    send_i, keep_i, isum_b, gb, gm, sums1 = chain(
        inner_back,
        (2, 3),
        *common,
        acc,
        n1,
        inv1,
        output_weight,
        mixed,
        send_i,
        keep_i,
    )
    inner = Sum(keep_i, 1)
    beat("beat3", [conv, outer], [(send_i, inner.core)])
    beat("beat3i", [inner])
    grads = ()
    for r in range(rows):
        grads = chain(attention_back, q, kv, probs, gm, rows, r, tuple(grads))
        beat("beat%d" % (4 + r), [conv, outer, inner])
    dq, dk, dv, sums_a = grads
    send_p, keep_p = chain(
        project_grad, meta, dq, chars, dk, low, high, dv, sums_a, sums1, sums3, isum_a, isum_b
    )
    proj = Sum(keep_p, 1)
    beside = {}

    def from_prev(value):
        beside["low"] = lax.ppermute(value, "seq", forward_pairs)

    def from_next(value):
        beside["high"] = lax.ppermute(value, "seq", backward_pairs)

    quarter = width // 4
    wide = [[(j, quarter) for j in range(4)]]
    holds = lambda *chunks: [(chunk.arrived, chunk.hold) for chunk in chunks]
    beat("tail0", [conv, outer, inner], [(send_p, proj.core)])
    beat("tail1", [proj])
    grad_low, grad_high = chain(halo_grad, dk, dv, key_weight, value_weight)
    beat("tail2", [proj, inner], [(grad_high, from_prev), (grad_low, from_next)])
    beat("tail3", [proj, outer, inner], holds(conv))
    beat("tail4", [proj])
    grad_chars = chain(
        chars_grad,
        gb,
        dq,
        dk,
        dv,
        beside["low"],
        beside["high"],
        query_weight,
        key_weight,
        value_weight,
    )
    while proj.next != proj.join:
        beat("tail_more", [chunk for chunk in (proj, conv, outer, inner) if chunk.next == chunk.more])
    for chunk in (conv, outer, inner):
        while chunk.next is not None:
            beat("tail_rest", [chunk])
    beat("tail6", [proj], holds(outer, inner))
    beat("ends0", [], (), [(outer, wide), (inner, [[(0, width)], [(0, quarter)]])])
    beat("ends1", [], (), [(conv, wide)])
    beat("tail7", [], (), [(proj, [[(0, quarter)]] * 3 + [[(0, 16)]])])
    (full_c,), (full_u,) = conv.made, outer.made
    full_i, full_o = inner.made
    full_q, full_k, full_v, small = proj.made
    vec_of = lambda i: small[i, :quarter]
    return (
        molecules,
        grad_chars,
        full_q.T,
        vec_of(0),
        full_k.T,
        full_v.T,
        vec_of(1),
        full_o.T,
        vec_of(2),
        vec_of(3),
        vec_of(4),
        full_i,
        small[11:15, :quarter].reshape(-1),
        full_u.T,
        vec_of(5),
        vec_of(6),
        vec_of(7),
        full_c.T,
        vec_of(8),
        vec_of(9),
        vec_of(10),
    )


def solution(mesh):
    split = P("dp", "seq", None)
    placed = (split, P("dp", None), P("dp"), split) + (P(),) * 19
    by_column, by_place = P(None, "seq"), P("seq")
    outs = (
        split,
        split,
        by_column,
        by_place,
        by_column,
        by_column,
        by_place,
        by_column,
        by_place,
        by_place,
        by_place,
        by_column,
        by_place,
        by_column,
        by_place,
        by_place,
        by_place,
        by_column,
        by_place,
        by_place,
        by_place,
    )
    return jax.shard_map(shards, mesh=mesh, in_specs=placed, out_specs=outs, check_vma=False)
```

```python
import functools

import jax
import jax.numpy as jnp
from jax import lax
from jax.experimental import pallas as pl
from jax.experimental.pallas import tpu as pltpu
from jax.sharding import PartitionSpec as P

HEADS = 12
HEAD_DIM = 64
WIN = 128
DOWN = 4
MICRO = 2
EPSILON = 1e-06
NEG_FILL = -1e30
GELU_A = 0.7978845608028654
GELU_B = 0.044715
BF = jnp.bfloat16
F32 = jnp.float32
LANES = 128
MIB = 1 << 20

NN = (((1,), (0,)), ((), ()))
NT = (((1,), (1,)), ((), ()))
TN = (((0,), (0,)), ((), ()))

(V_QB, V_VB, V_OB, V_G1, V_S1, V_OUTB, V_G2, V_S2, V_CB, V_G3, V_S3, V_IB) = range(12)


def dot(left, right, dims=NN):
    return lax.dot_general(left, right, dims, preferred_element_type=F32)


def gelu_both(u):
    square = u * u
    t = jnp.tanh(u * (GELU_A + (GELU_A * GELU_B) * square))
    half = 0.5 + 0.5 * t
    value = u * half
    slope = half + value * (1.0 - t) * (GELU_A + (3.0 * GELU_A * GELU_B) * square)
    return value, slope


def layer_stats(u):
    center = u - jnp.mean(u, axis=-1, keepdims=True)
    inv_dev = lax.rsqrt(jnp.mean(center * center, axis=-1, keepdims=True) + EPSILON)
    return center * inv_dev, inv_dev


def norm_back(grad_out, normal, inv_dev, gain_vec):
    scaled = grad_out * gain_vec
    return inv_dev * (
        scaled
        - jnp.mean(scaled, axis=-1, keepdims=True)
        - normal * jnp.mean(scaled * normal, axis=-1, keepdims=True)
    )


def col_sum(value):
    return jnp.sum(value, axis=0, keepdims=True)


def params(mib=56, **more):
    return pltpu.CompilerParams(vmem_limit_bytes=mib * MIB, **more)


def cost(flops, nbytes):
    return pl.CostEstimate(flops=int(flops), bytes_accessed=int(nbytes), transcendentals=0)


def spec_any():
    return pl.BlockSpec(memory_space=pl.ANY)


def spec_hbm():
    return pl.BlockSpec(memory_space=pltpu.HBM)


def spec_smem():
    return pl.BlockSpec(memory_space=pltpu.SMEM)


def spec_vmem():
    return pl.BlockSpec(memory_space=pltpu.VMEM)


def shape(dims, dtype=BF):
    return jax.ShapeDtypeStruct(tuple(dims), dtype)


def run(body, deps, args, out_shape, in_specs, out_specs, scratch=(), grid=(), prefetch=0, mib=56, flops=10**12, nbytes=10**6, name=None, aliases=None):
    given = len(args)
    single = not isinstance(out_shape, (list, tuple))
    outs = [out_shape] if single else list(out_shape)
    specs = [out_specs] if single else list(out_specs)
    mark = pl.BlockSpec((8, LANES), lambda *_: (0, 0)) if grid else spec_vmem()

    def wrapped(*refs):
        rest = refs[given + len(deps) :]
        rest[len(outs)][...] = jnp.zeros((8, LANES), F32)
        body(*refs[:given], *rest[: len(outs)], *rest[len(outs) + 1 :])

    made = pl.pallas_call(
        wrapped,
        grid_spec=pltpu.PrefetchScalarGridSpec(
            num_scalar_prefetch=prefetch,
            grid=grid,
            in_specs=list(in_specs) + [spec_any()] * len(deps),
            out_specs=specs + [mark],
            scratch_shapes=list(scratch),
        ),
        out_shape=outs + [shape((8, LANES), F32)],
        compiler_params=pltpu.CompilerParams(vmem_limit_bytes=mib * MIB),
        cost_estimate=cost(flops, nbytes),
        input_output_aliases=aliases or {},
        name=name,
    )(*args, *deps)
    return made[0] if single else made[:-1], made[-1]


def head_masks():
    lane = lax.broadcasted_iota(jnp.int32, (1, LANES), 1)
    first = jnp.where(lane < HEAD_DIM, 1.0, 0.0).astype(BF)
    return first, (1.0 - first.astype(F32)).astype(BF)


def twice(block, masks):
    return jnp.concatenate([block * masks[0], block * masks[1]], axis=0)


def slot_of(quarter, place):
    same_x = (quarter // 2 == place // 2).astype(jnp.int32)
    same_core = (quarter % 2 == place % 2).astype(jnp.int32)
    return 2 * same_core + same_x


def project_kernel(names, x_ref, *refs):
    vectors, (wq_ref, wk_ref, wv_ref, q_ref, k_ref, v_ref, vec_ref) = refs[:names], refs[names:]
    width = x_ref.shape[1]
    part = wq_ref.shape[1]
    step = pl.program_id(0)

    @pl.when(step == 0)
    def _():
        row = 0
        for ref in vectors:
            value = ref[...].astype(F32)
            for k in range(value.shape[0] // width):
                vec_ref[row : row + 1, :] = value[k * width : (k + 1) * width].reshape(1, width)
                row += 1
        vec_ref[row:, :] = jnp.zeros((vec_ref.shape[0] - row, width), F32)

    x = x_ref[...]
    at = pl.ds(pl.multiple_of(step * part, part), part)
    queries = (dot(x, wq_ref[...]) + vec_ref[V_QB : V_QB + 1, at]).astype(BF)
    q_ref[...] = queries * jnp.asarray(HEAD_DIM**-0.5, BF)
    k_ref[...] = dot(x, wk_ref[...]).astype(BF)
    v_ref[...] = (dot(x, wv_ref[...]) + vec_ref[V_VB : V_VB + 1, at]).astype(BF)


def project(deps, tokens, vectors, wq, wk, wv):
    count, width = tokens.shape
    part = 256
    column = pl.BlockSpec((width, part), lambda i: (0, i))
    out = pl.BlockSpec((count, part), lambda i: (0, i))
    height = rounded_up(sum(v.shape[0] for v in vectors) // width, 8)
    return run(
        functools.partial(project_kernel, len(vectors)),
        deps,
        (tokens, *vectors, wq, wk, wv),
        [shape((count, width))] * 3 + [shape((height, width), F32)],
        [pl.BlockSpec((count, width), lambda i: (0, 0))]
        + [pl.BlockSpec(v.shape, lambda i: (0,)) for v in vectors]
        + [column] * 3,
        [out] * 3 + [pl.BlockSpec((height, width), lambda i: (0, 0))],
        grid=(width // part,),
        mib=60,
        name="project",
    )


def forward_kernel(
    rows,
    wins,
    windows_all,
    meta,
    wmask,
    mbatch,
    vec,
    chars_h,
    low_h,
    high_h,
    q_h,
    k_h,
    v_h,
    wk_h,
    wv_h,
    wo_h,
    wi_h,
    wout_h,
    wc_h,
    mg_h,
    kv_o,
    pt_o,
    mixed_o,
    n1_o,
    inv1_o,
    low1_o,
    slope_o,
    hidden_o,
    mol_o,
    go_o,
    sums_o,
    send_o,
    keep_o,
    q,
    kv,
    halo,
    wkv,
    wo,
    chars,
    wi,
    wout,
    wc,
    mg,
    probs,
    mixed,
    acc,
    strips,
    low1,
    n1,
    inv1,
    slope,
    hidden,
    n2,
    inv2,
    merged,
    mol,
    sem_in,
    sem_p,
    sem_h,
    sem_out,
):
    place = meta[0]
    block = wins * WIN
    width = chars.shape[-1]
    count = rows * block
    pairs = width // LANES
    parts = wi.shape[1] // width

    def copy_in(index, src, dst):
        made = pltpu.make_async_copy(src, dst, sem_in.at[index])
        made.start()
        return made

    halo_in = [
        copy_in(0, low_h, halo.at[0]),
        copy_in(1, high_h, halo.at[1]),
        copy_in(2, wk_h, wkv.at[0]),
        copy_in(3, wv_h, wkv.at[1]),
    ]
    qkv_in = [copy_in(4, q_h, q)]
    for r in range(rows):
        qkv_in.append(
            copy_in(5 + 2 * r, k_h.at[pl.ds(r * block, block)], kv.at[r, pl.ds(WIN, block)])
        )
        qkv_in.append(
            copy_in(
                6 + 2 * r, v_h.at[pl.ds(r * block, block)], kv.at[rows + r, pl.ds(WIN, block)]
            )
        )
    base = 5 + 2 * rows

    def copy_out(index, src, dst):
        made = pltpu.make_async_copy(src, dst, sem_out.at[index])
        made.start()
        return made

    for made in halo_in:
        made.wait()
    beside = halo[...].reshape(2 * rows * WIN, width)
    keys = dot(beside, wkv[0]).astype(BF)
    values = (dot(beside, wkv[1]) + vec[V_VB : V_VB + 1, :]).astype(BF)
    for side in range(2):
        start = side * (block + WIN)
        for r in range(rows):
            at = (side * rows + r) * WIN
            kv[r, pl.ds(start, WIN), :] = keys[at : at + WIN]
            kv[rows + r, pl.ds(start, WIN), :] = values[at : at + WIN]
    for made in qkv_in:
        made.wait()
    wo_in = copy_in(base, wo_h, wo)
    chars_in = copy_in(base + 1, chars_h, chars)
    wi_in = copy_in(base + 2, wi_h, wi)
    wout_in = copy_in(base + 3, wout_h, wout)
    kv_out = copy_out(0, kv, kv_o)

    masks = head_masks()

    def pair_step(it, carry):
        r = it // pairs
        pair = it % pairs
        slot = it % 2
        lanes = pl.ds(pl.multiple_of(pair * LANES, LANES), LANES)

        @pl.when(it >= 2)
        def _():
            pltpu.make_async_copy(probs.at[slot], pt_o.at[it - 2], sem_p.at[slot]).wait()

        every = []
        for w in range(wins):
            queries = twice(q[pl.ds(r * block + w * WIN, WIN), lanes], masks)
            every.append(dot(kv[r, pl.ds(w * WIN, 3 * WIN), lanes], queries, NT))
        chances = []
        for w, scores in enumerate(every):
            at = place * wins + w
            low_ok = (at >= 1) & (wmask[r, jnp.maximum(at - 1, 0)] > 0)
            high_ok = (at + 1 < windows_all) & (wmask[r, jnp.minimum(at + 1, windows_all - 1)] > 0)
            scores = jnp.concatenate(
                [
                    scores[0:WIN] + jnp.where(low_ok, 0.0, NEG_FILL),
                    scores[WIN : 2 * WIN],
                    scores[2 * WIN :] + jnp.where(high_ok, 0.0, NEG_FILL),
                ],
                axis=0,
            )
            shifted = jnp.exp(scores - jnp.max(scores, axis=0, keepdims=True))
            total = jnp.sum(shifted, axis=0, keepdims=True)
            chances.append((shifted * (1.0 / total)).astype(BF))
            probs[slot, w] = chances[w]
        for w, chance in enumerate(chances):
            stacked = jnp.concatenate([chance[:, :LANES], chance[:, LANES:]], axis=0)
            values_win = twice(kv[rows + r, pl.ds(w * WIN, 3 * WIN), lanes], masks)
            mixed[pl.ds(r * block + w * WIN, WIN), lanes] = dot(stacked, values_win, TN).astype(BF)
        pltpu.make_async_copy(probs.at[slot], pt_o.at[it], sem_p.at[slot]).start()
        return carry

    steps = rows * pairs
    lax.fori_loop(0, steps, pair_step, 0)
    mixed_out = copy_out(1, mixed, mixed_o)

    wo_in.wait()
    chars_in.wait()
    wc_in = copy_in(base + 4, wc_h, wc)
    mg_in = copy_in(base + 5, mg_h, mg)
    piece = 256

    pieces = [pl.ds(i * piece, piece) for i in range(count // piece)]
    branches = [dot(mixed[at, :], wo[...]) for at in pieces]
    for at, branch in zip(pieces, branches, strict=True):
        u = branch + vec[V_OB : V_OB + 1, :] + chars[at, :].astype(F32)
        normal, inv = layer_stats(u)
        first = normal * vec[V_G1 : V_G1 + 1, :] + vec[V_S1 : V_S1 + 1, :]
        n1[at, :] = normal.astype(BF)
        inv1[at, :] = inv
        low1[at, :] = first.astype(BF)
        acc[at, :] = first + vec[V_OUTB : V_OUTB + 1, :]
    outs = [mixed_out, copy_out(2, n1, n1_o), copy_out(3, inv1, inv1_o), copy_out(4, low1, low1_o)]

    wi_in.wait()
    wout_in.wait()

    def ffn_step(c, carry):
        slot = c % 2
        columns = pl.ds(pl.multiple_of(c * width, width), width)

        @pl.when(c >= 2)
        def _():
            pltpu.make_async_copy(slope.at[slot], slope_o.at[c - 2], sem_h.at[slot]).wait()
            pltpu.make_async_copy(hidden.at[slot], hidden_o.at[c - 2], sem_h.at[2 + slot]).wait()

        bias = vec[pl.ds(V_IB + c, 1), :]
        half = count // 2
        parts_of = [pl.ds(k * half, half) for k in range(2)]
        upper, lower = (dot(low1[at, :], wi[:, columns]) + bias for at in parts_of)
        for at, u in zip(parts_of, (upper, lower), strict=True):
            value, steep = gelu_both(u)
            slope[slot, at, :] = steep.astype(BF)
            h = value.astype(BF)
            hidden[slot, at, :] = h
            acc[at, :] += dot(h, wout[columns, :])
        pltpu.make_async_copy(slope.at[slot], slope_o.at[c], sem_h.at[slot]).start()
        pltpu.make_async_copy(hidden.at[slot], hidden_o.at[c], sem_h.at[2 + slot]).start()
        return carry

    lax.fori_loop(0, parts, ffn_step, 0)

    def second_step(i, carry):
        at = pl.ds(pl.multiple_of(i * piece, piece), piece)
        normal, inv = layer_stats(acc[at, :])
        n2[at, :] = normal.astype(BF)
        inv2[at, :] = inv
        second = normal * vec[V_G2 : V_G2 + 1, :] + vec[V_S2 : V_S2 + 1, :]
        for t in range(pairs):
            strips[t, at, :] = second[:, t * LANES : (t + 1) * LANES]
        return carry

    lax.fori_loop(0, count // piece, second_step, 0, unroll=True)

    wc_in.wait()
    mg_in.wait()
    mols = count // DOWN
    conv = jnp.zeros((mols, width), F32) + vec[V_CB : V_CB + 1, :]
    for i in range(DOWN):
        for t in range(pairs):
            merged[i, :, t * LANES : (t + 1) * LANES] = strips[
                t, pl.ds(i, mols, stride=DOWN), :
            ].astype(BF)
        part = merged[i]
        conv = conv + dot(part, wc[pl.ds(i * width, width), :])
    value, steep = gelu_both(conv)
    normal, inv = layer_stats(value)
    per_win = WIN // DOWN
    which = lax.broadcasted_iota(jnp.int32, (mols, 1), 0) // per_win
    live = jnp.zeros((mols, 1), F32)
    total = jnp.ones((mols, 1), F32)
    lengths = []
    for r in range(rows):
        length = wmask[r, 0]
        for w in range(1, windows_all):
            length = length + wmask[r, w]
        lengths.append(length)
    for r in range(rows):
        same = jnp.int32(0)
        for other in range(rows):
            same = same + jnp.where(mbatch[other] == mbatch[r], lengths[other], 0)
        same = (same * per_win).astype(F32)
        for w in range(wins):
            here = which == r * wins + w
            live = jnp.where(here, wmask[r, place * wins + w].astype(F32), live)
            total = jnp.where(here, same, total)
    weight = (rows // MICRO * windows_all * per_win) / total
    gain = vec[V_G3 : V_G3 + 1, :]
    mol[...] = ((normal * gain + vec[V_S3 : V_S3 + 1, :]) * live).astype(BF)
    outs.append(copy_out(5, mol, mol_o))
    grad_mol = mg[...].astype(F32) * (weight * live)
    grad_conv = (steep * norm_back(grad_mol, normal, inv, gain)).astype(BF)
    sums_o[0:1, :] = col_sum(grad_mol * normal)
    sums_o[1:2, :] = col_sum(grad_mol)
    sums_o[2:3, :] = col_sum(grad_conv.astype(F32))
    sums_o[3:, :] = jnp.zeros((sums_o.shape[0] - 3, width), F32)

    kv_out.wait()
    across = grad_conv.T
    quarter = width // 4
    for i in range(DOWN):
        made = dot(across, merged[i]).astype(BF)
        for number in range(4):
            kv[slot_of(jnp.int32(number), place), pl.ds(i * quarter, quarter), :] = made[
                number * quarter : (number + 1) * quarter
            ]
    outs.append(copy_out(6, kv.at[pl.ds(0, 2)], send_o))
    outs.append(copy_out(7, kv.at[pl.ds(2, 2)], keep_o))

    for i in range(DOWN):
        made = dot(grad_conv, wc[pl.ds(i * width, width), :], NT)
        for t in range(pairs):
            strips[t, pl.ds(i, mols, stride=DOWN), :] = made[:, t * LANES : (t + 1) * LANES]
    gain = vec[V_G2 : V_G2 + 1, :]

    def back_step(i, carry):
        at = pl.ds(pl.multiple_of(i * piece, piece), piece)
        grad = jnp.concatenate([strips[t, at, :] for t in range(pairs)], axis=1)
        normal = n2[at, :].astype(F32)
        made = norm_back(grad, normal, inv2[at, :], gain).astype(BF)
        n2[at, :] = made
        sums_o[3:4, :] += col_sum(grad * normal)
        sums_o[4:5, :] += col_sum(grad)
        sums_o[5:6, :] += col_sum(made.astype(F32))
        return carry

    lax.fori_loop(0, count // piece, back_step, 0, unroll=True)
    outs.append(copy_out(8, n2, go_o))

    for made in outs:
        made.wait()
    for it in range(max(0, steps - 2), steps):
        pltpu.make_async_copy(probs.at[it % 2], pt_o.at[it], sem_p.at[it % 2]).wait()
    for c in range(max(0, parts - 2), parts):
        pltpu.make_async_copy(slope.at[c % 2], slope_o.at[c], sem_h.at[c % 2]).wait()
        pltpu.make_async_copy(hidden.at[c % 2], hidden_o.at[c], sem_h.at[2 + c % 2]).wait()


def forward(deps, meta, wmask, mbatch, vecs, chars, low, high, q, k, v, wk, wv, wo, wi, wout, wc, mg):
    rows = wmask.shape[0]
    windows_all = wmask.shape[1]
    count, width = q.shape
    block = count // rows
    wins = block // WIN
    ff = wi.shape[1]
    parts = ff // width
    mols = count // DOWN
    pairs = width // LANES
    ext = block + 2 * WIN
    outs = [
        shape((2 * rows, ext, width)),
        shape((rows * pairs, wins, 3 * WIN, 2 * LANES)),
        shape((count, width)),
        shape((count, width)),
        shape((count, 1), F32),
        shape((count, width)),
        shape((parts, count, width)),
        shape((parts, count, width)),
        shape((mols, width)),
        shape((count, width)),
        shape((8, width), F32),
        shape((2, DOWN * width // 4, width)),
        shape((2, DOWN * width // 4, width)),
    ]
    out_specs = [spec_any()] * len(outs)
    out_specs[10] = spec_vmem()
    return run(
        functools.partial(forward_kernel, rows, wins, windows_all),
        deps,
        (meta, wmask, mbatch, vecs, chars, low, high, q, k, v, wk, wv, wo, wi, wout, wc, mg),
        outs,
        [spec_smem()] * 3 + [spec_vmem()] + [spec_any()] * 13,
        out_specs,
        scratch=[
            pltpu.VMEM((count, width), BF),
            pltpu.VMEM((2 * rows, ext, width), BF),
            pltpu.VMEM((2, rows, WIN, width), BF),
            pltpu.VMEM((2, width, width), BF),
            pltpu.VMEM((width, width), BF),
            pltpu.VMEM((count, width), BF),
            pltpu.VMEM((width, ff), BF),
            pltpu.VMEM((ff, width), BF),
            pltpu.VMEM((DOWN * width, width), BF),
            pltpu.VMEM((mols, width), BF),
            pltpu.VMEM((2, wins, 3 * WIN, 2 * LANES), BF),
            pltpu.VMEM((count, width), BF),
            pltpu.VMEM((count, width), F32),
            pltpu.VMEM((pairs, count, LANES), F32),
            pltpu.VMEM((count, width), BF),
            pltpu.VMEM((count, width), BF),
            pltpu.VMEM((count, 1), F32),
            pltpu.VMEM((2, count, width), BF),
            pltpu.VMEM((2, count, width), BF),
            pltpu.VMEM((count, width), BF),
            pltpu.VMEM((count, 1), F32),
            pltpu.VMEM((DOWN, mols, width), BF),
            pltpu.VMEM((mols, width), BF),
            pltpu.SemaphoreType.DMA((11 + 2 * rows,)),
            pltpu.SemaphoreType.DMA((2,)),
            pltpu.SemaphoreType.DMA((4,)),
            pltpu.SemaphoreType.DMA((9,)),
        ],
        mib=60,
        name="forward",
    )


def outer_grad_kernel(meta, go, hidden, send, keep, across):
    place = meta[0]
    width = go.shape[1]
    quarter = width // 4

    @pl.when(pl.program_id(0) == 0)
    def _():
        turned = go[...].T
        for number in range(4):
            across[slot_of(jnp.int32(number), place)] = turned[
                number * quarter : (number + 1) * quarter
            ]

    left = across[...].reshape(width, go.shape[0])
    made = dot(left, hidden[0]).astype(BF)
    for j in range(2):
        send[j] = made[j * quarter : (j + 1) * quarter]
        keep[j] = made[(2 + j) * quarter : (3 + j) * quarter]


def outer_grad(deps, meta, go, hidden):
    parts, count, width = hidden.shape
    quarter = width // 4
    out = pl.BlockSpec((2, quarter, width), lambda i, m: (0, i, 0))
    return run(
        outer_grad_kernel,
        deps,
        (meta, go, hidden),
        [shape((2, parts * quarter, width))] * 2,
        [
            pl.BlockSpec((count, width), lambda i, m: (0, 0)),
            pl.BlockSpec((1, count, width), lambda i, m: (i, 0, 0)),
        ],
        [out] * 2,
        scratch=[pltpu.VMEM((4, quarter, count), BF)],
        grid=(parts,),
        prefetch=1,
        name="outer_grad",
    )


def slot_copies(src, send, keep, slot, at, sem):
    out = pltpu.make_async_copy(src, send.at[jnp.minimum(slot, 1), at], sem)
    own = pltpu.make_async_copy(src, keep.at[jnp.maximum(slot - 2, 0), at], sem)

    def start():
        @pl.when(slot < 2)
        def _():
            out.start()

        @pl.when(slot >= 2)
        def _():
            own.start()

    return start, out.wait


def inner_back_kernel(first, chosen, meta, vec, go_h, slope_h, wout_h, wi_h, low1_h, *refs):
    if first:
        ins, refs = (), refs
    else:
        ins, refs = refs[:5], refs[7:]
    send, keep, isum, *refs = refs
    if first:
        acc_o, *refs = refs
    else:
        gb_o, gm_o, sums, *refs = refs
    go, slope, wout, wi, low1, acc, grads, *refs = refs
    if not first:
        n1, inv1, wo, mixed, gb, gm, rest, *refs = refs
    sem_in, sem_out = refs
    count, width = go.shape
    place = meta[0]
    quarter = width // 4
    waits = []

    def bring(src, dst):
        made = pltpu.make_async_copy(src, dst, sem_in.at[len(waits)])
        made.start()
        waits.append(made)
        return made

    go_in = bring(go_h, go)
    parts_in = []
    for k, c in enumerate(chosen):
        at = pl.ds(c * width, width)
        parts_in.append(
            [
                bring(wout_h.at[at], wout.at[k]),
                bring(slope_h.at[c], slope.at[k]),
                bring(wi_h.at[:, at], wi.at[k]),
            ]
        )
        if k == 0:
            low1_in = bring(low1_h, low1)
            acc_in = None if first else bring(ins[0], acc)
    if not first:
        late = [bring(src, dst) for src, dst in zip(ins[1:], (n1, inv1, wo, mixed), strict=True)]
    go_in.wait()
    half = count // 2
    halves = [slice(k * half, (k + 1) * half) for k in range(2)]
    outs = []
    across = None
    for k, c in enumerate(chosen):
        parts_in[k][0].wait()
        steep = [dot(go[at, :], wout[k], NT) for at in halves]
        if across is None:
            low1_in.wait()
            across = low1[...].T
        parts_in[k][1].wait()
        parts_in[k][2].wait()
        if k == 0 and not first:
            acc_in.wait()
        low = []
        for at, grad in zip(halves, steep, strict=True):
            low.append((slope[k, at, :].astype(F32) * grad).astype(BF))
            added = dot(low[-1], wi[k], NT)
            if first and k == 0:
                acc[at, :] = go[at, :].astype(F32) + added
            else:
                acc[at, :] += added
        made = jnp.concatenate(low, axis=0)
        isum[k] = jnp.broadcast_to(col_sum(made.astype(F32)), (8, width))
        grads[k] = dot(across, made).astype(BF)
        slot = slot_of(jnp.int32(c), place)
        start, wait = slot_copies(
            grads.at[k], send, keep, slot, pl.ds(0, width), sem_out.at[len(outs)]
        )
        start()
        outs.append(wait)

    def leave(src, dst):
        made = pltpu.make_async_copy(src, dst, sem_out.at[len(outs)])
        made.start()
        outs.append(made.wait)

    if first:
        leave(acc, acc_o)
    else:
        for made in late:
            made.wait()
        gain = vec[V_G1 : V_G1 + 1, :]
        piece = 256
        sums[...] = jnp.zeros(sums.shape, F32)
        lows = []
        for j in range(count // piece):
            at = slice(j * piece, (j + 1) * piece)
            grad = acc[at, :]
            normal = n1[at, :].astype(F32)
            lows.append(norm_back(grad, normal, inv1[at, :], gain).astype(BF))
            gb[at, :] = lows[-1]
            sums[0:1, :] += col_sum(grad * normal)
            sums[1:2, :] += col_sum(grad)
            sums[2:3, :] += col_sum(lows[-1].astype(F32))
        leave(gb, gb_o)
        for j in range(count // piece):
            gm[j * piece : (j + 1) * piece, :] = dot(lows[j], wo[...], NT).astype(BF)
        leave(gm, gm_o)
        rest[...] = jnp.zeros(rest.shape, BF)
        extra = rest.shape[1] - quarter
        made = dot(gb[...], mixed[...], TN).astype(BF)
        for number in range(4):
            rest[number, 0:quarter, :] = made[number * quarter : (number + 1) * quarter]
            slot = slot_of(jnp.int32(number), place)
            start, wait = slot_copies(
                rest.at[number],
                send,
                keep,
                slot,
                pl.ds(width, quarter + extra),
                sem_out.at[len(outs)],
            )
            start()
            outs.append(wait)
    for wait in outs:
        wait()


def rounded_up(value, unit):
    return -(-value // unit) * unit


def inner_back(deps, chosen, meta, vecs, go, slope, wout, wi, low1, *more):
    _, count, width = slope.shape
    first = not more
    quarter = width // 4
    height = rounded_up(width + quarter, 8 * 16)
    both = shape((2, height, width))
    outs = [both, both, shape((2, 8, width), F32)]
    out_specs = [spec_hbm(), spec_hbm(), spec_vmem()]
    scratch = [
        pltpu.VMEM((count, width), BF),
        pltpu.VMEM((2, count, width), BF),
        pltpu.VMEM((2, width, width), BF),
        pltpu.VMEM((2, width, width), BF),
        pltpu.VMEM((count, width), BF),
        pltpu.VMEM((count, width), F32),
        pltpu.VMEM((2, width, width), BF),
    ]
    if first:
        outs += [shape((count, width), F32)]
        out_specs += [spec_hbm()]
    else:
        outs += [shape((count, width)), shape((count, width)), shape((8, width), F32)]
        out_specs += [spec_hbm(), spec_hbm(), spec_vmem()]
        scratch += [
            pltpu.VMEM((count, width), BF),
            pltpu.VMEM((count, 1), F32),
            pltpu.VMEM((width, width), BF),
            pltpu.VMEM((count, width), BF),
            pltpu.VMEM((count, width), BF),
            pltpu.VMEM((count, width), BF),
            pltpu.VMEM((4, height - width, width), BF),
        ]
    scratch += [pltpu.SemaphoreType.DMA((13,)), pltpu.SemaphoreType.DMA((8,))]
    return run(
        functools.partial(inner_back_kernel, first, chosen),
        deps,
        (meta, vecs, go, slope, wout, wi, low1, *more),
        outs,
        [spec_smem(), spec_vmem()] + [spec_any()] * (5 + len(more)),
        out_specs,
        scratch=scratch,
        aliases={} if first else {12: 0, 13: 1},
        name="inner_back%d" % chosen[0],
    )


def attention_back_kernel(wins, q, k, v, probs, gm, dq, dk, dv, sums):
    masks = head_masks()
    here = [slice(w * WIN, (w + 1) * WIN) for w in range(wins)]
    span = [slice(w * WIN, (w + 3) * WIN) for w in range(wins)]
    grad_out = [twice(gm[0, at, :], masks) for at in here]
    queries = [twice(q[0, at, :], masks) for at in here]
    grad_probs = [dot(v[0, span[w], :], grad_out[w], NT) for w in range(wins)]
    grad_values = [dot(probs[0, w], grad_out[w]) for w in range(wins)]
    grad_scores = []
    for w in range(wins):
        chance = probs[0, w].astype(F32)
        product = chance * grad_probs[w]
        total = jnp.sum(product, axis=0, keepdims=True)
        grad_scores.append((product - chance * total).astype(BF))
    grad_keys = [dot(grad_scores[w], queries[w]) for w in range(wins)]
    q_sum = jnp.zeros((1, LANES), F32)
    for w in range(wins):
        made = grad_scores[w]
        stacked = jnp.concatenate([made[:, :LANES], made[:, LANES:]], axis=0)
        made = dot(stacked, twice(k[0, span[w], :], masks), TN) * HEAD_DIM**-0.5
        low = made.astype(BF)
        dq[0, here[w], :] = low
        q_sum = q_sum + col_sum(low.astype(F32))
    v_sum = jnp.zeros((1, LANES), F32)
    for parts, out in ((grad_keys, dk), (grad_values, dv)):
        for b in range(wins + 2):
            uses = [w for w in range(wins) if 0 <= b - w < 3]
            pieces = [parts[w][(b - w) * WIN : (b - w + 1) * WIN] for w in uses]
            made = sum(pieces[1:], pieces[0])
            out[0, b * WIN : (b + 1) * WIN, :] = made.astype(BF)
            if out is dv:
                v_sum = v_sum + col_sum(made)
    sums[0, 0:1, :] = q_sum
    sums[0, 1:2, :] = v_sum
    sums[0, 2:, :] = jnp.zeros((6, LANES), F32)


def attention_back(deps, q, kv, probs, gm, rows, row, before):
    count, width = q.shape
    block = count // rows
    wins = block // WIN
    ext = kv.shape[1]
    pairs = width // LANES
    own = pl.BlockSpec((1, block, LANES), lambda p: (row, 0, p))
    keys = pl.BlockSpec((1, ext, LANES), lambda p: (row, 0, p))
    values = pl.BlockSpec((1, ext, LANES), lambda p: (rows + row, 0, p))

    def body(q, k, v, probs, gm, *refs):
        attention_back_kernel(wins, q, k, v, probs, gm, *refs[len(before) :])

    return run(
        body,
        deps,
        (q.reshape(rows, block, width), kv, kv, probs, gm.reshape(rows, block, width), *before),
        [
            shape((rows, block, width)),
            shape((rows, ext, width)),
            shape((rows, ext, width)),
            shape((rows, 8, width), F32),
        ],
        [
            own,
            keys,
            values,
            pl.BlockSpec((1, wins, 3 * WIN, 2 * LANES), lambda p: (row * pairs + p, 0, 0, 0)),
            own,
        ]
        + [spec_any()] * len(before),
        [own, keys, keys, pl.BlockSpec((1, 8, LANES), lambda p: (row, 0, p))],
        grid=(pairs,),
        mib=56,
        aliases={5 + k: k for k in range(len(before))},
        name="attention_back%d" % row,
    )


VEC_ROWS = 64


def project_grad_kernel(
    meta,
    dq_h,
    chars_h,
    dk_h,
    low_h,
    high_h,
    dv_h,
    sums_a,
    sums1,
    sums3,
    isum_a,
    isum_b,
    send_o,
    keep_o,
    dq,
    dk,
    dv,
    ext,
    made_all,
    small,
    sem_in,
    sem_out,
):
    rows, full, width = dk.shape
    block = full - 2 * WIN
    count = rows * block
    place = meta[0]
    quarter = width // 4
    started = []
    pairs = [
        (dq_h, dq),
        (chars_h, ext.at[:, pl.ds(WIN, block)]),
        (dk_h, dk),
        (low_h, ext.at[:, pl.ds(0, WIN)]),
        (high_h, ext.at[:, pl.ds(WIN + block, WIN)]),
        (dv_h, dv),
    ]
    for k, (src, dst) in enumerate(pairs):
        started.append(pltpu.make_async_copy(src, dst, sem_in.at[k]))
        started[-1].start()
    leaving = []

    def leave(src, dst):
        leaving.append(pltpu.make_async_copy(src, dst, sem_out.at[len(leaving)]))
        leaving[-1].start()

    def put(index, made):
        at = pl.ds(index * quarter, quarter)
        for number in range(4):
            made_all[slot_of(jnp.int32(number), place), at, :] = made[
                number * quarter : (number + 1) * quarter
            ]
        leave(made_all.at[pl.ds(0, 2), at], send_o.at[:, at])
        leave(made_all.at[pl.ds(2, 2), at], keep_o.at[:, at])

    att = sums_a[0]
    for r in range(1, rows):
        att = att + sums_a[r]
    stack = [att[0:1], att[1:2], sums1[2:3], sums1[0:1], sums1[1:2], sums3[5:6]]
    stack += [sums3[3:4], sums3[4:5], sums3[2:3], sums3[0:1], sums3[1:2]]
    at = pl.ds(3 * quarter, VEC_ROWS)
    for number in range(4):
        mine = slice(number * quarter, (number + 1) * quarter)
        small[...] = jnp.zeros(small.shape, F32)
        for row, vector in enumerate(stack):
            small[row : row + 1, 0:quarter] = vector[:, mine]
        for j in range(4):
            small[len(stack) + j : len(stack) + j + 1, 0:quarter] = (isum_a, isum_b)[number // 2][
                number % 2, 0:1, j * quarter : (j + 1) * quarter
            ]
        made_all[slot_of(jnp.int32(number), place), at, :] = small[...].astype(BF)
    leave(made_all.at[pl.ds(0, 2), at], send_o.at[:, at])
    leave(made_all.at[pl.ds(2, 2), at], keep_o.at[:, at])

    started[0].wait()
    started[1].wait()
    own = ext[:, WIN : WIN + block, :].reshape(count, width)
    put(0, dot(dq[...].reshape(count, width), own, TN).astype(BF))
    started[2].wait()
    started[3].wait()
    started[4].wait()
    every = ext[...].reshape(rows * full, width)
    put(1, dot(dk[...].reshape(rows * full, width), every, TN).astype(BF))
    started[5].wait()
    put(2, dot(dv[...].reshape(rows * full, width), every, TN).astype(BF))
    for made in leaving:
        made.wait()


def project_grad(deps, meta, dq, chars, dk, low, high, dv, *sums):
    rows, full, width = dk.shape
    height = 3 * width // 4 + VEC_ROWS
    return run(
        project_grad_kernel,
        deps,
        (meta, dq, chars, dk, low, high, dv, *sums),
        [shape((2, height, width))] * 2,
        [spec_smem()] + [spec_any()] * 6 + [spec_vmem()] * len(sums),
        [spec_hbm()] * 2,
        scratch=[
            pltpu.VMEM(dq.shape, BF),
            pltpu.VMEM(dk.shape, BF),
            pltpu.VMEM(dk.shape, BF),
            pltpu.VMEM(dk.shape, BF),
            pltpu.VMEM((4, height, width), BF),
            pltpu.VMEM((VEC_ROWS, width), F32),
            pltpu.SemaphoreType.DMA((6,)),
            pltpu.SemaphoreType.DMA((8,)),
        ],
        name="project_grad",
    )


def halo_grad_kernel(dk_low, dv_low, dk_high, dv_high, wk, wv, low, high):
    rows, edge, width = low.shape
    for dk, dv, out in ((dk_low, dv_low, low), (dk_high, dv_high, high)):
        keys = dk[...].reshape(rows * edge, width)
        values = dv[...].reshape(rows * edge, width)
        made = dot(keys, wk[...], NT) + dot(values, wv[...], NT)
        out[...] = made.astype(BF).reshape(rows, edge, width)


def halo_grad(deps, dk, dv, wk, wv):
    rows, full, width = dk.shape
    edge = (rows, WIN, width)
    first = pl.BlockSpec(edge, lambda i: (0, 0, 0))
    last = pl.BlockSpec(edge, lambda i: (0, full // WIN - 1, 0))
    whole = pl.BlockSpec((width, width), lambda i: (0, 0))
    return run(
        halo_grad_kernel,
        deps,
        (dk, dv, dk, dv, wk, wv),
        [shape(edge)] * 2,
        [first, first, last, last, whole, whole],
        [first] * 2,
        grid=(1,),
        mib=24,
        name="halo_grad",
    )


def chars_grad_kernel(gb, dq, dk, dv, low, high, wq, wk, wv, out):
    _, block, width = dq.shape
    own = slice(WIN, WIN + block)
    made = gb[0].astype(F32)
    made = made + dot(dq[0], wq[...], NT)
    made = made + dot(dk[0, own, :], wk[...], NT)
    made = made + dot(dv[0, own, :], wv[...], NT)
    out[0, WIN : block - WIN, :] = made[WIN : block - WIN].astype(BF)
    out[0, 0:WIN, :] = (made[0:WIN] + low[0].astype(F32)).astype(BF)
    out[0, block - WIN :, :] = (made[block - WIN :] + high[0].astype(F32)).astype(BF)


def chars_grad(deps, gb, dq, dk, dv, low, high, wq, wk, wv):
    rows, block, width = dq.shape
    ext = dk.shape[1]
    row = lambda n: pl.BlockSpec((1, n, width), lambda r: (r, 0, 0))
    weight = pl.BlockSpec((width, width), lambda r: (0, 0))
    return run(
        chars_grad_kernel,
        deps,
        (gb.reshape(rows, block, width), dq, dk, dv, low, high, wq, wk, wv),
        shape((rows, block, width)),
        [row(block), row(block), row(ext), row(ext), row(WIN), row(WIN)] + [weight] * 3,
        row(block),
        grid=(rows,),
        mib=63,
        name="chars_grad",
    )


def swap(value, axis, bit):
    count = lax.axis_size(axis)
    return lax.ppermute(value, axis, [(i, i ^ bit) for i in range(count)])


def plus(left, right):
    return (left.astype(F32) + right.astype(F32)).astype(BF)


def add_kernel(meta, left, right, out):
    out[...] = plus(left[...], right[...])


class Beat:
    def __init__(self, chain, meta):
        self.chain, self.meta = chain, meta
        self.steps, self.carried = [], []
        self.fed = False

    def add(self, body, args, outs, then, scratch=()):
        self.steps.append((body, args, outs, then, scratch))

    def carry(self, value, then):
        self.carried.append((value, then))

    def emit(self, name):
        args = [self.meta] + [a for step in self.steps for a in step[1]]
        outs = [o for step in self.steps for o in step[2]]
        scratch = [x for step in self.steps for x in step[4]]
        moved = [value for value, _ in self.carried]
        counts = [len(args), len(moved), len(outs), len(moved)]

        def body(*refs):
            ins = refs[1 : counts[0]]
            results = refs[counts[0] + counts[1] : sum(counts[:3])]
            rest = refs[sum(counts) :]
            for step_body, step_args, step_outs, _, step_scratch in self.steps:
                a, o, x = len(step_args), len(step_outs), len(step_scratch)
                step_body(refs[0], *ins[:a], *results[:o], *rest[:x])
                ins, results, rest = ins[a:], results[o:], rest[x:]

        def call(deps, *given):
            return run(
                body,
                () if self.fed else deps,
                given,
                outs + [shape(value.shape, value.dtype) for value in moved],
                [spec_smem()] + [spec_vmem()] * (len(args) - 1) + [spec_hbm()] * len(moved),
                [spec_vmem()] * len(outs) + [spec_hbm()] * len(moved),
                scratch=scratch,
                mib=24,
                flops=1 if self.steps and self.steps[0][4] == () else 10**12,
                nbytes=10**9 if self.steps and self.steps[0][4] == () else 1,
                aliases={len(args) + k: len(outs) + k for k in range(len(moved))},
                name=name,
            )

        made = self.chain(call, *args, *moved)
        for step in self.steps:
            step[3](*made[: len(step[2])])
            made = made[len(step[2]) :]
        for (_, then), value in zip(self.carried, made, strict=True):
            then(value)


def split_kernel(role, meta, keep, arrived, a_out, a_keep, b_out, b_keep):
    half = keep.shape[1] // 2
    part = half // 2
    mine = meta[role]
    for slot, out in ((0, a_out), (1, a_keep)):
        out[...] = plus(keep[slot, 0:half, :], arrived[slot, 0:half, :])
    for slot in range(2):
        for out, which in ((b_out, 1 - mine), (b_keep, mine)):
            at = pl.ds(pl.multiple_of(half + which * part, 16), part)
            out[slot] = plus(keep[slot, at, :], arrived[slot, at, :])


def cross_kernel(role, meta, a, a_in, b, b_in, a_out, a_keep, b_out, b_keep):
    part = a.shape[0] // 2
    mine = meta[role]
    for out, which in ((a_out, 1 - mine), (a_keep, mine)):
        at = pl.ds(pl.multiple_of(which * part, 16), part)
        out[...] = plus(a[at, :], a_in[at, :])
    b_out[...] = plus(b[0], b_in[0])
    b_keep[...] = plus(b[1], b_in[1])


def merge_kernel(role, meta, a, a_in, b, b_in, out, keep):
    part = a.shape[0] // 2
    mine = meta[3 - role]
    for k, (left, right) in enumerate(((a, a_in), (b, b_in))):
        for made, which in ((out, 1 - mine), (keep, mine)):
            at = pl.ds(pl.multiple_of(which * part, 16), part)
            made[k] = plus(left[at, :], right[at, :])


def join_kernel(role, meta, own, other, out):
    part = own.shape[1]
    mine = meta[3 - role]
    for source, which in ((own, mine), (other, 1 - mine)):
        at = pl.ds(pl.multiple_of(which * part, 16), part)
        for k in range(2):
            out[k, at, :] = source[k]


def end_kernel(role, plan, meta, own, other, *refs):
    outs, whole = refs[:-1], refs[-1]
    part, width = own.shape[1:]
    mine = meta[role]
    for source, which in ((own, mine), (other, 1 - mine)):
        for k in range(2):
            at = pl.ds(pl.multiple_of((2 * k + which) * part, 16), part)
            whole[at, :] = source[k]
    row = 0
    for out, pieces in zip(outs, plan, strict=True):
        for at, rows in pieces:
            out[:, at * width : (at + 1) * width] = whole[row : row + rows, :].astype(F32)
            row += rows


class Sum:
    def __init__(self, keep, role):
        self.height, self.width = keep.shape[1:]
        self.keep, self.role = keep, role
        self.next = self.split
        self.bit = 2

    def of(self, body):
        return functools.partial(body, self.role)

    def core(self, send):
        self.arrived = swap(send, "seq", 1)

    def split(self, beat):
        height, width = self.height, self.width
        half, part = shape((height // 2, width)), shape((2, height // 4, width))

        def then(a_out, a, b_out, b):
            self.a, self.b = a, b
            self.a_in, self.b_in = swap(a_out, "seq", 2), swap(b_out, "dp", self.role)
            self.next = self.cross

        beat.add(self.of(split_kernel), [self.keep, self.arrived], [half, half, part, part], then)

    def cross(self, beat):
        part = shape((self.height // 4, self.width))

        def then(a_out, a, b_out, b):
            self.a, self.b = a, b
            self.a_in, self.b_in = swap(a_out, "dp", self.role), swap(b_out, "seq", 2)
            self.next = self.merge

        beat.add(self.of(cross_kernel), [self.a, self.a_in, self.b, self.b_in], [part] * 4, then)

    def merge(self, beat):
        part = shape((2, self.height // 8, self.width))

        def then(out, keep):
            self.keep = keep
            self.arrived = swap(out, "dp", 3 - self.role)
            self.next = self.more

        beat.add(self.of(merge_kernel), [self.a, self.a_in, self.b, self.b_in], [part] * 2, then)

    def more(self, beat):
        def then(total):
            self.keep = total
            self.bit *= 2
            last = self.bit >= lax.axis_size("dp")
            self.arrived = swap(total, "dp", 3 - self.role if last else self.bit)
            self.next = self.join if last else self.more

        beat.add(add_kernel, [self.keep, self.arrived], [shape(self.keep.shape)], then)

    def join(self, beat):
        def then(whole):
            self.keep = whole
            self.arrived = swap(whole, "dp", self.role)
            self.next = None

        whole = shape((2, self.height // 4, self.width))
        beat.add(self.of(join_kernel), [self.keep, self.arrived], [whole], then)

    def hold(self, arrived):
        self.arrived = arrived

    def end(self, beat, plan):
        width = self.width
        outs = [shape((pieces[0][1], width * len(pieces)), F32) for pieces in plan]

        def then(*made):
            self.made = made

        beat.add(
            functools.partial(end_kernel, self.role, plan),
            [self.keep, self.arrived],
            outs,
            then,
            [pltpu.VMEM((self.height, width), BF)],
        )


class Chain:
    def __init__(self):
        self.last = ()

    def __call__(self, made, *args):
        outs, mark = made(self.last, *args)
        self.last = (mark,)
        return outs


def shards(
    chars,
    window_mask,
    micro_batch,
    mol_grad,
    query_weight,
    query_bias,
    key_weight,
    value_weight,
    value_bias,
    output_weight,
    output_bias,
    first_gain,
    first_shift,
    inner_weight,
    inner_bias,
    outer_weight,
    outer_bias,
    second_gain,
    second_shift,
    conv_weight,
    conv_bias,
    third_gain,
    third_shift,
):
    rows, block, width = chars.shape
    count = rows * block
    place = lax.axis_index("seq").astype(jnp.int32)
    group = lax.axis_index("dp").astype(jnp.int32)
    meta = jnp.stack([place, group % 2, group // 2 % 2])
    size = lax.axis_size("seq")
    forward_pairs = [(i, i + 1) for i in range(size - 1)]
    backward_pairs = [(i + 1, i) for i in range(size - 1)]
    low = lax.ppermute(chars[:, block - WIN :], "seq", forward_pairs)
    high = lax.ppermute(chars[:, :WIN], "seq", backward_pairs)
    vectors = (
        query_bias,
        value_bias,
        output_bias,
        first_gain,
        first_shift,
        outer_bias,
        second_gain,
        second_shift,
        conv_bias,
        third_gain,
        third_shift,
        inner_bias,
    )
    tokens = chars.reshape(count, width)
    chain = Chain()
    q, k, v, vecs = chain(project, tokens, vectors, query_weight, key_weight, value_weight)
    kv, probs, mixed, n1, inv1, low1, slope, hidden, mol, go, sums3, send_c, keep_c = chain(
        forward,
        meta,
        window_mask,
        micro_batch,
        vecs,
        tokens,
        low,
        high,
        q,
        k,
        v,
        key_weight,
        value_weight,
        output_weight,
        inner_weight,
        outer_weight,
        conv_weight,
        mol_grad.reshape(-1, width),
    )
    molecules = mol.reshape(mol_grad.shape)
    conv = Sum(keep_c, 2)
    conv.core(send_c)
    send_u, keep_u = chain(outer_grad, meta, go, hidden)
    outer = Sum(keep_u, 2)

    def beat(name, chunks, carried=(), ends=(), fed=False):
        made = Beat(chain, meta)
        made.fed = fed
        for chunk in chunks:
            chunk.next(made)
        for chunk, plan in ends:
            chunk.end(made, plan)
        for value, then in carried:
            made.carry(value, then)
        made.emit(name)

    beat("beat1", [conv], [(send_u, outer.core)], fed=True)
    common = (meta, vecs, go, slope, outer_weight, inner_weight, low1)
    send_i, keep_i, isum_a, acc = chain(inner_back, (0, 1), *common)
    beat("beat2", [conv, outer])
    send_i, keep_i, isum_b, gb, gm, sums1 = chain(
        inner_back,
        (2, 3),
        *common,
        acc,
        n1,
        inv1,
        output_weight,
        mixed,
        send_i,
        keep_i,
    )
    inner = Sum(keep_i, 1)
    beat("beat3", [conv, outer], [(send_i, inner.core)], fed=True)
    beat("beat3i", [inner])
    grads = ()
    for r in range(rows):
        grads = chain(attention_back, q, kv, probs, gm, rows, r, tuple(grads))
        beat("beat%d" % (4 + r), [conv, outer, inner])
    dq, dk, dv, sums_a = grads
    send_p, keep_p = chain(
        project_grad, meta, dq, chars, dk, low, high, dv, sums_a, sums1, sums3, isum_a, isum_b
    )
    proj = Sum(keep_p, 1)
    beside = {}

    def from_prev(value):
        beside["low"] = lax.ppermute(value, "seq", forward_pairs)

    def from_next(value):
        beside["high"] = lax.ppermute(value, "seq", backward_pairs)

    quarter = width // 4
    wide = [[(j, quarter) for j in range(4)]]
    holds = lambda *chunks: [(chunk.arrived, chunk.hold) for chunk in chunks]
    beat("tail0", [conv, outer, inner], [(send_p, proj.core)], fed=True)
    beat("tail1", [proj])
    grad_low, grad_high = chain(halo_grad, dk, dv, key_weight, value_weight)
    beat("tail2", [proj, inner], [(grad_high, from_prev), (grad_low, from_next)])
    beat("tail3", [proj, outer, inner], holds(conv))
    beat("tail4", [proj])
    grad_chars = chain(
        chars_grad,
        gb,
        dq,
        dk,
        dv,
        beside["low"],
        beside["high"],
        query_weight,
        key_weight,
        value_weight,
    )
    while proj.next != proj.join:
        beat("tail_more", [chunk for chunk in (proj, conv, outer, inner) if chunk.next == chunk.more])
    for chunk in (conv, outer, inner):
        while chunk.next is not None:
            beat("tail_rest", [chunk])
    beat("tail6", [proj], holds(outer, inner))
    beat("ends0", [], (), [(outer, wide), (inner, [[(0, width)], [(0, quarter)]])])
    beat("ends1", [], (), [(conv, wide)])
    beat("tail7", [], (), [(proj, [[(0, quarter)]] * 3 + [[(0, 16)]])])
    (full_c,), (full_u,) = conv.made, outer.made
    full_i, full_o = inner.made
    full_q, full_k, full_v, small = proj.made
    vec_of = lambda i: small[i, :quarter]
    return (
        molecules,
        grad_chars,
        full_q.T,
        vec_of(0),
        full_k.T,
        full_v.T,
        vec_of(1),
        full_o.T,
        vec_of(2),
        vec_of(3),
        vec_of(4),
        full_i,
        small[11:15, :quarter].reshape(-1),
        full_u.T,
        vec_of(5),
        vec_of(6),
        vec_of(7),
        full_c.T,
        vec_of(8),
        vec_of(9),
        vec_of(10),
    )


def solution(mesh):
    split = P("dp", "seq", None)
    placed = (split, P("dp", None), P("dp"), split) + (P(),) * 19
    by_column, by_place = P(None, "seq"), P("seq")
    outs = (
        split,
        split,
        by_column,
        by_place,
        by_column,
        by_column,
        by_place,
        by_column,
        by_place,
        by_place,
        by_place,
        by_column,
        by_place,
        by_column,
        by_place,
        by_place,
        by_place,
        by_column,
        by_place,
        by_place,
        by_place,
    )
    return jax.shard_map(shards, mesh=mesh, in_specs=placed, out_specs=outs, check_vma=False)
```

```python
import functools

import jax
import jax.numpy as jnp
from jax import lax
from jax.experimental import pallas as pl
from jax.experimental.pallas import tpu as pltpu
from jax.sharding import PartitionSpec as P

HEADS = 12
HEAD_DIM = 64
WIN = 128
DOWN = 4
MICRO = 2
EPSILON = 1e-06
NEG_FILL = -1e30
GELU_A = 0.7978845608028654
GELU_B = 0.044715
BF = jnp.bfloat16
F32 = jnp.float32
LANES = 128
MIB = 1 << 20

NN = (((1,), (0,)), ((), ()))
NT = (((1,), (1,)), ((), ()))
TN = (((0,), (0,)), ((), ()))

(V_QB, V_VB, V_OB, V_G1, V_S1, V_OUTB, V_G2, V_S2, V_CB, V_G3, V_S3, V_IB) = range(12)


def dot(left, right, dims=NN):
    return lax.dot_general(left, right, dims, preferred_element_type=F32)


def gelu_both(u):
    square = u * u
    t = jnp.tanh(u * (GELU_A + (GELU_A * GELU_B) * square))
    half = 0.5 + 0.5 * t
    value = u * half
    slope = half + value * (1.0 - t) * (GELU_A + (3.0 * GELU_A * GELU_B) * square)
    return value, slope


def layer_stats(u):
    center = u - jnp.mean(u, axis=-1, keepdims=True)
    inv_dev = lax.rsqrt(jnp.mean(center * center, axis=-1, keepdims=True) + EPSILON)
    return center * inv_dev, inv_dev


def norm_back(grad_out, normal, inv_dev, gain_vec):
    scaled = grad_out * gain_vec
    return inv_dev * (
        scaled
        - jnp.mean(scaled, axis=-1, keepdims=True)
        - normal * jnp.mean(scaled * normal, axis=-1, keepdims=True)
    )


def col_sum(value):
    return jnp.sum(value, axis=0, keepdims=True)


def params(mib=56, **more):
    return pltpu.CompilerParams(vmem_limit_bytes=mib * MIB, **more)


def cost(flops, nbytes):
    return pl.CostEstimate(flops=int(flops), bytes_accessed=int(nbytes), transcendentals=0)


def spec_any():
    return pl.BlockSpec(memory_space=pl.ANY)


def spec_hbm():
    return pl.BlockSpec(memory_space=pltpu.HBM)


def spec_smem():
    return pl.BlockSpec(memory_space=pltpu.SMEM)


def spec_vmem():
    return pl.BlockSpec(memory_space=pltpu.VMEM)


def shape(dims, dtype=BF):
    return jax.ShapeDtypeStruct(tuple(dims), dtype)


def run(body, deps, args, out_shape, in_specs, out_specs, scratch=(), grid=(), prefetch=0, mib=56, flops=10**12, nbytes=10**6, name=None, aliases=None):
    given = len(args)
    single = not isinstance(out_shape, (list, tuple))
    outs = [out_shape] if single else list(out_shape)
    specs = [out_specs] if single else list(out_specs)
    mark = pl.BlockSpec((8, LANES), lambda *_: (0, 0)) if grid else spec_vmem()

    def wrapped(*refs):
        rest = refs[given + len(deps) :]
        rest[len(outs)][...] = jnp.zeros((8, LANES), F32)
        body(*refs[:given], *rest[: len(outs)], *rest[len(outs) + 1 :])

    made = pl.pallas_call(
        wrapped,
        grid_spec=pltpu.PrefetchScalarGridSpec(
            num_scalar_prefetch=prefetch,
            grid=grid,
            in_specs=list(in_specs) + [spec_any()] * len(deps),
            out_specs=specs + [mark],
            scratch_shapes=list(scratch),
        ),
        out_shape=outs + [shape((8, LANES), F32)],
        compiler_params=pltpu.CompilerParams(vmem_limit_bytes=mib * MIB),
        cost_estimate=cost(flops, nbytes),
        input_output_aliases=aliases or {},
        name=name,
    )(*args, *deps)
    return made[0] if single else made[:-1], made[-1]


def head_masks():
    lane = lax.broadcasted_iota(jnp.int32, (1, LANES), 1)
    first = jnp.where(lane < HEAD_DIM, 1.0, 0.0).astype(BF)
    return first, (1.0 - first.astype(F32)).astype(BF)


def twice(block, masks):
    return jnp.concatenate([block * masks[0], block * masks[1]], axis=0)


def slot_of(quarter, place):
    same_x = (quarter // 2 == place // 2).astype(jnp.int32)
    same_core = (quarter % 2 == place % 2).astype(jnp.int32)
    return 2 * same_core + same_x


def project_kernel(names, x_ref, *refs):
    vectors, (wq_ref, wk_ref, wv_ref, q_ref, k_ref, v_ref, vec_ref) = refs[:names], refs[names:]
    width = x_ref.shape[1]
    part = wq_ref.shape[1]
    step = pl.program_id(0)

    @pl.when(step == 0)
    def _():
        row = 0
        for ref in vectors:
            value = ref[...].astype(F32)
            for k in range(value.shape[0] // width):
                vec_ref[row : row + 1, :] = value[k * width : (k + 1) * width].reshape(1, width)
                row += 1
        vec_ref[row:, :] = jnp.zeros((vec_ref.shape[0] - row, width), F32)

    x = x_ref[...]
    at = pl.ds(pl.multiple_of(step * part, part), part)
    queries = (dot(x, wq_ref[...]) + vec_ref[V_QB : V_QB + 1, at]).astype(BF)
    q_ref[...] = queries * jnp.asarray(HEAD_DIM**-0.5, BF)
    k_ref[...] = dot(x, wk_ref[...]).astype(BF)
    v_ref[...] = (dot(x, wv_ref[...]) + vec_ref[V_VB : V_VB + 1, at]).astype(BF)


def project(deps, tokens, vectors, wq, wk, wv):
    count, width = tokens.shape
    part = 256
    column = pl.BlockSpec((width, part), lambda i: (0, i))
    out = pl.BlockSpec((count, part), lambda i: (0, i))
    height = rounded_up(sum(v.shape[0] for v in vectors) // width, 8)
    return run(
        functools.partial(project_kernel, len(vectors)),
        deps,
        (tokens, *vectors, wq, wk, wv),
        [shape((count, width))] * 3 + [shape((height, width), F32)],
        [pl.BlockSpec((count, width), lambda i: (0, 0))]
        + [pl.BlockSpec(v.shape, lambda i: (0,)) for v in vectors]
        + [column] * 3,
        [out] * 3 + [pl.BlockSpec((height, width), lambda i: (0, 0))],
        grid=(width // part,),
        mib=60,
        name="project",
    )


def forward_kernel(
    rows,
    wins,
    windows_all,
    meta,
    wmask,
    mbatch,
    vec,
    chars_h,
    low_h,
    high_h,
    q_h,
    k_h,
    v_h,
    wk_h,
    wv_h,
    wo_h,
    wi_h,
    wout_h,
    wc_h,
    mg_h,
    kv_o,
    pt_o,
    mixed_o,
    n1_o,
    inv1_o,
    low1_o,
    slope_o,
    hidden_o,
    mol_o,
    go_o,
    sums_o,
    send_o,
    keep_o,
    q,
    kv,
    halo,
    wkv,
    wo,
    chars,
    wi,
    wout,
    wc,
    mg,
    probs,
    mixed,
    acc,
    strips,
    low1,
    n1,
    inv1,
    slope,
    hidden,
    n2,
    inv2,
    merged,
    mol,
    sem_in,
    sem_p,
    sem_h,
    sem_out,
):
    place = meta[0]
    block = wins * WIN
    width = chars.shape[-1]
    count = rows * block
    pairs = width // LANES
    parts = wi.shape[1] // width

    def copy_in(index, src, dst):
        made = pltpu.make_async_copy(src, dst, sem_in.at[index])
        made.start()
        return made

    halo_in = [
        copy_in(0, low_h, halo.at[0]),
        copy_in(1, high_h, halo.at[1]),
        copy_in(2, wk_h, wkv.at[0]),
        copy_in(3, wv_h, wkv.at[1]),
    ]
    qkv_in = [copy_in(4, q_h, q)]
    for r in range(rows):
        qkv_in.append(
            copy_in(5 + 2 * r, k_h.at[pl.ds(r * block, block)], kv.at[r, pl.ds(WIN, block)])
        )
        qkv_in.append(
            copy_in(
                6 + 2 * r, v_h.at[pl.ds(r * block, block)], kv.at[rows + r, pl.ds(WIN, block)]
            )
        )
    base = 5 + 2 * rows

    def copy_out(index, src, dst):
        made = pltpu.make_async_copy(src, dst, sem_out.at[index])
        made.start()
        return made

    for made in halo_in:
        made.wait()
    beside = halo[...].reshape(2 * rows * WIN, width)
    keys = dot(beside, wkv[0]).astype(BF)
    values = (dot(beside, wkv[1]) + vec[V_VB : V_VB + 1, :]).astype(BF)
    for side in range(2):
        start = side * (block + WIN)
        for r in range(rows):
            at = (side * rows + r) * WIN
            kv[r, pl.ds(start, WIN), :] = keys[at : at + WIN]
            kv[rows + r, pl.ds(start, WIN), :] = values[at : at + WIN]
    for made in qkv_in:
        made.wait()
    wo_in = copy_in(base, wo_h, wo)
    chars_in = copy_in(base + 1, chars_h, chars)
    wi_in = copy_in(base + 2, wi_h, wi)
    wout_in = copy_in(base + 3, wout_h, wout)
    kv_out = copy_out(0, kv, kv_o)

    masks = head_masks()

    def pair_step(it, carry):
        r = it // pairs
        pair = it % pairs
        slot = it % 2
        lanes = pl.ds(pl.multiple_of(pair * LANES, LANES), LANES)

        @pl.when(it >= 2)
        def _():
            pltpu.make_async_copy(probs.at[slot], pt_o.at[it - 2], sem_p.at[slot]).wait()

        every = []
        for w in range(wins):
            queries = twice(q[pl.ds(r * block + w * WIN, WIN), lanes], masks)
            every.append(dot(kv[r, pl.ds(w * WIN, 3 * WIN), lanes], queries, NT))
        chances = []
        for w, scores in enumerate(every):
            at = place * wins + w
            low_ok = (at >= 1) & (wmask[r, jnp.maximum(at - 1, 0)] > 0)
            high_ok = (at + 1 < windows_all) & (wmask[r, jnp.minimum(at + 1, windows_all - 1)] > 0)
            scores = jnp.concatenate(
                [
                    scores[0:WIN] + jnp.where(low_ok, 0.0, NEG_FILL),
                    scores[WIN : 2 * WIN],
                    scores[2 * WIN :] + jnp.where(high_ok, 0.0, NEG_FILL),
                ],
                axis=0,
            )
            shifted = jnp.exp(scores - jnp.max(scores, axis=0, keepdims=True))
            total = jnp.sum(shifted, axis=0, keepdims=True)
            chances.append((shifted * (1.0 / total)).astype(BF))
            probs[slot, w] = chances[w]
        for w, chance in enumerate(chances):
            stacked = jnp.concatenate([chance[:, :LANES], chance[:, LANES:]], axis=0)
            values_win = twice(kv[rows + r, pl.ds(w * WIN, 3 * WIN), lanes], masks)
            mixed[pl.ds(r * block + w * WIN, WIN), lanes] = dot(stacked, values_win, TN).astype(BF)
        pltpu.make_async_copy(probs.at[slot], pt_o.at[it], sem_p.at[slot]).start()
        return carry

    steps = rows * pairs
    lax.fori_loop(0, steps, pair_step, 0)
    mixed_out = copy_out(1, mixed, mixed_o)

    wo_in.wait()
    chars_in.wait()
    wc_in = copy_in(base + 4, wc_h, wc)
    mg_in = copy_in(base + 5, mg_h, mg)
    piece = 256

    pieces = [pl.ds(i * piece, piece) for i in range(count // piece)]
    branches = [dot(mixed[at, :], wo[...]) for at in pieces]
    for at, branch in zip(pieces, branches, strict=True):
        u = branch + vec[V_OB : V_OB + 1, :] + chars[at, :].astype(F32)
        normal, inv = layer_stats(u)
        first = normal * vec[V_G1 : V_G1 + 1, :] + vec[V_S1 : V_S1 + 1, :]
        n1[at, :] = normal.astype(BF)
        inv1[at, :] = inv
        low1[at, :] = first.astype(BF)
        acc[at, :] = first + vec[V_OUTB : V_OUTB + 1, :]
    outs = [mixed_out, copy_out(2, n1, n1_o), copy_out(3, inv1, inv1_o), copy_out(4, low1, low1_o)]

    wi_in.wait()
    wout_in.wait()

    def ffn_step(c, carry):
        slot = c % 2
        columns = pl.ds(pl.multiple_of(c * width, width), width)

        @pl.when(c >= 2)
        def _():
            pltpu.make_async_copy(slope.at[slot], slope_o.at[c - 2], sem_h.at[slot]).wait()
            pltpu.make_async_copy(hidden.at[slot], hidden_o.at[c - 2], sem_h.at[2 + slot]).wait()

        bias = vec[pl.ds(V_IB + c, 1), :]
        half = count // 2
        parts_of = [pl.ds(k * half, half) for k in range(2)]
        upper, lower = (dot(low1[at, :], wi[:, columns]) + bias for at in parts_of)
        for at, u in zip(parts_of, (upper, lower), strict=True):
            value, steep = gelu_both(u)
            slope[slot, at, :] = steep.astype(BF)
            h = value.astype(BF)
            hidden[slot, at, :] = h
            acc[at, :] += dot(h, wout[columns, :])
        pltpu.make_async_copy(slope.at[slot], slope_o.at[c], sem_h.at[slot]).start()
        pltpu.make_async_copy(hidden.at[slot], hidden_o.at[c], sem_h.at[2 + slot]).start()
        return carry

    lax.fori_loop(0, parts, ffn_step, 0)

    def second_step(i, carry):
        at = pl.ds(pl.multiple_of(i * piece, piece), piece)
        normal, inv = layer_stats(acc[at, :])
        n2[at, :] = normal.astype(BF)
        inv2[at, :] = inv
        second = normal * vec[V_G2 : V_G2 + 1, :] + vec[V_S2 : V_S2 + 1, :]
        for t in range(pairs):
            strips[t, at, :] = second[:, t * LANES : (t + 1) * LANES]
        return carry

    lax.fori_loop(0, count // piece, second_step, 0, unroll=True)

    wc_in.wait()
    mg_in.wait()
    mols = count // DOWN
    conv = jnp.zeros((mols, width), F32) + vec[V_CB : V_CB + 1, :]
    for i in range(DOWN):
        for t in range(pairs):
            merged[i, :, t * LANES : (t + 1) * LANES] = strips[
                t, pl.ds(i, mols, stride=DOWN), :
            ].astype(BF)
        part = merged[i]
        conv = conv + dot(part, wc[pl.ds(i * width, width), :])
    value, steep = gelu_both(conv)
    normal, inv = layer_stats(value)
    per_win = WIN // DOWN
    which = lax.broadcasted_iota(jnp.int32, (mols, 1), 0) // per_win
    live = jnp.zeros((mols, 1), F32)
    total = jnp.ones((mols, 1), F32)
    lengths = []
    for r in range(rows):
        length = wmask[r, 0]
        for w in range(1, windows_all):
            length = length + wmask[r, w]
        lengths.append(length)
    for r in range(rows):
        same = jnp.int32(0)
        for other in range(rows):
            same = same + jnp.where(mbatch[other] == mbatch[r], lengths[other], 0)
        same = (same * per_win).astype(F32)
        for w in range(wins):
            here = which == r * wins + w
            live = jnp.where(here, wmask[r, place * wins + w].astype(F32), live)
            total = jnp.where(here, same, total)
    weight = (rows // MICRO * windows_all * per_win) / total
    gain = vec[V_G3 : V_G3 + 1, :]
    mol[...] = ((normal * gain + vec[V_S3 : V_S3 + 1, :]) * live).astype(BF)
    outs.append(copy_out(5, mol, mol_o))
    grad_mol = mg[...].astype(F32) * (weight * live)
    grad_conv = (steep * norm_back(grad_mol, normal, inv, gain)).astype(BF)
    sums_o[0:1, :] = col_sum(grad_mol * normal)
    sums_o[1:2, :] = col_sum(grad_mol)
    sums_o[2:3, :] = col_sum(grad_conv.astype(F32))
    sums_o[3:, :] = jnp.zeros((sums_o.shape[0] - 3, width), F32)

    kv_out.wait()
    across = grad_conv.T
    quarter = width // 4
    for i in range(DOWN):
        made = dot(across, merged[i]).astype(BF)
        for number in range(4):
            kv[slot_of(jnp.int32(number), place), pl.ds(i * quarter, quarter), :] = made[
                number * quarter : (number + 1) * quarter
            ]
    outs.append(copy_out(6, kv.at[pl.ds(0, 2)], send_o))
    outs.append(copy_out(7, kv.at[pl.ds(2, 2)], keep_o))

    for i in range(DOWN):
        made = dot(grad_conv, wc[pl.ds(i * width, width), :], NT)
        for t in range(pairs):
            strips[t, pl.ds(i, mols, stride=DOWN), :] = made[:, t * LANES : (t + 1) * LANES]
    gain = vec[V_G2 : V_G2 + 1, :]

    def back_step(i, carry):
        at = pl.ds(pl.multiple_of(i * piece, piece), piece)
        grad = jnp.concatenate([strips[t, at, :] for t in range(pairs)], axis=1)
        normal = n2[at, :].astype(F32)
        made = norm_back(grad, normal, inv2[at, :], gain).astype(BF)
        n2[at, :] = made
        sums_o[3:4, :] += col_sum(grad * normal)
        sums_o[4:5, :] += col_sum(grad)
        sums_o[5:6, :] += col_sum(made.astype(F32))
        return carry

    lax.fori_loop(0, count // piece, back_step, 0, unroll=True)
    outs.append(copy_out(8, n2, go_o))

    for made in outs:
        made.wait()
    for it in range(max(0, steps - 2), steps):
        pltpu.make_async_copy(probs.at[it % 2], pt_o.at[it], sem_p.at[it % 2]).wait()
    for c in range(max(0, parts - 2), parts):
        pltpu.make_async_copy(slope.at[c % 2], slope_o.at[c], sem_h.at[c % 2]).wait()
        pltpu.make_async_copy(hidden.at[c % 2], hidden_o.at[c], sem_h.at[2 + c % 2]).wait()


def forward(deps, meta, wmask, mbatch, vecs, chars, low, high, q, k, v, wk, wv, wo, wi, wout, wc, mg):
    rows = wmask.shape[0]
    windows_all = wmask.shape[1]
    count, width = q.shape
    block = count // rows
    wins = block // WIN
    ff = wi.shape[1]
    parts = ff // width
    mols = count // DOWN
    pairs = width // LANES
    ext = block + 2 * WIN
    outs = [
        shape((2 * rows, ext, width)),
        shape((rows * pairs, wins, 3 * WIN, 2 * LANES)),
        shape((count, width)),
        shape((count, width)),
        shape((count, 1), F32),
        shape((count, width)),
        shape((parts, count, width)),
        shape((parts, count, width)),
        shape((mols, width)),
        shape((count, width)),
        shape((8, width), F32),
        shape((2, DOWN * width // 4, width)),
        shape((2, DOWN * width // 4, width)),
    ]
    out_specs = [spec_any()] * len(outs)
    out_specs[10] = spec_vmem()
    return run(
        functools.partial(forward_kernel, rows, wins, windows_all),
        deps,
        (meta, wmask, mbatch, vecs, chars, low, high, q, k, v, wk, wv, wo, wi, wout, wc, mg),
        outs,
        [spec_smem()] * 3 + [spec_vmem()] + [spec_any()] * 13,
        out_specs,
        scratch=[
            pltpu.VMEM((count, width), BF),
            pltpu.VMEM((2 * rows, ext, width), BF),
            pltpu.VMEM((2, rows, WIN, width), BF),
            pltpu.VMEM((2, width, width), BF),
            pltpu.VMEM((width, width), BF),
            pltpu.VMEM((count, width), BF),
            pltpu.VMEM((width, ff), BF),
            pltpu.VMEM((ff, width), BF),
            pltpu.VMEM((DOWN * width, width), BF),
            pltpu.VMEM((mols, width), BF),
            pltpu.VMEM((2, wins, 3 * WIN, 2 * LANES), BF),
            pltpu.VMEM((count, width), BF),
            pltpu.VMEM((count, width), F32),
            pltpu.VMEM((pairs, count, LANES), F32),
            pltpu.VMEM((count, width), BF),
            pltpu.VMEM((count, width), BF),
            pltpu.VMEM((count, 1), F32),
            pltpu.VMEM((2, count, width), BF),
            pltpu.VMEM((2, count, width), BF),
            pltpu.VMEM((count, width), BF),
            pltpu.VMEM((count, 1), F32),
            pltpu.VMEM((DOWN, mols, width), BF),
            pltpu.VMEM((mols, width), BF),
            pltpu.SemaphoreType.DMA((11 + 2 * rows,)),
            pltpu.SemaphoreType.DMA((2,)),
            pltpu.SemaphoreType.DMA((4,)),
            pltpu.SemaphoreType.DMA((9,)),
        ],
        mib=60,
        name="forward",
    )


def outer_grad_kernel(meta, go, hidden, send, keep, across):
    place = meta[0]
    width = go.shape[1]
    quarter = width // 4

    @pl.when(pl.program_id(0) == 0)
    def _():
        turned = go[...].T
        for number in range(4):
            across[slot_of(jnp.int32(number), place)] = turned[
                number * quarter : (number + 1) * quarter
            ]

    left = across[...].reshape(width, go.shape[0])
    made = dot(left, hidden[0]).astype(BF)
    for j in range(2):
        send[j] = made[j * quarter : (j + 1) * quarter]
        keep[j] = made[(2 + j) * quarter : (3 + j) * quarter]


def outer_grad(deps, meta, go, hidden):
    parts, count, width = hidden.shape
    quarter = width // 4
    out = pl.BlockSpec((2, quarter, width), lambda i, m: (0, i, 0))
    return run(
        outer_grad_kernel,
        deps,
        (meta, go, hidden),
        [shape((2, parts * quarter, width))] * 2,
        [
            pl.BlockSpec((count, width), lambda i, m: (0, 0)),
            pl.BlockSpec((1, count, width), lambda i, m: (i, 0, 0)),
        ],
        [out] * 2,
        scratch=[pltpu.VMEM((4, quarter, count), BF)],
        grid=(parts,),
        prefetch=1,
        name="outer_grad",
    )


def slot_copies(src, send, keep, slot, at, sem):
    out = pltpu.make_async_copy(src, send.at[jnp.minimum(slot, 1), at], sem)
    own = pltpu.make_async_copy(src, keep.at[jnp.maximum(slot - 2, 0), at], sem)

    def start():
        @pl.when(slot < 2)
        def _():
            out.start()

        @pl.when(slot >= 2)
        def _():
            own.start()

    return start, out.wait


def inner_back_kernel(first, chosen, meta, vec, go_h, slope_h, wout_h, wi_h, low1_h, *refs):
    if first:
        ins, refs = (), refs
    else:
        ins, refs = refs[:5], refs[7:]
    send, keep, isum, *refs = refs
    if first:
        acc_o, *refs = refs
    else:
        gb_o, gm_o, sums, *refs = refs
    go, slope, wout, wi, low1, acc, grads, *refs = refs
    if not first:
        n1, inv1, wo, mixed, gb, gm, rest, *refs = refs
    sem_in, sem_out = refs
    count, width = go.shape
    place = meta[0]
    quarter = width // 4
    waits = []

    def bring(src, dst):
        made = pltpu.make_async_copy(src, dst, sem_in.at[len(waits)])
        made.start()
        waits.append(made)
        return made

    go_in = bring(go_h, go)
    parts_in = []
    for k, c in enumerate(chosen):
        at = pl.ds(c * width, width)
        parts_in.append(
            [
                bring(wout_h.at[at], wout.at[k]),
                bring(slope_h.at[c], slope.at[k]),
                bring(wi_h.at[:, at], wi.at[k]),
            ]
        )
        if k == 0:
            low1_in = bring(low1_h, low1)
            acc_in = None if first else bring(ins[0], acc)
    if not first:
        late = [bring(src, dst) for src, dst in zip(ins[1:], (n1, inv1, wo, mixed), strict=True)]
    go_in.wait()
    half = count // 2
    halves = [slice(k * half, (k + 1) * half) for k in range(2)]
    outs = []
    across = None
    for k, c in enumerate(chosen):
        parts_in[k][0].wait()
        if k > 0:
            parts_in[k][1].wait()
            parts_in[k][2].wait()
        steep = [dot(go[at, :], wout[k], NT) for at in halves]
        if across is None:
            low1_in.wait()
            across = low1[...].T
        if k == 0:
            parts_in[k][1].wait()
            parts_in[k][2].wait()
            if not first:
                acc_in.wait()
        low = []
        for at, grad in zip(halves, steep, strict=True):
            low.append((slope[k, at, :].astype(F32) * grad).astype(BF))
            added = dot(low[-1], wi[k], NT)
            if first and k == 0:
                acc[at, :] = go[at, :].astype(F32) + added
            else:
                acc[at, :] += added
        made = jnp.concatenate(low, axis=0)
        isum[k] = jnp.broadcast_to(col_sum(made.astype(F32)), (8, width))
        grads[k] = dot(across, made).astype(BF)
        slot = slot_of(jnp.int32(c), place)
        start, wait = slot_copies(
            grads.at[k], send, keep, slot, pl.ds(0, width), sem_out.at[len(outs)]
        )
        start()
        outs.append(wait)

    def leave(src, dst):
        made = pltpu.make_async_copy(src, dst, sem_out.at[len(outs)])
        made.start()
        outs.append(made.wait)

    if first:
        leave(acc, acc_o)
    else:
        for made in late:
            made.wait()
        gain = vec[V_G1 : V_G1 + 1, :]
        piece = 256
        sums[...] = jnp.zeros(sums.shape, F32)
        lows = []
        for j in range(count // piece):
            at = slice(j * piece, (j + 1) * piece)
            grad = acc[at, :]
            normal = n1[at, :].astype(F32)
            lows.append(norm_back(grad, normal, inv1[at, :], gain).astype(BF))
            gb[at, :] = lows[-1]
            sums[0:1, :] += col_sum(grad * normal)
            sums[1:2, :] += col_sum(grad)
            sums[2:3, :] += col_sum(lows[-1].astype(F32))
        leave(gb, gb_o)
        for j in range(count // piece):
            gm[j * piece : (j + 1) * piece, :] = dot(lows[j], wo[...], NT).astype(BF)
        leave(gm, gm_o)
        rest[...] = jnp.zeros(rest.shape, BF)
        extra = rest.shape[1] - quarter
        made = dot(gb[...], mixed[...], TN).astype(BF)
        for number in range(4):
            rest[number, 0:quarter, :] = made[number * quarter : (number + 1) * quarter]
            slot = slot_of(jnp.int32(number), place)
            start, wait = slot_copies(
                rest.at[number],
                send,
                keep,
                slot,
                pl.ds(width, quarter + extra),
                sem_out.at[len(outs)],
            )
            start()
            outs.append(wait)
    for wait in outs:
        wait()


def rounded_up(value, unit):
    return -(-value // unit) * unit


def inner_back(deps, chosen, meta, vecs, go, slope, wout, wi, low1, *more):
    _, count, width = slope.shape
    first = not more
    quarter = width // 4
    height = rounded_up(width + quarter, 8 * 16)
    both = shape((2, height, width))
    outs = [both, both, shape((2, 8, width), F32)]
    out_specs = [spec_hbm(), spec_hbm(), spec_vmem()]
    scratch = [
        pltpu.VMEM((count, width), BF),
        pltpu.VMEM((2, count, width), BF),
        pltpu.VMEM((2, width, width), BF),
        pltpu.VMEM((2, width, width), BF),
        pltpu.VMEM((count, width), BF),
        pltpu.VMEM((count, width), F32),
        pltpu.VMEM((2, width, width), BF),
    ]
    if first:
        outs += [shape((count, width), F32)]
        out_specs += [spec_hbm()]
    else:
        outs += [shape((count, width)), shape((count, width)), shape((8, width), F32)]
        out_specs += [spec_hbm(), spec_hbm(), spec_vmem()]
        scratch += [
            pltpu.VMEM((count, width), BF),
            pltpu.VMEM((count, 1), F32),
            pltpu.VMEM((width, width), BF),
            pltpu.VMEM((count, width), BF),
            pltpu.VMEM((count, width), BF),
            pltpu.VMEM((count, width), BF),
            pltpu.VMEM((4, height - width, width), BF),
        ]
    scratch += [pltpu.SemaphoreType.DMA((13,)), pltpu.SemaphoreType.DMA((8,))]
    return run(
        functools.partial(inner_back_kernel, first, chosen),
        deps,
        (meta, vecs, go, slope, wout, wi, low1, *more),
        outs,
        [spec_smem(), spec_vmem()] + [spec_any()] * (5 + len(more)),
        out_specs,
        scratch=scratch,
        aliases={} if first else {12: 0, 13: 1},
        name="inner_back%d" % chosen[0],
    )


def attention_back_kernel(wins, q, k, v, probs, gm, dq, dk, dv, sums):
    masks = head_masks()
    here = [slice(w * WIN, (w + 1) * WIN) for w in range(wins)]
    span = [slice(w * WIN, (w + 3) * WIN) for w in range(wins)]
    grad_out = [twice(gm[0, at, :], masks) for at in here]
    queries = [twice(q[0, at, :], masks) for at in here]
    grad_probs = [dot(v[0, span[w], :], grad_out[w], NT) for w in range(wins)]
    grad_values = [dot(probs[0, w], grad_out[w]) for w in range(wins)]
    grad_scores = []
    for w in range(wins):
        chance = probs[0, w].astype(F32)
        product = chance * grad_probs[w]
        total = jnp.sum(product, axis=0, keepdims=True)
        grad_scores.append((product - chance * total).astype(BF))
    grad_keys = [dot(grad_scores[w], queries[w]) for w in range(wins)]
    q_sum = jnp.zeros((1, LANES), F32)
    for w in range(wins):
        made = grad_scores[w]
        stacked = jnp.concatenate([made[:, :LANES], made[:, LANES:]], axis=0)
        made = dot(stacked, twice(k[0, span[w], :], masks), TN) * HEAD_DIM**-0.5
        low = made.astype(BF)
        dq[0, here[w], :] = low
        q_sum = q_sum + col_sum(low.astype(F32))
    v_sum = jnp.zeros((1, LANES), F32)
    for parts, out in ((grad_keys, dk), (grad_values, dv)):
        for b in range(wins + 2):
            uses = [w for w in range(wins) if 0 <= b - w < 3]
            pieces = [parts[w][(b - w) * WIN : (b - w + 1) * WIN] for w in uses]
            made = sum(pieces[1:], pieces[0])
            out[0, b * WIN : (b + 1) * WIN, :] = made.astype(BF)
            if out is dv:
                v_sum = v_sum + col_sum(made)
    sums[0, 0:1, :] = q_sum
    sums[0, 1:2, :] = v_sum
    sums[0, 2:, :] = jnp.zeros((6, LANES), F32)


def attention_back(deps, q, kv, probs, gm, rows, row, before):
    count, width = q.shape
    block = count // rows
    wins = block // WIN
    ext = kv.shape[1]
    pairs = width // LANES
    own = pl.BlockSpec((1, block, LANES), lambda p: (row, 0, p))
    keys = pl.BlockSpec((1, ext, LANES), lambda p: (row, 0, p))
    values = pl.BlockSpec((1, ext, LANES), lambda p: (rows + row, 0, p))

    def body(q, k, v, probs, gm, *refs):
        attention_back_kernel(wins, q, k, v, probs, gm, *refs[len(before) :])

    return run(
        body,
        deps,
        (q.reshape(rows, block, width), kv, kv, probs, gm.reshape(rows, block, width), *before),
        [
            shape((rows, block, width)),
            shape((rows, ext, width)),
            shape((rows, ext, width)),
            shape((rows, 8, width), F32),
        ],
        [
            own,
            keys,
            values,
            pl.BlockSpec((1, wins, 3 * WIN, 2 * LANES), lambda p: (row * pairs + p, 0, 0, 0)),
            own,
        ]
        + [spec_any()] * len(before),
        [own, keys, keys, pl.BlockSpec((1, 8, LANES), lambda p: (row, 0, p))],
        grid=(pairs,),
        mib=56,
        aliases={5 + k: k for k in range(len(before))},
        name="attention_back%d" % row,
    )


VEC_ROWS = 64


def project_grad_kernel(
    meta,
    dq_h,
    chars_h,
    dk_h,
    low_h,
    high_h,
    dv_h,
    sums_a,
    sums1,
    sums3,
    isum_a,
    isum_b,
    send_o,
    keep_o,
    dq,
    dk,
    dv,
    ext,
    made_all,
    small,
    sem_in,
    sem_out,
):
    rows, full, width = dk.shape
    block = full - 2 * WIN
    count = rows * block
    place = meta[0]
    quarter = width // 4
    started = []
    pairs = [
        (dq_h, dq),
        (chars_h, ext.at[:, pl.ds(WIN, block)]),
        (dk_h, dk),
        (low_h, ext.at[:, pl.ds(0, WIN)]),
        (high_h, ext.at[:, pl.ds(WIN + block, WIN)]),
        (dv_h, dv),
    ]
    for k, (src, dst) in enumerate(pairs):
        started.append(pltpu.make_async_copy(src, dst, sem_in.at[k]))
        started[-1].start()
    leaving = []

    def leave(src, dst):
        leaving.append(pltpu.make_async_copy(src, dst, sem_out.at[len(leaving)]))
        leaving[-1].start()

    def put(index, made):
        at = pl.ds(index * quarter, quarter)
        for number in range(4):
            made_all[slot_of(jnp.int32(number), place), at, :] = made[
                number * quarter : (number + 1) * quarter
            ]
        leave(made_all.at[pl.ds(0, 2), at], send_o.at[:, at])
        leave(made_all.at[pl.ds(2, 2), at], keep_o.at[:, at])

    att = sums_a[0]
    for r in range(1, rows):
        att = att + sums_a[r]
    stack = [att[0:1], att[1:2], sums1[2:3], sums1[0:1], sums1[1:2], sums3[5:6]]
    stack += [sums3[3:4], sums3[4:5], sums3[2:3], sums3[0:1], sums3[1:2]]
    at = pl.ds(3 * quarter, VEC_ROWS)
    for number in range(4):
        mine = slice(number * quarter, (number + 1) * quarter)
        small[...] = jnp.zeros(small.shape, F32)
        for row, vector in enumerate(stack):
            small[row : row + 1, 0:quarter] = vector[:, mine]
        for j in range(4):
            small[len(stack) + j : len(stack) + j + 1, 0:quarter] = (isum_a, isum_b)[number // 2][
                number % 2, 0:1, j * quarter : (j + 1) * quarter
            ]
        made_all[slot_of(jnp.int32(number), place), at, :] = small[...].astype(BF)
    leave(made_all.at[pl.ds(0, 2), at], send_o.at[:, at])
    leave(made_all.at[pl.ds(2, 2), at], keep_o.at[:, at])

    started[0].wait()
    started[1].wait()
    own = ext[:, WIN : WIN + block, :].reshape(count, width)
    put(0, dot(dq[...].reshape(count, width), own, TN).astype(BF))
    for made in started[2:]:
        made.wait()
    every = ext[...].reshape(rows * full, width)
    mades = [dot(ref[...].reshape(rows * full, width), every, TN) for ref in (dk, dv)]
    for index, made in enumerate(mades):
        put(1 + index, made.astype(BF))
    for made in leaving:
        made.wait()


def project_grad(deps, meta, dq, chars, dk, low, high, dv, *sums):
    rows, full, width = dk.shape
    height = 3 * width // 4 + VEC_ROWS
    return run(
        project_grad_kernel,
        deps,
        (meta, dq, chars, dk, low, high, dv, *sums),
        [shape((2, height, width))] * 2,
        [spec_smem()] + [spec_any()] * 6 + [spec_vmem()] * len(sums),
        [spec_hbm()] * 2,
        scratch=[
            pltpu.VMEM(dq.shape, BF),
            pltpu.VMEM(dk.shape, BF),
            pltpu.VMEM(dk.shape, BF),
            pltpu.VMEM(dk.shape, BF),
            pltpu.VMEM((4, height, width), BF),
            pltpu.VMEM((VEC_ROWS, width), F32),
            pltpu.SemaphoreType.DMA((6,)),
            pltpu.SemaphoreType.DMA((8,)),
        ],
        name="project_grad",
    )


def halo_grad_kernel(dk_low, dv_low, dk_high, dv_high, wk, wv, low, high):
    rows, edge, width = low.shape
    for dk, dv, out in ((dk_low, dv_low, low), (dk_high, dv_high, high)):
        keys = dk[...].reshape(rows * edge, width)
        values = dv[...].reshape(rows * edge, width)
        made = dot(keys, wk[...], NT) + dot(values, wv[...], NT)
        out[...] = made.astype(BF).reshape(rows, edge, width)


def halo_grad(deps, dk, dv, wk, wv):
    rows, full, width = dk.shape
    edge = (rows, WIN, width)
    first = pl.BlockSpec(edge, lambda i: (0, 0, 0))
    last = pl.BlockSpec(edge, lambda i: (0, full // WIN - 1, 0))
    whole = pl.BlockSpec((width, width), lambda i: (0, 0))
    return run(
        halo_grad_kernel,
        deps,
        (dk, dv, dk, dv, wk, wv),
        [shape(edge)] * 2,
        [first, first, last, last, whole, whole],
        [first] * 2,
        grid=(1,),
        mib=24,
        name="halo_grad",
    )


def chars_grad_kernel(gb, dq, dk, dv, low, high, wq, wk, wv, out):
    _, block, width = dq.shape
    own = slice(WIN, WIN + block)
    made = gb[0].astype(F32)
    made = made + dot(dq[0], wq[...], NT)
    made = made + dot(dk[0, own, :], wk[...], NT)
    made = made + dot(dv[0, own, :], wv[...], NT)
    out[0, WIN : block - WIN, :] = made[WIN : block - WIN].astype(BF)
    out[0, 0:WIN, :] = (made[0:WIN] + low[0].astype(F32)).astype(BF)
    out[0, block - WIN :, :] = (made[block - WIN :] + high[0].astype(F32)).astype(BF)


def chars_grad(deps, gb, dq, dk, dv, low, high, wq, wk, wv):
    rows, block, width = dq.shape
    ext = dk.shape[1]
    row = lambda n: pl.BlockSpec((1, n, width), lambda r: (r, 0, 0))
    weight = pl.BlockSpec((width, width), lambda r: (0, 0))
    return run(
        chars_grad_kernel,
        deps,
        (gb.reshape(rows, block, width), dq, dk, dv, low, high, wq, wk, wv),
        shape((rows, block, width)),
        [row(block), row(block), row(ext), row(ext), row(WIN), row(WIN)] + [weight] * 3,
        row(block),
        grid=(rows,),
        mib=63,
        name="chars_grad",
    )


def swap(value, axis, bit):
    count = lax.axis_size(axis)
    return lax.ppermute(value, axis, [(i, i ^ bit) for i in range(count)])


def plus(left, right):
    return (left.astype(F32) + right.astype(F32)).astype(BF)


def add_kernel(meta, left, right, out):
    out[...] = plus(left[...], right[...])


class Beat:
    def __init__(self, chain, meta):
        self.chain, self.meta = chain, meta
        self.steps, self.carried = [], []
        self.fed = False

    def add(self, body, args, outs, then, scratch=()):
        self.steps.append((body, args, outs, then, scratch))

    def carry(self, value, then):
        self.carried.append((value, then))

    def emit(self, name):
        args = [self.meta] + [a for step in self.steps for a in step[1]]
        outs = [o for step in self.steps for o in step[2]]
        scratch = [x for step in self.steps for x in step[4]]
        moved = [value for value, _ in self.carried]
        counts = [len(args), len(moved), len(outs), len(moved)]

        def body(*refs):
            ins = refs[1 : counts[0]]
            results = refs[counts[0] + counts[1] : sum(counts[:3])]
            rest = refs[sum(counts) :]
            for step_body, step_args, step_outs, _, step_scratch in self.steps:
                a, o, x = len(step_args), len(step_outs), len(step_scratch)
                step_body(refs[0], *ins[:a], *results[:o], *rest[:x])
                ins, results, rest = ins[a:], results[o:], rest[x:]

        def call(deps, *given):
            return run(
                body,
                () if self.fed else deps,
                given,
                outs + [shape(value.shape, value.dtype) for value in moved],
                [spec_smem()] + [spec_vmem()] * (len(args) - 1) + [spec_hbm()] * len(moved),
                [spec_vmem()] * len(outs) + [spec_hbm()] * len(moved),
                scratch=scratch,
                mib=24,
                flops=1 if self.steps and self.steps[0][4] == () else 10**12,
                nbytes=10**9 if self.steps and self.steps[0][4] == () else 1,
                aliases={len(args) + k: len(outs) + k for k in range(len(moved))},
                name=name,
            )

        made = self.chain(call, *args, *moved)
        for step in self.steps:
            step[3](*made[: len(step[2])])
            made = made[len(step[2]) :]
        for (_, then), value in zip(self.carried, made, strict=True):
            then(value)


def split_kernel(role, meta, keep, arrived, a_out, a_keep, b_out, b_keep):
    half = keep.shape[1] // 2
    part = half // 2
    mine = meta[role]
    for slot, out in ((0, a_out), (1, a_keep)):
        out[...] = plus(keep[slot, 0:half, :], arrived[slot, 0:half, :])
    for slot in range(2):
        for out, which in ((b_out, 1 - mine), (b_keep, mine)):
            at = pl.ds(pl.multiple_of(half + which * part, 16), part)
            out[slot] = plus(keep[slot, at, :], arrived[slot, at, :])


def cross_kernel(role, meta, a, a_in, b, b_in, a_out, a_keep, b_out, b_keep):
    part = a.shape[0] // 2
    mine = meta[role]
    for out, which in ((a_out, 1 - mine), (a_keep, mine)):
        at = pl.ds(pl.multiple_of(which * part, 16), part)
        out[...] = plus(a[at, :], a_in[at, :])
    b_out[...] = plus(b[0], b_in[0])
    b_keep[...] = plus(b[1], b_in[1])


def merge_kernel(role, meta, a, a_in, b, b_in, out, keep):
    part = a.shape[0] // 2
    mine = meta[3 - role]
    for k, (left, right) in enumerate(((a, a_in), (b, b_in))):
        for made, which in ((out, 1 - mine), (keep, mine)):
            at = pl.ds(pl.multiple_of(which * part, 16), part)
            made[k] = plus(left[at, :], right[at, :])


def join_kernel(role, meta, own, other, out):
    part = own.shape[1]
    mine = meta[3 - role]
    for source, which in ((own, mine), (other, 1 - mine)):
        at = pl.ds(pl.multiple_of(which * part, 16), part)
        for k in range(2):
            out[k, at, :] = source[k]


def end_kernel(role, plan, meta, own, other, *refs):
    outs, whole = refs[:-1], refs[-1]
    part, width = own.shape[1:]
    mine = meta[role]
    for source, which in ((own, mine), (other, 1 - mine)):
        for k in range(2):
            at = pl.ds(pl.multiple_of((2 * k + which) * part, 16), part)
            whole[at, :] = source[k]
    row = 0
    for out, pieces in zip(outs, plan, strict=True):
        for at, rows in pieces:
            out[:, at * width : (at + 1) * width] = whole[row : row + rows, :].astype(F32)
            row += rows


class Sum:
    def __init__(self, keep, role):
        self.height, self.width = keep.shape[1:]
        self.keep, self.role = keep, role
        self.next = self.split
        self.bit = 2

    def of(self, body):
        return functools.partial(body, self.role)

    def core(self, send):
        self.arrived = swap(send, "seq", 1)

    def split(self, beat):
        height, width = self.height, self.width
        half, part = shape((height // 2, width)), shape((2, height // 4, width))

        def then(a_out, a, b_out, b):
            self.a, self.b = a, b
            self.a_in, self.b_in = swap(a_out, "seq", 2), swap(b_out, "dp", self.role)
            self.next = self.cross

        beat.add(self.of(split_kernel), [self.keep, self.arrived], [half, half, part, part], then)

    def cross(self, beat):
        part = shape((self.height // 4, self.width))

        def then(a_out, a, b_out, b):
            self.a, self.b = a, b
            self.a_in, self.b_in = swap(a_out, "dp", self.role), swap(b_out, "seq", 2)
            self.next = self.merge

        beat.add(self.of(cross_kernel), [self.a, self.a_in, self.b, self.b_in], [part] * 4, then)

    def merge(self, beat):
        part = shape((2, self.height // 8, self.width))

        def then(out, keep):
            self.keep = keep
            self.arrived = swap(out, "dp", 3 - self.role)
            self.next = self.more

        beat.add(self.of(merge_kernel), [self.a, self.a_in, self.b, self.b_in], [part] * 2, then)

    def more(self, beat):
        def then(total):
            self.keep = total
            self.bit *= 2
            last = self.bit >= lax.axis_size("dp")
            self.arrived = swap(total, "dp", 3 - self.role if last else self.bit)
            self.next = self.join if last else self.more

        beat.add(add_kernel, [self.keep, self.arrived], [shape(self.keep.shape)], then)

    def join(self, beat):
        def then(whole):
            self.keep = whole
            self.arrived = swap(whole, "dp", self.role)
            self.next = None

        whole = shape((2, self.height // 4, self.width))
        beat.add(self.of(join_kernel), [self.keep, self.arrived], [whole], then)

    def hold(self, arrived):
        self.arrived = arrived

    def end(self, beat, plan):
        width = self.width
        outs = [shape((pieces[0][1], width * len(pieces)), F32) for pieces in plan]

        def then(*made):
            self.made = made

        beat.add(
            functools.partial(end_kernel, self.role, plan),
            [self.keep, self.arrived],
            outs,
            then,
            [pltpu.VMEM((self.height, width), BF)],
        )


class Chain:
    def __init__(self):
        self.last = ()

    def __call__(self, made, *args):
        outs, mark = made(self.last, *args)
        self.last = (mark,)
        return outs


def shards(
    chars,
    window_mask,
    micro_batch,
    mol_grad,
    query_weight,
    query_bias,
    key_weight,
    value_weight,
    value_bias,
    output_weight,
    output_bias,
    first_gain,
    first_shift,
    inner_weight,
    inner_bias,
    outer_weight,
    outer_bias,
    second_gain,
    second_shift,
    conv_weight,
    conv_bias,
    third_gain,
    third_shift,
):
    rows, block, width = chars.shape
    count = rows * block
    place = lax.axis_index("seq").astype(jnp.int32)
    group = lax.axis_index("dp").astype(jnp.int32)
    meta = jnp.stack([place, group % 2, group // 2 % 2])
    size = lax.axis_size("seq")
    forward_pairs = [(i, i + 1) for i in range(size - 1)]
    backward_pairs = [(i + 1, i) for i in range(size - 1)]
    low = lax.ppermute(chars[:, block - WIN :], "seq", forward_pairs)
    high = lax.ppermute(chars[:, :WIN], "seq", backward_pairs)
    vectors = (
        query_bias,
        value_bias,
        output_bias,
        first_gain,
        first_shift,
        outer_bias,
        second_gain,
        second_shift,
        conv_bias,
        third_gain,
        third_shift,
        inner_bias,
    )
    tokens = chars.reshape(count, width)
    chain = Chain()
    q, k, v, vecs = chain(project, tokens, vectors, query_weight, key_weight, value_weight)
    kv, probs, mixed, n1, inv1, low1, slope, hidden, mol, go, sums3, send_c, keep_c = chain(
        forward,
        meta,
        window_mask,
        micro_batch,
        vecs,
        tokens,
        low,
        high,
        q,
        k,
        v,
        key_weight,
        value_weight,
        output_weight,
        inner_weight,
        outer_weight,
        conv_weight,
        mol_grad.reshape(-1, width),
    )
    molecules = mol.reshape(mol_grad.shape)
    conv = Sum(keep_c, 2)
    conv.core(send_c)
    send_u, keep_u = chain(outer_grad, meta, go, hidden)
    outer = Sum(keep_u, 2)

    def beat(name, chunks, carried=(), ends=(), fed=False):
        made = Beat(chain, meta)
        made.fed = fed
        for chunk in chunks:
            chunk.next(made)
        for chunk, plan in ends:
            chunk.end(made, plan)
        for value, then in carried:
            made.carry(value, then)
        made.emit(name)

    beat("beat1", [conv], [(send_u, outer.core)], fed=True)
    common = (meta, vecs, go, slope, outer_weight, inner_weight, low1)
    send_i, keep_i, isum_a, acc = chain(inner_back, (0, 1), *common)
    beat("beat2", [conv, outer])
    send_i, keep_i, isum_b, gb, gm, sums1 = chain(
        inner_back,
        (2, 3),
        *common,
        acc,
        n1,
        inv1,
        output_weight,
        mixed,
        send_i,
        keep_i,
    )
    inner = Sum(keep_i, 1)
    beat("beat3", [conv, outer], [(send_i, inner.core)], fed=True)
    beat("beat3i", [inner])
    grads = ()
    for r in range(rows):
        grads = chain(attention_back, q, kv, probs, gm, rows, r, tuple(grads))
        beat("beat%d" % (4 + r), [conv, outer, inner])
    dq, dk, dv, sums_a = grads
    send_p, keep_p = chain(
        project_grad, meta, dq, chars, dk, low, high, dv, sums_a, sums1, sums3, isum_a, isum_b
    )
    proj = Sum(keep_p, 1)
    beside = {}

    def from_prev(value):
        beside["low"] = lax.ppermute(value, "seq", forward_pairs)

    def from_next(value):
        beside["high"] = lax.ppermute(value, "seq", backward_pairs)

    quarter = width // 4
    wide = [[(j, quarter) for j in range(4)]]
    holds = lambda *chunks: [(chunk.arrived, chunk.hold) for chunk in chunks]
    beat("tail0", [conv, outer, inner], [(send_p, proj.core)], fed=True)
    beat("tail1", [proj])
    grad_low, grad_high = chain(halo_grad, dk, dv, key_weight, value_weight)
    beat("tail2", [proj, inner], [(grad_high, from_prev), (grad_low, from_next)])
    beat("tail3", [proj, outer, inner], holds(conv))
    beat("tail4", [proj])
    grad_chars = chain(
        chars_grad,
        gb,
        dq,
        dk,
        dv,
        beside["low"],
        beside["high"],
        query_weight,
        key_weight,
        value_weight,
    )
    while proj.next != proj.join:
        beat("tail_more", [chunk for chunk in (proj, conv, outer, inner) if chunk.next == chunk.more])
    for chunk in (conv, outer, inner):
        while chunk.next is not None:
            beat("tail_rest", [chunk])
    beat("tail6", [proj], holds(outer, inner))
    beat("ends0", [], (), [(outer, wide), (inner, [[(0, width)], [(0, quarter)]])])
    beat("ends1", [], (), [(conv, wide)])
    beat("tail7", [], (), [(proj, [[(0, quarter)]] * 3 + [[(0, 16)]])])
    (full_c,), (full_u,) = conv.made, outer.made
    full_i, full_o = inner.made
    full_q, full_k, full_v, small = proj.made
    vec_of = lambda i: small[i, :quarter]
    return (
        molecules,
        grad_chars,
        full_q.T,
        vec_of(0),
        full_k.T,
        full_v.T,
        vec_of(1),
        full_o.T,
        vec_of(2),
        vec_of(3),
        vec_of(4),
        full_i,
        small[11:15, :quarter].reshape(-1),
        full_u.T,
        vec_of(5),
        vec_of(6),
        vec_of(7),
        full_c.T,
        vec_of(8),
        vec_of(9),
        vec_of(10),
    )


def solution(mesh):
    split = P("dp", "seq", None)
    placed = (split, P("dp", None), P("dp"), split) + (P(),) * 19
    by_column, by_place = P(None, "seq"), P("seq")
    outs = (
        split,
        split,
        by_column,
        by_place,
        by_column,
        by_column,
        by_place,
        by_column,
        by_place,
        by_place,
        by_place,
        by_column,
        by_place,
        by_column,
        by_place,
        by_place,
        by_place,
        by_column,
        by_place,
        by_place,
        by_place,
    )
    return jax.shard_map(shards, mesh=mesh, in_specs=placed, out_specs=outs, check_vma=False)
```
